128 devices in a mesh: beam: 8 (over y_lo, z), det: 16 (over y_hi, x, core).
Axes of the slice: x: 4, y: 4 (y_hi: 2, y_lo: 2; y = y_hi * 2 + y_lo), z: 4, core: 2. Of those that a mesh axis runs over, the one named last changes fastest.
Arguments:
- concentration: float32 [10, 4, 1024, 2048], P(None, None, 'beam', 'det'), may hold values from 0.1 to 1
- incident_sigma: float32 [2, 10], replicated, may hold values from 0.1 to 0.8
- line_sigma: float32 [12, 10], replicated, may hold values from 0.05 to 0.4
- line_yield: float32 [12, 10], replicated, may hold values from 0.05 to 0.4
- step_rate: float32 [10], replicated, may hold values from 1 to 4
- view_axis: int32 [2], replicated, may hold values from 0 to 1, each once
- measured_first: float32 [12, 4, 2048], P(None, None, 'det'), may hold values from 0 to 0.8
- live_first: int32 [4, 2048], P(None, 'det'), may hold values 0 or 1
- measured_second: float32 [12, 4, 1024], P(None, None, 'beam'), may hold values from 0 to 0.8
- live_second: int32 [4, 1024], P(None, 'beam'), may hold values 0 or 1
Outputs:
- updated: float32 [10, 4, 1024, 2048], P(None, None, 'beam', 'det')
The draws below stay inside these ranges and needn't reach their ends.
Inputs may be any that keep to these rules, and one draw needn't show every extreme that they name: `view_axis`: holds 0 once and 1 once. `live_first`: 1 marks a live pixel. `live_second`: 1 marks a live pixel.
All inputs are finite; a program needn't handle non-finite values. No bound on the sum of `live_first` or of `live_second` on one device may be relied on, other than what follows from the above.
Results may differ from the reference program's by a relative error of at most 0.00011.
Values sent between devices are 32-bit elements; how exact they have to be, the bound alone decides.
A program may use at most 128 MiB of HBM per device.

```python
import math
import jax
import jax.numpy as jnp
from jax import lax

ELEMENTS = 10
LINES = 12
ZS = 4
STEPS = 2
NX = 1024
NY = 2048


def set_ends(values, key, low, largest):
    shape = values.shape
    spot = [jax.random.randint(jax.random.fold_in(key, axis), (), 0, shape[axis]) for axis in range(len(shape))]
    values = values.at[tuple(spot)].set(low)
    longest = shape.index(max(shape))
    spot[longest] = (spot[longest] + 1) % shape[longest]
    return values.at[tuple(spot)].set(largest)


def block_scale(stream_key, extent, cuts, smallest, top_value):
    def one(position, blocks):
        heights = jax.random.uniform(jax.random.fold_in(jax.random.fold_in(stream_key, 6), position), (blocks,), jnp.float32, smallest / len(cuts), top_value / len(cuts))
        return jnp.repeat(jnp.exp(heights), extent[position] // blocks).reshape((-1,) + (1,) * (len(extent) - position - 1))

    level = one(*cuts[0])
    for cut in cuts[1:]:
        level = level * one(*cut)
    return level


def setup_inputs(seed: int = 0) -> dict:
    key_list = jax.random.split(jax.random.key(seed), 11)
    concentration = jnp.clip(0.1 + 0.9 * jax.random.uniform(key_list[0], (ELEMENTS, ZS, NX, NY), jnp.float32) ** block_scale(key_list[0], (ELEMENTS, ZS, NX, NY), ((2, 8), (3, 16)), -0.2, 0.2), 0.1, 1.0)
    incident_sigma = jnp.clip(jnp.exp(jax.random.uniform(key_list[1], (2, ELEMENTS), jnp.float32, math.log(0.1), math.log(0.8))), 0.1, 0.8)
    line_sigma = jnp.clip(jnp.exp(jax.random.uniform(key_list[2], (LINES, ELEMENTS), jnp.float32, math.log(0.05), math.log(0.4))), 0.05, 0.4)
    line_yield = jnp.clip(jnp.exp(jax.random.uniform(key_list[3], (LINES, ELEMENTS), jnp.float32, math.log(0.05), math.log(0.4))), 0.05, 0.4)
    step_rate = jnp.clip(jnp.exp(jax.random.uniform(key_list[4], (ELEMENTS,), jnp.float32, math.log(1.0), math.log(4.0))), 1.0, 4.0)
    view_axis = jax.random.permutation(key_list[5], 2).astype(jnp.int32)
    measured_first = jnp.clip(0.8 * jax.random.uniform(key_list[6], (LINES, ZS, NY), jnp.float32) ** block_scale(key_list[6], (LINES, ZS, NY), ((2, 16),), -0.2, 0.2), 0.0, 0.8)
    live_first = set_ends((jax.random.randint(key_list[7], (ZS, NY), 0, 8) < 7).astype(jnp.int32), jax.random.fold_in(key_list[7], 1), 0, 1)
    measured_second = jnp.clip(0.8 * jax.random.uniform(key_list[8], (LINES, ZS, NX), jnp.float32) ** block_scale(key_list[8], (LINES, ZS, NX), ((2, 8),), -0.2, 0.2), 0.0, 0.8)
    live_second = set_ends((jax.random.randint(key_list[9], (ZS, NX), 0, 8) < 7).astype(jnp.int32), jax.random.fold_in(key_list[9], 1), 0, 1)
    return dict(concentration=concentration, incident_sigma=incident_sigma, line_sigma=line_sigma, line_yield=line_yield, step_rate=step_rate, view_axis=view_axis, measured_first=measured_first, live_first=live_first, measured_second=measured_second, live_second=live_second)


HIGH = lax.Precision.HIGHEST


def exclusive(values, axis, backward):
    if backward:
        values = jnp.flip(values, axis)
    count = values.shape[axis]
    running = jnp.cumsum(values, axis=axis)
    leading = jnp.zeros_like(lax.slice_in_dim(values, 0, 1, axis=axis))
    shifted = jnp.concatenate([leading, lax.slice_in_dim(running, 0, count - 1, axis=axis)], axis)
    if backward:
        shifted = jnp.flip(shifted, axis)
    return shifted


def slice_steps(conc, measured_first, live_first, measured_second, live_second, sigma_first, sigma_second, line_sigma, line_yield, step_rate):
    step_x = 1.0 / NX
    step_y = 1.0 / NY
    live_one = live_first.astype(jnp.float32)
    live_two = live_second.astype(jnp.float32)
    for turn in range(STEPS):
        mu_first = jnp.einsum('e,eij->ij', sigma_first, conc, precision=HIGH)
        mu_second = jnp.einsum('e,eij->ij', sigma_second, conc, precision=HIGH)
        mu_line = jnp.einsum('le,eij->lij', line_sigma, conc, precision=HIGH)
        emitted = jnp.einsum('le,eij->lij', line_yield, conc, precision=HIGH)
        tin_first = jnp.exp(-step_x * exclusive(mu_first, 0, False))
        tout_first = jnp.exp(-step_y * exclusive(mu_line, 2, False))
        tin_second = jnp.exp(-step_y * exclusive(mu_second, 1, False))
        tout_second = jnp.exp(-step_x * exclusive(mu_line, 1, False))
        pred_first = step_x * jnp.sum(emitted * tin_first[None] * tout_first, axis=1)
        pred_second = step_y * jnp.sum(emitted * tin_second[None] * tout_second, axis=2)
        res_first = live_one[None] * (pred_first - measured_first)
        res_second = live_two[None] * (pred_second - measured_second)
        w_first = res_first[:, None, :] * tin_first[None] * tout_first
        w_second = res_second[:, :, None] * tin_second[None] * tout_second
        p_first = w_first * emitted
        p_second = w_second * emitted
        grad = jnp.einsum('le,lij->eij', line_yield, w_first + w_second, precision=HIGH)
        grad = grad - step_x * sigma_first[:, None, None] * exclusive(jnp.sum(p_first, axis=0), 0, True)[None]
        grad = grad - step_x * exclusive(jnp.einsum('le,lij->eij', line_sigma, p_second, precision=HIGH), 1, True)
        grad = grad - step_y * sigma_second[:, None, None] * exclusive(jnp.sum(p_second, axis=0), 1, True)[None]
        grad = grad - step_y * exclusive(jnp.einsum('le,lij->eij', line_sigma, p_first, precision=HIGH), 2, True)
        conc = conc - step_rate[:, None, None] * grad
    return conc


def reference(concentration, incident_sigma, line_sigma, line_yield, step_rate, view_axis, measured_first, live_first, measured_second, live_second):
    sigma_first = jnp.where(view_axis[0] == 0, incident_sigma[0], incident_sigma[1])
    sigma_second = jnp.where(view_axis[0] == 0, incident_sigma[1], incident_sigma[0])
    slices = (jnp.transpose(concentration, (1, 0, 2, 3)), jnp.transpose(measured_first, (1, 0, 2)), live_first, jnp.transpose(measured_second, (1, 0, 2)), live_second)

    def one_slice(items):
        return slice_steps(items[0], items[1], items[2], items[3], items[4], sigma_first, sigma_second, line_sigma, line_yield, step_rate)

    result = lax.map(one_slice, slices)
    return jnp.transpose(result, (1, 0, 2, 3))
```

```python
import math

import jax
import jax.numpy as jnp
from jax import lax
from jax.experimental import pallas as pl
from jax.experimental.pallas import tpu as pltpu
from jax.sharding import PartitionSpec as P

STEPS = 2
HIGH = lax.Precision.HIGHEST
MESH = pl.DeviceIdType.MESH
F32 = jnp.float32
BF16 = jnp.bfloat16
ELEMENTS = 10
LINES = 12
ZS = 4
N = 128
FIELDS = 26
LOG2E = math.log2(math.e)


def split(value):
    high = value.astype(BF16)
    return high, (value - high.astype(F32)).astype(BF16)


def iota(shape, dim):
    return lax.broadcasted_iota(jnp.int32, shape, dim)


def dot(a, b):
    return jnp.dot(a, b, preferred_element_type=F32)


def exact(a, b):
    return jnp.dot(a, b, preferred_element_type=F32, precision=HIGH)


def exact_nt(a, b):
    return lax.dot_general(
        a, b, (((1,), (1,)), ((), ())), preferred_element_type=F32, precision=HIGH
    )


def one_hot(condition):
    return jnp.where(condition, 1.0, 0.0).astype(F32)


def cum_cols(value, table):
    high, low = split(value)
    return dot(jnp.concatenate([high, low], 1), table)


def cum_rows(value, table):
    high, low = split(value)
    return dot(table, jnp.concatenate([high, low], 0))


class Ring:
    def __init__(self, axis, send, recv, back, done, sems):
        self.axis = axis
        self.count = recv.shape[2]
        self.me = lax.axis_index(axis)
        self.send, self.recv, self.back, self.done, self.sems = send, recv, back, done, sems
        self.tiles = self.count // ZS

    def greet(self, barrier):
        def one(d, carry):
            peer = lax.rem(self.me + d, self.count)
            pl.semaphore_signal(
                barrier, inc=1, device_id={self.axis: peer}, device_id_type=MESH
            )
            return carry

        lax.fori_loop(1, self.count, one, 0)

    def copy(self, src, dst, step, phase, leg, peer):
        return pltpu.make_async_remote_copy(
            src_ref=src,
            dst_ref=dst,
            send_sem=self.sems.at[step, phase, leg, 0],
            recv_sem=self.sems.at[step, phase, leg, 1],
            device_id={self.axis: peer},
            device_id_type=MESH,
        )

    def start(self, step, phase):
        mine = (step, phase, pl.ds(self.me, 1))
        self.recv[mine] = self.send[mine]

        def one(d, carry):
            peer = lax.rem(self.me + d, self.count)
            self.copy(
                self.send.at[step, phase, peer], self.recv.at[step, phase, self.me], step, phase, 0, peer
            ).start()
            return carry

        lax.fori_loop(1, self.count, one, 0)

    def wait(self, src, dst, step, phase, leg):
        several = (step, phase, pl.ds(0, self.count - 1))
        peer = lax.rem(self.me + 1, self.count)
        whole = self.copy(src.at[several], dst.at[several], step, phase, leg, peer)
        whole.wait_send()
        whole.wait_recv()

    def middle(self, step, phase, mode):
        self.wait(self.send, self.recv, step, phase, 0)
        total = jnp.zeros((8, N), F32)
        order = range(self.count)
        for t in reversed(order) if mode == "later" else order:
            if mode != "sum":
                self.back[step, phase, t] = total
            total = total + self.recv[step, phase, t]
        if mode == "sum":
            self.back[step, phase, 0] = total
            self.done[step, phase, pl.ds(self.me, 1)] = total[None]
        else:
            mine = (step, phase, pl.ds(self.me, 1))
            self.done[mine] = self.back[mine]

        def one(d, carry):
            peer = lax.rem(self.me + d, self.count)
            source = 0 if mode == "sum" else peer
            self.copy(
                self.back.at[step, phase, source], self.done.at[step, phase, self.me], step, phase, 1, peer
            ).start()
            return carry

        lax.fori_loop(1, self.count, one, 0)

    def finish(self, step, phase):
        self.wait(self.back, self.done, step, phase, 1)

    def put(self, step, phase, z, row, per, value):
        self.send[step, phase, z * self.tiles + row // per, pl.ds(row % per, 1), :] = value

    def get(self, step, phase, z, row, per):
        return self.done[step, phase, z * self.tiles + row // per, pl.ds(row % per, 1), :]

    def got(self, step, phase, z):
        rows = self.done[step, phase, pl.ds(z * self.tiles, self.tiles)]
        return rows.reshape(self.tiles * 8, N)

    def put_all(self, step, phase, z, rows):
        self.send[step, phase, pl.ds(z * self.tiles, self.tiles)] = rows.reshape(self.tiles, 8, N)


def over_z(body):
    def one(z, carry):
        body(z)
        return carry

    lax.fori_loop(0, ZS, one, 0)


def kernel(
    step_x, step_y,
    axis_ref, conc_ref, inc_ref, sig_ref, yld_ref, rate_ref, m1_ref, live1_ref, m2_ref, live2_ref,
    c_ref,
    f_ref, a1_ref, a2_ref, s2c_ref, ex_ref, ey_ref, q1_ref, q2_ref, r1_ref, r2_ref, mx_ref, my_ref,
    tx_ref, ty_ref, tab_ref, back_ref, mix_ref, unmix_ref, up_ref, down_ref, left_ref, right_ref,
    wax_ref, way_ref, wcx_ref, wcy_ref,
    bsend, brecv, bback, bdone, bsems, dsend, drecv, dback, ddone, dsems,
):
    beam = Ring("beam", bsend, brecv, bback, bdone, bsems)
    det = Ring("det", dsend, drecv, dback, ddone, dsems)
    per_x = {ELEMENTS: -(-ELEMENTS // beam.tiles), LINES: -(-LINES // beam.tiles)}
    per_y = {ELEMENTS: -(-ELEMENTS // det.tiles), LINES: -(-LINES // det.tiles)}
    barrier = pltpu.get_barrier_semaphore()
    beam.greet(barrier)
    det.greet(barrier)

    for ref in (bsend, dsend, q1_ref, q2_ref, r1_ref, r2_ref, tx_ref, ty_ref, tab_ref, back_ref):
        ref[...] = jnp.zeros(ref.shape, F32)

    lane = iota((N, N), 1)

    def totals(z, step):
        acc = jnp.zeros((N, N), F32)
        for e in range(ELEMENTS):
            c = c_ref[e, z]
            beam.put(step, 0, z, e, per_x[ELEMENTS], jnp.sum(c, 0, keepdims=True))
            acc = jnp.where(lane == e, jnp.sum(c, 1, keepdims=True), acc)
        rows = acc.T
        for e in range(ELEMENTS):
            det.put(step, 0, z, e, per_y[ELEMENTS], rows[e : e + 1])

    def begin(z):
        c_ref[:, z] = conc_ref[:, z]
        totals(z, 0)

    over_z(begin)
    pl.semaphore_wait(barrier, beam.count + det.count - 2)

    def tables():
        first = axis_ref[0] == 0
        one, two = inc_ref[0:1, :], inc_ref[1:2, :]
        s1 = jnp.where(first, one, two)
        s2 = jnp.where(first, two, one)
        scale = -LOG2E * step_y
        sig, yld, rate = sig_ref[...], yld_ref[...], rate_ref[...]
        cols = pl.ds(0, ELEMENTS)
        tab_ref[0:LINES, cols] = scale * sig
        tab_ref[LINES : LINES + 1, cols] = scale * s2
        tab_ref[LINES + 1 : LINES + 2, cols] = scale * s1
        tab_ref[LINES + 2 : FIELDS, cols] = yld
        back_ref[0:LINES, cols] = yld * rate
        back_ref[LINES : 2 * LINES, cols] = -sig * rate
        back_ref[2 * LINES : 2 * LINES + 1, cols] = -s1 * rate
        back_ref[2 * LINES + 1 : FIELDS, cols] = -s2 * rate

        tab, back = tab_ref[...], back_ref[...]
        wide = 8 * ELEMENTS
        pick = one_hot((iota((8 * FIELDS, 32), 0) >> 3) == iota((8 * FIELDS, 32), 1))
        col = iota((N, 256), 1)
        part = (col >= wide).astype(jnp.int32) + (col >= 2 * wide).astype(jnp.int32)
        spread = one_hot(((col - wide * part) >> 3) == iota((N, 256), 0))
        spread = jnp.where(col < 3 * wide, spread, 0.0)
        full = exact(pick, exact(tab, spread))
        shape = (8 * FIELDS, 256)
        full = jnp.where((iota(shape, 0) & 7) == (iota(shape, 1) & 7), full, 0.0)
        high, low = split(full)
        part = iota(shape, 1)
        mix_ref[...] = jnp.where((part >= wide) & (part < 2 * wide), low.astype(F32), high.astype(F32)).astype(BF16)

        pick = one_hot((iota((wide, N), 0) >> 3) == iota((wide, N), 1))
        shape = (wide, 8 * FIELDS)
        spread = one_hot((iota((32, 8 * FIELDS), 1) >> 3) == iota((32, 8 * FIELDS), 0))
        full = exact(exact_nt(pick, back), spread)
        full = jnp.where((iota(shape, 0) & 7) == (iota(shape, 1) & 7), full, 0.0)
        high, low = split(full)
        unmix_ref[0:wide] = high
        unmix_ref[wide : 2 * wide] = low

        def layout(ring, per):
            shape = (8 * ring.tiles, N)
            row = iota(shape, 0)
            inside = row & 7
            return one_hot((inside < per) & ((row >> 3) * per + inside == iota(shape, 1)))

        place_x = layout(beam, per_x[ELEMENTS])
        place_y = layout(det, per_y[ELEMENTS])
        used = iota((32, N), 0) < LINES + 2
        rates = jnp.where(used, tab, 0.0)
        wax_ref[...] = exact_nt(rates * (step_x / step_y), place_x)
        way_ref[...] = exact_nt(rates, place_y)
        row = iota((32, N), 0)
        lines = (row >= LINES) & (row < 2 * LINES)
        wcx_ref[...] = exact_nt(place_x, jnp.where(lines | (row == 2 * LINES), -step_x * back, 0.0))
        wcy_ref[...] = exact_nt(place_y, jnp.where(lines | (row == 2 * LINES + 1), -step_y * back, 0.0))

        r, c = iota((2 * N, N), 0) & (N - 1), iota((2 * N, N), 1)
        up_ref[...] = one_hot(r < c).astype(BF16)
        down_ref[...] = (step_y * one_hot(r > c)).astype(BF16)
        r, c = iota((N, 2 * N), 0), iota((N, 2 * N), 1) & (N - 1)
        left_ref[...] = (step_x / step_y * one_hot(c < r)).astype(BF16)
        right_ref[...] = (step_x * one_hot(c > r)).astype(BF16)
        for z in range(ZS):
            for l in range(LINES):
                mx_ref[z, l : l + 1, :] = m1_ref[l, z : z + 1, :]
                my_ref[z, l : l + 1, :] = m2_ref[l, z : z + 1, :]

    def blocks(body):
        def one(n, carry):
            body(n // 4, pl.multiple_of((n % 4) * 32, 32))
            return carry

        lax.fori_loop(0, 4 * ZS, one, 0)

    def mix(z, r0):
        parts = []
        for b in range(4):
            high, low = split(c_ref[:, z, pl.ds(r0 + 8 * b, 8), :].reshape(8 * ELEMENTS, N))
            parts.append(jnp.concatenate([high, high, low, jnp.zeros((16, N), BF16)], 0))
        out = dot(mix_ref[...], jnp.concatenate(parts, 1))
        for b in range(4):
            f_ref[z, :, pl.ds(r0 + 8 * b, 8), :] = out[:, b * N : (b + 1) * N].reshape(FIELDS, 8, N)

    def unmix(z, r0):
        highs, lows = [], []
        for b in range(4):
            rows = pl.ds(r0 + 8 * b, 8)
            w = a1_ref[z, :, rows, :].reshape(8 * LINES, N)
            v = f_ref[z, 0 : LINES + 2, rows, :].reshape(8 * (LINES + 2), N)
            high, low = split(jnp.concatenate([w, v], 0))
            highs.append(high)
            lows.append(low)
        wide = 8 * ELEMENTS
        one = dot(unmix_ref[...], jnp.concatenate(highs, 1))
        two = dot(unmix_ref[0:wide], jnp.concatenate(lows, 1))
        out = one[0:wide] + (one[wide:] + two)
        for b in range(4):
            rows = pl.ds(r0 + 8 * b, 8)
            c_ref[:, z, rows, :] = c_ref[:, z, rows, :] - out[:, b * N : (b + 1) * N].reshape(ELEMENTS, 8, N)

    def attenuate(z):
        tin1 = jnp.exp2(cum_rows(f_ref[z, LINES + 1], left_ref[...]))
        tin2 = jnp.exp2(cum_cols(f_ref[z, LINES], up_ref[...]))
        for l in range(0, LINES, 2):
            high0, low0 = split(f_ref[z, l])
            high1, low1 = split(f_ref[z, l + 1])
            across = jnp.concatenate(
                [jnp.concatenate([high0, low0], 1), jnp.concatenate([high1, low1], 1)], 0
            )
            along = jnp.concatenate(
                [jnp.concatenate([high0, high1], 1), jnp.concatenate([low0, low1], 1)], 0
            )
            over_y = jnp.exp2(dot(across, up_ref[...]))
            over_x = jnp.exp2(dot(left_ref[...], along))
            for k in range(2):
                a1_ref[z, l + k] = tin1 * over_y[k * N : (k + 1) * N]
                a2_ref[z, l + k] = tin2 * over_x[:, k * N : (k + 1) * N]

    def turned(rows):
        return jnp.concatenate([rows, jnp.zeros((N - rows.shape[0], N), F32)], 0).T

    def counts(z, step):
        ex = jnp.exp2(exact(wax_ref[...], beam.got(step, 0, z))[0:16])
        ey = jnp.exp2(exact(way_ref[...], det.got(step, 0, z))[0:16])
        ex_ref[z], ey_ref[z] = ex, ey
        cols = turned(ey)
        enter = step_x * ex[LINES + 1 : LINES + 2]
        acc = jnp.zeros((N, N), F32)
        for l in range(LINES):
            q = f_ref[z, LINES + 2 + l]
            a1 = a1_ref[z, l] * cols[:, l : l + 1]
            a1_ref[z, l] = a1
            part = enter * jnp.sum(q * a1, 0, keepdims=True)
            q1_ref[z, l : l + 1, :] = part
            beam.put(step, 1, z, l, per_x[LINES], part)
            acc = jnp.where(lane == l, jnp.sum(q * (a2_ref[z, l] * ex[l : l + 1]), 1, keepdims=True), acc)
        rows = acc.T
        part = step_y * ey[LINES : LINES + 1] * rows[0:16]
        q2_ref[z] = part
        for l in range(LINES):
            det.put(step, 1, z, l, per_y[LINES], part[l : l + 1])

    def residuals(z, step):
        live1 = live1_ref[pl.ds(z, 1), :].astype(F32)
        live2 = live2_ref[pl.ds(z, 1), :].astype(F32)
        for l in range(LINES):
            row = pl.ds(l, 1)
            r1_ref[z, row, :] = live1 * (beam.get(step, 1, z, l, per_x[LINES]) - mx_ref[z, row, :])
            r2_ref[z, row, :] = live2 * (det.get(step, 1, z, l, per_y[LINES]) - my_ref[z, row, :])
        ex, ey = ex_ref[z], ey_ref[z]
        res1, res2 = r1_ref[z], r2_ref[z]
        tx_ref[2 * LINES : 2 * LINES + 1] = jnp.sum(res1 * q1_ref[z], 0, keepdims=True) / step_x
        ty_ref[2 * LINES + 1 : 2 * LINES + 2] = jnp.sum(res2 * q2_ref[z], 0, keepdims=True) / step_y
        r1 = res1 * ex[LINES + 1 : LINES + 2]
        r1_ref[z] = r1
        cols = turned(res2 * ey[LINES : LINES + 1])
        s2c_ref[z] = cols
        acc = jnp.zeros((N, N), F32)
        for l in range(LINES):
            q = f_ref[z, LINES + 2 + l]
            acc = jnp.where(lane == LINES + l, jnp.sum(q * (a1_ref[z, l] * r1[l : l + 1]), 1, keepdims=True), acc)
            seen = jnp.sum(q * (a2_ref[z, l] * cols[:, l : l + 1]), 0, keepdims=True)
            tx_ref[LINES + l : LINES + l + 1, :] = ex[l : l + 1] * seen
        ty_ref[LINES : 2 * LINES, :] = acc.T[LINES : 2 * LINES]
        beam.put_all(step, 2, z, exact(wcx_ref[...], tx_ref[...]))
        det.put_all(step, 2, z, exact(wcy_ref[...], ty_ref[...]))

    def weights(z):
        ex, r1 = ex_ref[z], r1_ref[z]
        cols = s2c_ref[z]
        sum1 = jnp.zeros((N, N), F32)
        sum2 = jnp.zeros((N, N), F32)
        for l in range(LINES):
            q = f_ref[z, LINES + 2 + l]
            w1 = a1_ref[z, l] * r1[l : l + 1]
            w2 = a2_ref[z, l] * ex[l : l + 1] * cols[:, l : l + 1]
            a1_ref[z, l] = w1 + w2
            p1, p2 = q * w1, q * w2
            sum1, sum2 = sum1 + p1, sum2 + p2
            f_ref[z, l] = cum_cols(p1, down_ref[...]) + cum_rows(p2, right_ref[...])
        f_ref[z, LINES] = cum_rows(sum1, right_ref[...])
        f_ref[z, LINES + 1] = cum_cols(sum2, down_ref[...])

    def update(z, step):
        cols = turned(det.got(step, 2, z))
        for e in range(ELEMENTS):
            per = per_y[ELEMENTS]
            spot = (e // per) * 8 + e % per
            c_ref[e, z] = c_ref[e, z] + beam.get(step, 2, z, e, per_x[ELEMENTS]) + cols[:, spot : spot + 1]

    def turn(step, carry):
        @pl.when(step > 0)
        def again():
            over_z(lambda z: totals(z, step))

        beam.start(step, 0)
        det.start(step, 0)

        @pl.when(step == 0)
        def prepare():
            tables()

        blocks(mix)
        beam.middle(step, 0, "earlier")
        det.middle(step, 0, "earlier")
        over_z(attenuate)
        beam.finish(step, 0)
        det.finish(step, 0)
        over_z(lambda z: counts(z, step))
        beam.start(step, 1)
        det.start(step, 1)
        beam.middle(step, 1, "sum")
        det.middle(step, 1, "sum")
        beam.finish(step, 1)
        det.finish(step, 1)
        over_z(lambda z: residuals(z, step))
        beam.start(step, 2)
        det.start(step, 2)
        over_z(weights)
        beam.middle(step, 2, "later")
        det.middle(step, 2, "later")
        blocks(unmix)
        beam.finish(step, 2)
        det.finish(step, 2)
        over_z(lambda z: update(z, step))
        return carry

    lax.fori_loop(0, STEPS, turn, 0)


def solution(mesh):
    beams, dets = mesh.shape["beam"], mesh.shape["det"]

    def shards(conc, inc, sig, yld, rate, axis, m1, live1, m2, live2):
        step_x = 1.0 / (conc.shape[2] * beams)
        step_y = 1.0 / (conc.shape[3] * dets)

        def body(*refs):
            kernel(step_x, step_y, *refs)

        field = (N, N)
        rows = pltpu.VMEM((ZS, 16, N), F32)

        def exchange(count):
            tiles = pltpu.VMEM((STEPS, 3, count, 8, N), F32)
            return [tiles] * 4 + [pltpu.SemaphoreType.DMA((STEPS, 3, 2, 2))]

        vmem = pl.BlockSpec(memory_space=pltpu.VMEM)
        return pl.pallas_call(
            body,
            out_shape=jax.ShapeDtypeStruct(conc.shape, F32),
            in_specs=[pl.BlockSpec(memory_space=pltpu.SMEM)] + [vmem] * 9,
            out_specs=vmem,
            scratch_shapes=[
                pltpu.VMEM((ZS, FIELDS) + field, F32),
                pltpu.VMEM((ZS, LINES) + field, F32),
                pltpu.VMEM((ZS, LINES) + field, F32),
                pltpu.VMEM((ZS,) + field, F32),
                *[rows] * 8,
                *[pltpu.VMEM((32, N), F32)] * 4,
                pltpu.VMEM((8 * FIELDS, 2 * N), BF16),
                pltpu.VMEM((16 * ELEMENTS, 8 * FIELDS), BF16),
                *[pltpu.VMEM((2 * N, N), BF16)] * 2,
                *[pltpu.VMEM((N, 2 * N), BF16)] * 2,
                pltpu.VMEM((32, 2 * beams), F32),
                pltpu.VMEM((32, 2 * dets), F32),
                pltpu.VMEM((2 * beams, 32), F32),
                pltpu.VMEM((2 * dets, 32), F32),
                *exchange(beams),
                *exchange(dets),
            ],
            compiler_params=pltpu.CompilerParams(
                collective_id=0, has_side_effects=True, vmem_limit_bytes=52 * 1024 * 1024
            ),
        )(axis, conc, inc, sig, yld, rate[None], m1, live1, m2, live2)

    in_specs = (
        P(None, None, "beam", "det"),
        P(),
        P(),
        P(),
        P(),
        P(),
        P(None, None, "det"),
        P(None, "det"),
        P(None, None, "beam"),
        P(None, "beam"),
    )
    out_specs = P(None, None, "beam", "det")
    return jax.shard_map(shards, mesh=mesh, in_specs=in_specs, out_specs=out_specs, check_vma=False)
```

```python
import math

import jax
import jax.numpy as jnp
from jax import lax
from jax.experimental import pallas as pl
from jax.experimental.pallas import tpu as pltpu
from jax.sharding import PartitionSpec as P

STEPS = 2
HIGH = lax.Precision.HIGHEST
MESH = pl.DeviceIdType.MESH
F32 = jnp.float32
BF16 = jnp.bfloat16
ELEMENTS = 10
LINES = 12
ZS = 4
N = 128
FIELDS = 26
LOG2E = math.log2(math.e)


def split(value):
    high = value.astype(BF16)
    return high, (value - high.astype(F32)).astype(BF16)


def iota(shape, dim):
    return lax.broadcasted_iota(jnp.int32, shape, dim)


def dot(a, b):
    return jnp.dot(a, b, preferred_element_type=F32)


def exact(a, b):
    return jnp.dot(a, b, preferred_element_type=F32, precision=HIGH)


def exact_nt(a, b):
    return lax.dot_general(
        a, b, (((1,), (1,)), ((), ())), preferred_element_type=F32, precision=HIGH
    )


def one_hot(condition):
    return jnp.where(condition, 1.0, 0.0).astype(F32)


def cum_cols(value, table):
    high, low = split(value)
    return dot(jnp.concatenate([high, low], 1), table)


def cum_rows(value, table):
    high, low = split(value)
    return dot(table, jnp.concatenate([high, low], 0))


class Ring:
    def __init__(self, axis, send, recv, back, done, sems):
        self.axis = axis
        self.count = recv.shape[2]
        self.me = lax.axis_index(axis)
        self.send, self.recv, self.back, self.done, self.sems = send, recv, back, done, sems
        self.tiles = self.count // ZS
        self.wide = 8 * self.tiles
        half = self.count // 2
        self.hops = sorted(range(1, self.count), key=lambda d: (abs(d - half), d))

    def peer(self, d):
        return lax.rem(self.me + d, self.count)

    def greet(self, barrier):
        for d in self.hops:
            pl.semaphore_signal(barrier, inc=1, device_id={self.axis: self.peer(d)}, device_id_type=MESH)

    def copy(self, src, dst, step, phase, leg, peer):
        return pltpu.make_async_remote_copy(
            src_ref=src,
            dst_ref=dst,
            send_sem=self.sems.at[step, phase, leg, 0],
            recv_sem=self.sems.at[step, phase, leg, 1],
            device_id={self.axis: peer},
            device_id_type=MESH,
        )

    def start(self, step, phase):
        mine = (step, phase, pl.ds(self.me, 1))
        self.recv[mine] = self.send[mine]
        for d in self.hops:
            peer = self.peer(d)
            src, dst = self.send.at[step, phase, peer], self.recv.at[step, phase, self.me]
            self.copy(src, dst, step, phase, 0, peer).start()

    def wait(self, src, dst, step, phase, leg):
        several = (step, phase, pl.ds(0, self.count - 1))
        whole = self.copy(src.at[several], dst.at[several], step, phase, leg, self.peer(1))
        whole.wait_send()
        whole.wait_recv()

    def middle(self, step, phase, mode):
        self.wait(self.send, self.recv, step, phase, 0)
        total = jnp.zeros((8, N), F32)
        order = range(self.count)
        for t in reversed(order) if mode == "later" else order:
            if mode != "sum":
                self.back[step, phase, t] = total
            total = total + self.recv[step, phase, t]
        mine = (step, phase, pl.ds(self.me, 1))
        if mode == "sum":
            self.back[step, phase, 0] = total
            self.done[mine] = total[None]
        else:
            self.done[mine] = self.back[mine]
        for d in self.hops:
            peer = self.peer(d)
            src = self.back.at[step, phase, 0 if mode == "sum" else peer]
            self.copy(src, self.done.at[step, phase, self.me], step, phase, 1, peer).start()

    def finish(self, step, phase):
        self.wait(self.back, self.done, step, phase, 1)

    def spot(self, z, row, of):
        per = -(-of // self.tiles)
        return self.wide * z + 8 * (row // per) + row % per

    def rows(self, ref, step, phase):
        return ref[step, phase].reshape(8 * self.count, N)

    def put(self, step, phase, spot, value):
        self.send[step, phase, spot // 8, spot % 8 : spot % 8 + 1, :] = value

    def put_all(self, step, phase, rows):
        self.send[step, phase] = rows.reshape(self.count, 8, N)


def kernel(
    step_x, step_y,
    axis_hbm, inc_hbm, sig_hbm, yld_hbm, rate_hbm, m1_hbm, live1_hbm, m2_hbm, live2_hbm, conc_hbm,
    out_hbm, dx_ref, dy_ref,
    axis_ref, inc_ref, sig_ref, yld_ref, rate_ref, m1_ref, live1_ref, m2_ref, live2_ref, c_ref,
    load_sems, conc_sems,
    f_ref, a1_ref, a2_ref, ex_ref, ey_ref, r1_ref, s2c_ref, mx_ref, my_ref, lx_ref, ly_ref,
    tx_ref, ty_ref, tab_ref, back_ref, mix_ref, unmix_ref, up_ref, down_ref, left_ref, right_ref,
    wax_ref, way_ref, wcx_ref, wcy_ref,
    bsend, brecv, bback, bdone, bsems, dsend, drecv, dback, ddone, dsems,
):
    conc_loads = [
        pltpu.make_async_copy(conc_hbm.at[:, z], c_ref.at[:, z], conc_sems.at[z]) for z in range(ZS)
    ]
    hbm = (axis_hbm, inc_hbm, sig_hbm, yld_hbm, rate_hbm, m1_hbm, live1_hbm, m2_hbm, live2_hbm)
    vmem = (axis_ref, inc_ref, sig_ref, yld_ref, rate_ref, m1_ref, live1_ref, m2_ref, live2_ref)
    loads = [pltpu.make_async_copy(a, b, load_sems.at[k]) for k, (a, b) in enumerate(zip(hbm, vmem))]
    for load in conc_loads + loads:
        load.start()
    beam = Ring("beam", bsend, brecv, bback, bdone, bsems)
    det = Ring("det", dsend, drecv, dback, ddone, dsems)
    barrier = pltpu.get_barrier_semaphore()
    det.greet(barrier)
    beam.greet(barrier)

    for ref in (bsend, dsend, mx_ref, my_ref, lx_ref, ly_ref, tx_ref, ty_ref, tab_ref, back_ref):
        ref[...] = jnp.zeros(ref.shape, F32)

    lane = iota((N, N), 1)

    def total(step, acc, z, e, c):
        beam.put(step, 0, beam.spot(z, e, ELEMENTS), jnp.sum(c, 0, keepdims=True))
        return jnp.where(lane == det.spot(z, e, ELEMENTS), jnp.sum(c, 1, keepdims=True), acc)

    def first_totals():
        acc = jnp.zeros((N, N), F32)
        for z in range(ZS):
            conc_loads[z].wait()
            for e in range(ELEMENTS):
                acc = total(0, acc, z, e, c_ref[e, z])
        det.put_all(0, 0, acc.T)

    first_totals()
    pl.semaphore_wait(barrier, beam.count + det.count - 2)
    det.start(0, 0)
    beam.start(0, 0)
    for load in loads:
        load.wait()

    def tables():
        first = axis_ref[0:1, 0:1] == 0
        one, two = inc_ref[0:1, :], inc_ref[1:2, :]
        s1 = jnp.where(first, one, two)
        s2 = jnp.where(first, two, one)
        scale = -LOG2E * step_y
        sig, yld, rate = sig_ref[...], yld_ref[...], rate_ref[...]
        cols = pl.ds(0, ELEMENTS)
        tab_ref[0:LINES, cols] = scale * sig
        tab_ref[LINES : LINES + 1, cols] = scale * s2
        tab_ref[LINES + 1 : LINES + 2, cols] = scale * s1
        tab_ref[LINES + 2 : FIELDS, cols] = yld
        back_ref[0:LINES, cols] = yld * rate
        back_ref[LINES : 2 * LINES, cols] = -sig * rate
        back_ref[2 * LINES : 2 * LINES + 1, cols] = -s1 * rate
        back_ref[2 * LINES + 1 : FIELDS, cols] = -s2 * rate

        tab, back = tab_ref[...], back_ref[...]
        wide = 8 * ELEMENTS
        pick = one_hot((iota((8 * FIELDS, 32), 0) >> 3) == iota((8 * FIELDS, 32), 1))
        col = iota((N, 256), 1)
        part = (col >= wide).astype(jnp.int32) + (col >= 2 * wide).astype(jnp.int32)
        spread = one_hot(((col - wide * part) >> 3) == iota((N, 256), 0))
        spread = jnp.where(col < 3 * wide, spread, 0.0)
        full = exact(pick, exact(tab, spread))
        shape = (8 * FIELDS, 256)
        full = jnp.where((iota(shape, 0) & 7) == (iota(shape, 1) & 7), full, 0.0)
        high, low = split(full)
        part = iota(shape, 1)
        mix_ref[...] = jnp.where((part >= wide) & (part < 2 * wide), low.astype(F32), high.astype(F32)).astype(BF16)

        pick = one_hot((iota((wide, N), 0) >> 3) == iota((wide, N), 1))
        shape = (wide, 8 * FIELDS)
        spread = one_hot((iota((32, 8 * FIELDS), 1) >> 3) == iota((32, 8 * FIELDS), 0))
        full = exact(exact_nt(pick, back), spread)
        full = jnp.where((iota(shape, 0) & 7) == (iota(shape, 1) & 7), full, 0.0)
        high, low = split(full)
        unmix_ref[0:wide] = high
        unmix_ref[wide : 2 * wide] = low

        r, m = iota((16 * ZS, 32), 0) & 15, iota((16 * ZS, 32), 1)
        rates = exact(one_hot((r == m) & (r < LINES + 2)), tab)
        sums_x = exact(one_hot(m == jnp.where(r < LINES, r + LINES, 2 * LINES)), back)
        sums_y = exact(one_hot(m == jnp.where(r < LINES, r + LINES, 2 * LINES + 1)), back)
        r = iota((16 * ZS, N), 0) & 15
        sums_x = jnp.where(r <= LINES, -step_x * sums_x, 0.0)
        sums_y = jnp.where(r <= LINES, -step_y * sums_y, 0.0)

        def place(ring):
            shape = (8 * ring.count, N)
            per = -(-ELEMENTS // ring.tiles)
            row = iota(shape, 0) & (ring.wide - 1)
            inside = row & 7
            return one_hot((inside < per) & ((row >> 3) * per + inside == iota(shape, 1)))

        def same(shape, rows, cols):
            shift = lambda n: n.bit_length() - 1
            return (iota(shape, 0) >> shift(rows)) == (iota(shape, 1) >> shift(cols))

        place_x, place_y = place(beam), place(det)
        wax_ref[...] = jnp.where(
            same(wax_ref.shape, 16, beam.wide), exact_nt(rates * (step_x / step_y), place_x), 0.0
        )
        way_ref[...] = jnp.where(same(way_ref.shape, 16, det.wide), exact_nt(rates, place_y), 0.0)
        wcx_ref[...] = jnp.where(same(wcx_ref.shape, beam.wide, 16), exact_nt(place_x, sums_x), 0.0)
        wcy_ref[...] = jnp.where(same(wcy_ref.shape, det.wide, 16), exact_nt(place_y, sums_y), 0.0)

        r, c = iota((2 * N, N), 0) & (N - 1), iota((2 * N, N), 1)
        up_ref[...] = one_hot(r < c).astype(BF16)
        down_ref[...] = (step_y * one_hot(r > c)).astype(BF16)
        r, c = iota((N, 2 * N), 0), iota((N, 2 * N), 1) & (N - 1)
        left_ref[...] = (step_x / step_y * one_hot(c < r)).astype(BF16)
        right_ref[...] = (step_x * one_hot(c > r)).astype(BF16)
        for z in range(ZS):
            live1 = live1_ref[z : z + 1, :].astype(F32)
            live2 = live2_ref[z : z + 1, :].astype(F32)
            for l in range(LINES):
                x, y = beam.spot(z, l, LINES), det.spot(z, l, LINES)
                lx_ref[x : x + 1, :] = live1
                ly_ref[y : y + 1, :] = live2
                mx_ref[x : x + 1, :] = m1_ref[l, z : z + 1, :]
                my_ref[y : y + 1, :] = m2_ref[l, z : z + 1, :]

    tables()

    def blocks(body):
        def one(n, carry):
            body(n // 4, pl.multiple_of((n % 4) * 32, 32))
            return carry

        lax.fori_loop(0, 4 * ZS, one, 0)

    def mix(z, r0):
        parts = []
        for b in range(4):
            high, low = split(c_ref[:, z, pl.ds(r0 + 8 * b, 8), :].reshape(8 * ELEMENTS, N))
            parts.append(jnp.concatenate([high, high, low, jnp.zeros((16, N), BF16)], 0))
        out = dot(mix_ref[...], jnp.concatenate(parts, 1))
        for b in range(4):
            f_ref[z, :, pl.ds(r0 + 8 * b, 8), :] = out[:, b * N : (b + 1) * N].reshape(FIELDS, 8, N)

    def unmix(z, r0):
        highs, lows = [], []
        for b in range(4):
            rows = pl.ds(r0 + 8 * b, 8)
            w = a1_ref[z, :, rows, :].reshape(8 * LINES, N)
            v = f_ref[z, 0 : LINES + 2, rows, :].reshape(8 * (LINES + 2), N)
            high, low = split(jnp.concatenate([w, v], 0))
            highs.append(high)
            lows.append(low)
        wide = 8 * ELEMENTS
        one = dot(unmix_ref[...], jnp.concatenate(highs, 1))
        two = dot(unmix_ref[0:wide], jnp.concatenate(lows, 1))
        out = one[0:wide] + (one[wide:] + two)
        for b in range(4):
            rows = pl.ds(r0 + 8 * b, 8)
            c_ref[:, z, rows, :] = c_ref[:, z, rows, :] - out[:, b * N : (b + 1) * N].reshape(ELEMENTS, 8, N)

    def attenuate(z, carry):
        tin1 = jnp.exp2(cum_rows(f_ref[z, LINES + 1], left_ref[...]))
        tin2 = jnp.exp2(cum_cols(f_ref[z, LINES], up_ref[...]))
        for l in range(0, LINES, 2):
            high0, low0 = split(f_ref[z, l])
            high1, low1 = split(f_ref[z, l + 1])
            across = jnp.concatenate(
                [jnp.concatenate([high0, low0], 1), jnp.concatenate([high1, low1], 1)], 0
            )
            along = jnp.concatenate(
                [jnp.concatenate([high0, high1], 1), jnp.concatenate([low0, low1], 1)], 0
            )
            over_y = jnp.exp2(dot(across, up_ref[...]))
            over_x = jnp.exp2(dot(left_ref[...], along))
            for k in range(2):
                a1_ref[z, l + k] = tin1 * over_y[k * N : (k + 1) * N]
                a2_ref[z, l + k] = tin2 * over_x[:, k * N : (k + 1) * N]
        return carry

    def times(rows, wide, factors, k):
        parts = [
            rows[wide * z : wide * (z + 1)] * factors[16 * z + k : 16 * z + k + 1] for z in range(ZS)
        ]
        return jnp.concatenate(parts, 0)

    def counts(step):
        ex = jnp.exp2(exact(wax_ref[...], beam.rows(bdone, step, 0)))
        ey = jnp.exp2(exact(way_ref[...], det.rows(ddone, step, 0)))
        ex_ref[...], ey_ref[...] = ex, ey
        cols = jnp.concatenate([ey, jnp.zeros((N - 16 * ZS, N), F32)], 0).T
        acc = jnp.zeros((N, N), F32)
        for z in range(ZS):
            enter = step_x * ex[16 * z + LINES + 1 : 16 * z + LINES + 2]
            for l in range(LINES):
                q = f_ref[z, LINES + 2 + l]
                k = 16 * z + l
                a1 = a1_ref[z, l] * cols[:, k : k + 1]
                a1_ref[z, l] = a1
                beam.put(step, 1, beam.spot(z, l, LINES), enter * jnp.sum(q * a1, 0, keepdims=True))
                seen = jnp.sum(q * (a2_ref[z, l] * ex[k : k + 1]), 1, keepdims=True)
                acc = jnp.where(lane == det.spot(z, l, LINES), seen, acc)
        det.put_all(step, 1, step_y * times(acc.T, det.wide, ey, LINES))

    def residuals(step):
        ex, ey = ex_ref[...], ey_ref[...]
        res1 = lx_ref[...] * (beam.rows(bdone, step, 1) - mx_ref[...])
        res2 = ly_ref[...] * (det.rows(ddone, step, 1) - my_ref[...])
        sum1 = res1 * beam.rows(bsend, step, 1) / step_x
        sum2 = res2 * det.rows(dsend, step, 1) / step_y
        r1 = times(res1, beam.wide, ex, LINES + 1)
        r1_ref[...] = r1
        cols = times(res2, det.wide, ey, LINES).T
        s2c_ref[...] = cols
        acc = jnp.zeros((N, N), F32)
        for z in range(ZS):
            for l in range(LINES):
                q = f_ref[z, LINES + 2 + l]
                k, x, y = 16 * z + l, beam.spot(z, l, LINES), det.spot(z, l, LINES)
                seen = jnp.sum(q * (a1_ref[z, l] * r1[x : x + 1]), 1, keepdims=True)
                acc = jnp.where(lane == k, seen, acc)
                seen = jnp.sum(q * (a2_ref[z, l] * cols[:, y : y + 1]), 0, keepdims=True)
                tx_ref[k : k + 1, :] = ex[k : k + 1] * seen
        ty_ref[...] = acc.T[0 : 16 * ZS]
        for z in range(ZS):
            k = 16 * z + LINES
            tx_ref[k : k + 1, :] = jnp.sum(sum1[beam.wide * z : beam.wide * (z + 1)], 0, keepdims=True)
            ty_ref[k : k + 1, :] = jnp.sum(sum2[det.wide * z : det.wide * (z + 1)], 0, keepdims=True)
        beam.put_all(step, 2, exact(wcx_ref[...], tx_ref[...]))
        det.put_all(step, 2, exact(wcy_ref[...], ty_ref[...]))

    def weights():
        ex, r1, cols = ex_ref[...], r1_ref[...], s2c_ref[...]
        for z in range(ZS):
            sum1 = jnp.zeros((N, N), F32)
            sum2 = jnp.zeros((N, N), F32)
            for l in range(LINES):
                q = f_ref[z, LINES + 2 + l]
                k, x, y = 16 * z + l, beam.spot(z, l, LINES), det.spot(z, l, LINES)
                w1 = a1_ref[z, l] * r1[x : x + 1]
                w2 = a2_ref[z, l] * ex[k : k + 1] * cols[:, y : y + 1]
                a1_ref[z, l] = w1 + w2
                p1, p2 = q * w1, q * w2
                sum1, sum2 = sum1 + p1, sum2 + p2
                f_ref[z, l] = cum_cols(p1, down_ref[...]) + cum_rows(p2, right_ref[...])
            f_ref[z, LINES] = cum_rows(sum1, right_ref[...])
            f_ref[z, LINES + 1] = cum_cols(sum2, down_ref[...])

    def update(step):
        cols = det.rows(ddone, step, 2).T
        rows = beam.rows(bdone, step, 2)
        acc = jnp.zeros((N, N), F32)
        for z in range(ZS):
            for e in range(ELEMENTS):
                x, y = beam.spot(z, e, ELEMENTS), det.spot(z, e, ELEMENTS)
                c = c_ref[e, z] + rows[x : x + 1] + cols[:, y : y + 1]
                c_ref[e, z] = c
                acc = total(step + 1, acc, z, e, c)
        det.put_all(step + 1, 0, acc.T)

    def turn(step, carry):
        last = step == STEPS - 1
        blocks(mix)
        det.middle(step, 0, "earlier")
        beam.middle(step, 0, "earlier")
        lax.fori_loop(0, ZS, attenuate, 0)
        det.finish(step, 0)
        beam.finish(step, 0)
        counts(step)
        det.start(step, 1)
        beam.start(step, 1)
        det.middle(step, 1, "sum")
        beam.middle(step, 1, "sum")
        det.finish(step, 1)
        beam.finish(step, 1)
        residuals(step)
        det.start(step, 2)
        beam.start(step, 2)
        weights()
        det.middle(step, 2, "later")
        beam.middle(step, 2, "later")
        blocks(unmix)

        @pl.when(last)
        def leave():
            stores = [
                pltpu.make_async_copy(c_ref.at[:, z], out_hbm.at[:, z], conc_sems.at[z]) for z in range(ZS)
            ]
            for store in stores:
                store.start()
            for store in stores:
                store.wait()

        det.finish(step, 2)
        beam.finish(step, 2)

        @pl.when(jnp.logical_not(last))
        def go_on():
            update(step)
            det.start(step + 1, 0)
            beam.start(step + 1, 0)

        return carry

    lax.fori_loop(0, STEPS, turn, 0)
    dx_ref[...] = bdone[STEPS - 1, 2]
    dy_ref[...] = ddone[STEPS - 1, 2]


def close(x_spots, y_spots, c_ref, dx_ref, dy_ref, out_ref):
    rows = dx_ref[...].reshape(-1, N)
    cols = dy_ref[...].reshape(-1, N)
    cols = jnp.concatenate([cols, jnp.zeros((N - cols.shape[0], N), F32)], 0).T
    for e in range(ELEMENTS):
        x, y = x_spots[e], y_spots[e]
        out_ref[e, 0] = c_ref[e, 0] + rows[x : x + 1] + cols[:, y : y + 1]


def solution(mesh):
    beams, dets = mesh.shape["beam"], mesh.shape["det"]

    def shards(conc, inc, sig, yld, rate, axis, m1, live1, m2, live2):
        step_x = 1.0 / (conc.shape[2] * beams)
        step_y = 1.0 / (conc.shape[3] * dets)

        def body(*refs):
            kernel(step_x, step_y, *refs)

        def exchange(count):
            tiles = pltpu.VMEM((STEPS, 3, count, 8, N), F32)
            return [tiles] * 4 + [pltpu.SemaphoreType.DMA((STEPS, 3, 2, 2))]

        def spots(tiles):
            per = -(-ELEMENTS // tiles)
            return [8 * (e // per) + e % per for e in range(ELEMENTS)]

        field = (N, N)
        anywhere = pl.BlockSpec(memory_space=pl.ANY)
        vmem = pl.BlockSpec(memory_space=pltpu.VMEM)
        small = (axis[None], inc, sig, yld, rate[None], m1, live1, m2, live2)
        inner, dx, dy = pl.pallas_call(
            body,
            out_shape=[
                jax.ShapeDtypeStruct(conc.shape, F32),
                jax.ShapeDtypeStruct((beams, 8, N), F32),
                jax.ShapeDtypeStruct((dets, 8, N), F32),
            ],
            in_specs=[anywhere] * (len(small) + 1),
            out_specs=[anywhere, vmem, vmem],
            scratch_shapes=[
                *[pltpu.VMEM(a.shape, a.dtype) for a in small + (conc,)],
                pltpu.SemaphoreType.DMA((len(small),)),
                pltpu.SemaphoreType.DMA((ZS,)),
                pltpu.VMEM((ZS, FIELDS) + field, F32),
                pltpu.VMEM((ZS, LINES) + field, F32),
                pltpu.VMEM((ZS, LINES) + field, F32),
                *[pltpu.VMEM((16 * ZS, N), F32)] * 2,
                pltpu.VMEM((8 * beams, N), F32),
                pltpu.VMEM(field, F32),
                pltpu.VMEM((8 * beams, N), F32),
                pltpu.VMEM((8 * dets, N), F32),
                pltpu.VMEM((8 * beams, N), F32),
                pltpu.VMEM((8 * dets, N), F32),
                *[pltpu.VMEM((16 * ZS, N), F32)] * 2,
                *[pltpu.VMEM((32, N), F32)] * 2,
                pltpu.VMEM((8 * FIELDS, 2 * N), BF16),
                pltpu.VMEM((16 * ELEMENTS, 8 * FIELDS), BF16),
                *[pltpu.VMEM((2 * N, N), BF16)] * 2,
                *[pltpu.VMEM((N, 2 * N), BF16)] * 2,
                pltpu.VMEM((16 * ZS, 8 * beams), F32),
                pltpu.VMEM((16 * ZS, 8 * dets), F32),
                pltpu.VMEM((8 * beams, 16 * ZS), F32),
                pltpu.VMEM((8 * dets, 16 * ZS), F32),
                *exchange(beams),
                *exchange(dets),
            ],
            compiler_params=pltpu.CompilerParams(
                collective_id=0, has_side_effects=True, vmem_limit_bytes=64 * 1024 * 1024
            ),
        )(*small, conc)

        x_tiles, y_tiles = beams // ZS, dets // ZS

        def last(*refs):
            close(spots(x_tiles), spots(y_tiles), *refs)

        block = pl.BlockSpec((ELEMENTS, 1, N, N), lambda z: (0, z, 0, 0))
        return pl.pallas_call(
            last,
            out_shape=jax.ShapeDtypeStruct(conc.shape, F32),
            grid=(ZS,),
            in_specs=[
                block,
                pl.BlockSpec((x_tiles, 8, N), lambda z: (z, 0, 0)),
                pl.BlockSpec((y_tiles, 8, N), lambda z: (z, 0, 0)),
            ],
            out_specs=block,
            compiler_params=pltpu.CompilerParams(vmem_limit_bytes=64 * 1024 * 1024),
        )(inner, dx, dy)

    in_specs = (
        P(None, None, "beam", "det"),
        P(),
        P(),
        P(),
        P(),
        P(),
        P(None, None, "det"),
        P(None, "det"),
        P(None, None, "beam"),
        P(None, "beam"),
    )
    out_specs = P(None, None, "beam", "det")
    return jax.shard_map(shards, mesh=mesh, in_specs=in_specs, out_specs=out_specs, check_vma=False)
```

```python
import math

import jax
import jax.numpy as jnp
from jax import lax
from jax.experimental import pallas as pl
from jax.experimental.pallas import tpu as pltpu
from jax.sharding import PartitionSpec as P

STEPS = 2
HIGH = lax.Precision.HIGHEST
MESH = pl.DeviceIdType.MESH
F32 = jnp.float32
BF16 = jnp.bfloat16
ELEMENTS = 10
LINES = 12
ZS = 4
N = 128
FIELDS = 26
LOG2E = math.log2(math.e)


def split(value):
    high = value.astype(BF16)
    return high, (value - high.astype(F32)).astype(BF16)


def iota(shape, dim):
    return lax.broadcasted_iota(jnp.int32, shape, dim)


def dot(a, b):
    return jnp.dot(a, b, preferred_element_type=F32)


def exact(a, b):
    return jnp.dot(a, b, preferred_element_type=F32, precision=HIGH)


def exact_nt(a, b):
    return lax.dot_general(
        a, b, (((1,), (1,)), ((), ())), preferred_element_type=F32, precision=HIGH
    )


def one_hot(condition):
    return jnp.where(condition, 1.0, 0.0).astype(F32)


def cum_cols(value, table):
    high, low = split(value)
    return dot(jnp.concatenate([high, low], 1), table)


def cum_rows(value, table):
    high, low = split(value)
    return dot(table, jnp.concatenate([high, low], 0))


class Ring:
    def __init__(self, axis, send, recv, back, done, sems):
        self.axis = axis
        self.count = recv.shape[2]
        self.me = lax.axis_index(axis)
        self.send, self.recv, self.back, self.done, self.sems = send, recv, back, done, sems
        self.tiles = self.count // ZS
        self.wide = 8 * self.tiles
        half = self.count // 2
        self.hops = sorted(range(1, self.count), key=lambda d: (abs(d - half), d))

    def peer(self, d):
        return lax.rem(self.me + d, self.count)

    def greet(self, barrier):
        for d in self.hops:
            pl.semaphore_signal(barrier, inc=1, device_id={self.axis: self.peer(d)}, device_id_type=MESH)

    def copy(self, src, dst, step, phase, leg, peer):
        return pltpu.make_async_remote_copy(
            src_ref=src,
            dst_ref=dst,
            send_sem=self.sems.at[step, phase, leg, 0],
            recv_sem=self.sems.at[step, phase, leg, 1],
            device_id={self.axis: peer},
            device_id_type=MESH,
        )

    def start(self, step, phase):
        mine = (step, phase, pl.ds(self.me, 1))
        self.recv[mine] = self.send[mine]
        for d in self.hops:
            peer = self.peer(d)
            src, dst = self.send.at[step, phase, peer], self.recv.at[step, phase, self.me]
            self.copy(src, dst, step, phase, 0, peer).start()

    def wait(self, src, dst, step, phase, leg):
        several = (step, phase, pl.ds(0, self.count - 1))
        whole = self.copy(src.at[several], dst.at[several], step, phase, leg, self.peer(1))
        whole.wait_send()
        whole.wait_recv()

    def middle(self, step, phase, mode):
        self.wait(self.send, self.recv, step, phase, 0)
        total = jnp.zeros((8, N), F32)
        order = range(self.count)
        for t in reversed(order) if mode == "later" else order:
            if mode != "sum":
                self.back[step, phase, t] = total
            total = total + self.recv[step, phase, t]
        mine = (step, phase, pl.ds(self.me, 1))
        if mode == "sum":
            self.back[step, phase, 0] = total
            self.done[mine] = total[None]
        else:
            self.done[mine] = self.back[mine]
        for d in self.hops:
            peer = self.peer(d)
            src = self.back.at[step, phase, 0 if mode == "sum" else peer]
            self.copy(src, self.done.at[step, phase, self.me], step, phase, 1, peer).start()

    def finish(self, step, phase):
        self.wait(self.back, self.done, step, phase, 1)

    def spot(self, z, row, of):
        per = -(-of // self.tiles)
        return self.wide * z + 8 * (row // per) + row % per

    def rows(self, ref, step, phase):
        return ref[step, phase].reshape(8 * self.count, N)

    def put(self, step, phase, spot, value):
        self.send[step, phase, spot // 8, spot % 8 : spot % 8 + 1, :] = value

    def put_all(self, step, phase, rows):
        self.send[step, phase] = rows.reshape(self.count, 8, N)


def kernel(
    step_x, step_y,
    axis_hbm, inc_hbm, sig_hbm, yld_hbm, rate_hbm, m1_hbm, live1_hbm, m2_hbm, live2_hbm, conc_hbm,
    out_hbm, dx_ref, dy_ref,
    axis_ref, inc_ref, sig_ref, yld_ref, rate_ref, m1_ref, live1_ref, m2_ref, live2_ref, c_ref,
    load_sems, conc_sems,
    f_ref, a1_ref, a2_ref, ex_ref, ey_ref, r1_ref, s2c_ref, mx_ref, my_ref, lx_ref, ly_ref,
    tx_ref, ty_ref, tab_ref, back_ref, mix_ref, unmix_ref, up_ref, down_ref, left_ref, right_ref,
    wax_ref, way_ref, wcx_ref, wcy_ref,
    bsend, brecv, bback, bdone, bsems, dsend, drecv, dback, ddone, dsems,
):
    conc_loads = [
        pltpu.make_async_copy(conc_hbm.at[:, z], c_ref.at[:, z], conc_sems.at[z]) for z in range(ZS)
    ]
    hbm = (axis_hbm, inc_hbm, sig_hbm, yld_hbm, rate_hbm, m1_hbm, live1_hbm, m2_hbm, live2_hbm)
    vmem = (axis_ref, inc_ref, sig_ref, yld_ref, rate_ref, m1_ref, live1_ref, m2_ref, live2_ref)
    loads = [pltpu.make_async_copy(a, b, load_sems.at[k]) for k, (a, b) in enumerate(zip(hbm, vmem))]
    for load in conc_loads + loads:
        load.start()
    beam = Ring("beam", bsend, brecv, bback, bdone, bsems)
    det = Ring("det", dsend, drecv, dback, ddone, dsems)
    barrier = pltpu.get_barrier_semaphore()
    det.greet(barrier)
    beam.greet(barrier)

    for ref in (bsend, dsend, mx_ref, my_ref, lx_ref, ly_ref, tx_ref, ty_ref, tab_ref, back_ref):
        ref[...] = jnp.zeros(ref.shape, F32)

    lane = iota((N, N), 1)

    def total(step, acc, z, e, c):
        beam.put(step, 0, beam.spot(z, e, ELEMENTS), jnp.sum(c, 0, keepdims=True))
        return jnp.where(lane == det.spot(z, e, ELEMENTS), jnp.sum(c, 1, keepdims=True), acc)

    def first_totals():
        acc = jnp.zeros((N, N), F32)
        for z in range(ZS):
            conc_loads[z].wait()
            for e in range(ELEMENTS):
                acc = total(0, acc, z, e, c_ref[e, z])
        det.put_all(0, 0, acc.T)

    first_totals()
    pl.semaphore_wait(barrier, beam.count + det.count - 2)
    det.start(0, 0)
    beam.start(0, 0)
    for load in loads:
        load.wait()

    def tables():
        first = axis_ref[0:1, 0:1] == 0
        one, two = inc_ref[0:1, :], inc_ref[1:2, :]
        s1 = jnp.where(first, one, two)
        s2 = jnp.where(first, two, one)
        scale = -LOG2E * step_y
        sig, yld, rate = sig_ref[...], yld_ref[...], rate_ref[...]
        cols = pl.ds(0, ELEMENTS)
        tab_ref[0:LINES, cols] = scale * sig
        tab_ref[LINES : LINES + 1, cols] = scale * s2
        tab_ref[LINES + 1 : LINES + 2, cols] = scale * s1
        tab_ref[LINES + 2 : FIELDS, cols] = yld
        back_ref[0:LINES, cols] = yld * rate
        back_ref[LINES : 2 * LINES, cols] = -sig * rate
        back_ref[2 * LINES : 2 * LINES + 1, cols] = -s1 * rate
        back_ref[2 * LINES + 1 : FIELDS, cols] = -s2 * rate

        tab, back = tab_ref[...], back_ref[...]
        wide = 8 * ELEMENTS
        pick = one_hot((iota((8 * FIELDS, 32), 0) >> 3) == iota((8 * FIELDS, 32), 1))
        col = iota((N, 256), 1)
        part = (col >= wide).astype(jnp.int32) + (col >= 2 * wide).astype(jnp.int32)
        spread = one_hot(((col - wide * part) >> 3) == iota((N, 256), 0))
        spread = jnp.where(col < 3 * wide, spread, 0.0)
        full = exact(pick, exact(tab, spread))
        shape = (8 * FIELDS, 256)
        full = jnp.where((iota(shape, 0) & 7) == (iota(shape, 1) & 7), full, 0.0)
        high, low = split(full)
        part = iota(shape, 1)
        mix_ref[...] = jnp.where((part >= wide) & (part < 2 * wide), low.astype(F32), high.astype(F32)).astype(BF16)

        pick = one_hot((iota((wide, N), 0) >> 3) == iota((wide, N), 1))
        shape = (wide, 8 * FIELDS)
        spread = one_hot((iota((32, 8 * FIELDS), 1) >> 3) == iota((32, 8 * FIELDS), 0))
        full = exact(exact_nt(pick, back), spread)
        full = jnp.where((iota(shape, 0) & 7) == (iota(shape, 1) & 7), full, 0.0)
        high, low = split(full)
        unmix_ref[0:wide] = high
        unmix_ref[wide : 2 * wide] = low

        r, m = iota((16 * ZS, 32), 0) & 15, iota((16 * ZS, 32), 1)
        rates = exact(one_hot((r == m) & (r < LINES + 2)), tab)
        sums_x = exact(one_hot(m == jnp.where(r < LINES, r + LINES, 2 * LINES)), back)
        sums_y = exact(one_hot(m == jnp.where(r < LINES, r + LINES, 2 * LINES + 1)), back)
        r = iota((16 * ZS, N), 0) & 15
        sums_x = jnp.where(r <= LINES, -step_x * sums_x, 0.0)
        sums_y = jnp.where(r <= LINES, -step_y * sums_y, 0.0)

        def place(ring):
            shape = (8 * ring.count, N)
            per = -(-ELEMENTS // ring.tiles)
            row = iota(shape, 0) & (ring.wide - 1)
            inside = row & 7
            return one_hot((inside < per) & ((row >> 3) * per + inside == iota(shape, 1)))

        def same(shape, rows, cols):
            shift = lambda n: n.bit_length() - 1
            return (iota(shape, 0) >> shift(rows)) == (iota(shape, 1) >> shift(cols))

        place_x, place_y = place(beam), place(det)
        wax_ref[...] = jnp.where(
            same(wax_ref.shape, 16, beam.wide), exact_nt(rates * (step_x / step_y), place_x), 0.0
        )
        way_ref[...] = jnp.where(same(way_ref.shape, 16, det.wide), exact_nt(rates, place_y), 0.0)
        wcx_ref[...] = jnp.where(same(wcx_ref.shape, beam.wide, 16), exact_nt(place_x, sums_x), 0.0)
        wcy_ref[...] = jnp.where(same(wcy_ref.shape, det.wide, 16), exact_nt(place_y, sums_y), 0.0)

        r, c = iota((2 * N, N), 0) & (N - 1), iota((2 * N, N), 1)
        up_ref[...] = one_hot(r < c).astype(BF16)
        down_ref[...] = (step_y * one_hot(r > c)).astype(BF16)
        r, c = iota((N, 2 * N), 0), iota((N, 2 * N), 1) & (N - 1)
        left_ref[...] = (step_x / step_y * one_hot(c < r)).astype(BF16)
        right_ref[...] = (step_x * one_hot(c > r)).astype(BF16)
        for z in range(ZS):
            live1 = live1_ref[z : z + 1, :].astype(F32)
            live2 = live2_ref[z : z + 1, :].astype(F32)
            for l in range(LINES):
                x, y = beam.spot(z, l, LINES), det.spot(z, l, LINES)
                lx_ref[x : x + 1, :] = live1
                ly_ref[y : y + 1, :] = live2
                mx_ref[x : x + 1, :] = m1_ref[l, z : z + 1, :]
                my_ref[y : y + 1, :] = m2_ref[l, z : z + 1, :]

    tables()

    def blocks(body):
        def one(z, carry):
            for r0 in range(0, N, 32):
                body(z, r0)
            return carry

        lax.fori_loop(0, ZS, one, 0)

    def mix(z, r0):
        parts = []
        for b in range(4):
            high, low = split(c_ref[:, z, pl.ds(r0 + 8 * b, 8), :].reshape(8 * ELEMENTS, N))
            parts.append(jnp.concatenate([high, high, low, jnp.zeros((16, N), BF16)], 0))
        out = dot(mix_ref[...], jnp.concatenate(parts, 1))
        for b in range(4):
            f_ref[z, :, pl.ds(r0 + 8 * b, 8), :] = out[:, b * N : (b + 1) * N].reshape(FIELDS, 8, N)

    def unmix(z, r0):
        highs, lows = [], []
        for b in range(4):
            rows = pl.ds(r0 + 8 * b, 8)
            w = a1_ref[z, :, rows, :].reshape(8 * LINES, N)
            v = f_ref[z, 0 : LINES + 2, rows, :].reshape(8 * (LINES + 2), N)
            high, low = split(jnp.concatenate([w, v], 0))
            highs.append(high)
            lows.append(low)
        wide = 8 * ELEMENTS
        one = dot(unmix_ref[...], jnp.concatenate(highs, 1))
        two = dot(unmix_ref[0:wide], jnp.concatenate(lows, 1))
        out = one[0:wide] + (one[wide:] + two)
        for b in range(4):
            rows = pl.ds(r0 + 8 * b, 8)
            c_ref[:, z, rows, :] = c_ref[:, z, rows, :] - out[:, b * N : (b + 1) * N].reshape(ELEMENTS, 8, N)

    def attenuate(z, carry):
        tin1 = jnp.exp2(cum_rows(f_ref[z, LINES + 1], left_ref[...]))
        tin2 = jnp.exp2(cum_cols(f_ref[z, LINES], up_ref[...]))
        for l in range(0, LINES, 2):
            high0, low0 = split(f_ref[z, l])
            high1, low1 = split(f_ref[z, l + 1])
            across = jnp.concatenate(
                [jnp.concatenate([high0, low0], 1), jnp.concatenate([high1, low1], 1)], 0
            )
            along = jnp.concatenate(
                [jnp.concatenate([high0, high1], 1), jnp.concatenate([low0, low1], 1)], 0
            )
            over_y = jnp.exp2(dot(across, up_ref[...]))
            over_x = jnp.exp2(dot(left_ref[...], along))
            for k in range(2):
                a1_ref[z, l + k] = tin1 * over_y[k * N : (k + 1) * N]
                a2_ref[z, l + k] = tin2 * over_x[:, k * N : (k + 1) * N]
        return carry

    def times(rows, wide, factors, k):
        parts = [
            rows[wide * z : wide * (z + 1)] * factors[16 * z + k : 16 * z + k + 1] for z in range(ZS)
        ]
        return jnp.concatenate(parts, 0)

    def counts(step):
        ex = jnp.exp2(exact(wax_ref[...], beam.rows(bdone, step, 0)))
        ey = jnp.exp2(exact(way_ref[...], det.rows(ddone, step, 0)))
        ex_ref[...], ey_ref[...] = ex, ey
        cols = jnp.concatenate([ey, jnp.zeros((N - 16 * ZS, N), F32)], 0).T
        acc = jnp.zeros((N, N), F32)
        for z in range(ZS):
            enter = step_x * ex[16 * z + LINES + 1 : 16 * z + LINES + 2]
            for l in range(LINES):
                q = f_ref[z, LINES + 2 + l]
                k = 16 * z + l
                a1 = a1_ref[z, l] * cols[:, k : k + 1]
                a1_ref[z, l] = a1
                beam.put(step, 1, beam.spot(z, l, LINES), enter * jnp.sum(q * a1, 0, keepdims=True))
                seen = jnp.sum(q * (a2_ref[z, l] * ex[k : k + 1]), 1, keepdims=True)
                acc = jnp.where(lane == det.spot(z, l, LINES), seen, acc)
        det.put_all(step, 1, step_y * times(acc.T, det.wide, ey, LINES))

    def residuals(step):
        ex, ey = ex_ref[...], ey_ref[...]
        res1 = lx_ref[...] * (beam.rows(bdone, step, 1) - mx_ref[...])
        res2 = ly_ref[...] * (det.rows(ddone, step, 1) - my_ref[...])
        sum1 = res1 * beam.rows(bsend, step, 1) / step_x
        sum2 = res2 * det.rows(dsend, step, 1) / step_y
        r1 = times(res1, beam.wide, ex, LINES + 1)
        r1_ref[...] = r1
        cols = times(res2, det.wide, ey, LINES).T
        s2c_ref[...] = cols
        acc = jnp.zeros((N, N), F32)
        for z in range(ZS):
            for l in range(LINES):
                q = f_ref[z, LINES + 2 + l]
                k, x, y = 16 * z + l, beam.spot(z, l, LINES), det.spot(z, l, LINES)
                seen = jnp.sum(q * (a1_ref[z, l] * r1[x : x + 1]), 1, keepdims=True)
                acc = jnp.where(lane == k, seen, acc)
                seen = jnp.sum(q * (a2_ref[z, l] * cols[:, y : y + 1]), 0, keepdims=True)
                tx_ref[k : k + 1, :] = ex[k : k + 1] * seen
        ty_ref[...] = acc.T[0 : 16 * ZS]
        for z in range(ZS):
            k = 16 * z + LINES
            tx_ref[k : k + 1, :] = jnp.sum(sum1[beam.wide * z : beam.wide * (z + 1)], 0, keepdims=True)
            ty_ref[k : k + 1, :] = jnp.sum(sum2[det.wide * z : det.wide * (z + 1)], 0, keepdims=True)
        beam.put_all(step, 2, exact(wcx_ref[...], tx_ref[...]))
        det.put_all(step, 2, exact(wcy_ref[...], ty_ref[...]))

    def weights():
        ex, r1, cols = ex_ref[...], r1_ref[...], s2c_ref[...]
        for z in range(ZS):
            sum1 = jnp.zeros((N, N), F32)
            sum2 = jnp.zeros((N, N), F32)
            for l in range(LINES):
                q = f_ref[z, LINES + 2 + l]
                k, x, y = 16 * z + l, beam.spot(z, l, LINES), det.spot(z, l, LINES)
                w1 = a1_ref[z, l] * r1[x : x + 1]
                w2 = a2_ref[z, l] * ex[k : k + 1] * cols[:, y : y + 1]
                a1_ref[z, l] = w1 + w2
                p1, p2 = q * w1, q * w2
                sum1, sum2 = sum1 + p1, sum2 + p2
                f_ref[z, l] = cum_cols(p1, down_ref[...]) + cum_rows(p2, right_ref[...])
            f_ref[z, LINES] = cum_rows(sum1, right_ref[...])
            f_ref[z, LINES + 1] = cum_cols(sum2, down_ref[...])

    def update(step):
        cols = det.rows(ddone, step, 2).T
        rows = beam.rows(bdone, step, 2)
        acc = jnp.zeros((N, N), F32)
        for z in range(ZS):
            for e in range(ELEMENTS):
                x, y = beam.spot(z, e, ELEMENTS), det.spot(z, e, ELEMENTS)
                c = c_ref[e, z] + rows[x : x + 1] + cols[:, y : y + 1]
                c_ref[e, z] = c
                acc = total(step + 1, acc, z, e, c)
        det.put_all(step + 1, 0, acc.T)

    def turn(step, carry):
        last = step == STEPS - 1
        blocks(mix)
        det.middle(step, 0, "earlier")
        beam.middle(step, 0, "earlier")
        lax.fori_loop(0, ZS, attenuate, 0)
        det.finish(step, 0)
        beam.finish(step, 0)
        counts(step)
        det.start(step, 1)
        beam.start(step, 1)
        det.middle(step, 1, "sum")
        beam.middle(step, 1, "sum")
        det.finish(step, 1)
        beam.finish(step, 1)
        residuals(step)
        det.start(step, 2)
        beam.start(step, 2)
        weights()
        det.middle(step, 2, "later")
        beam.middle(step, 2, "later")
        blocks(unmix)

        @pl.when(last)
        def leave():
            stores = [
                pltpu.make_async_copy(c_ref.at[:, z], out_hbm.at[:, z], conc_sems.at[z]) for z in range(ZS)
            ]
            for store in stores:
                store.start()
            for store in stores:
                store.wait()

        det.finish(step, 2)
        beam.finish(step, 2)

        @pl.when(jnp.logical_not(last))
        def go_on():
            update(step)
            det.start(step + 1, 0)
            beam.start(step + 1, 0)

        return carry

    lax.fori_loop(0, STEPS, turn, 0)
    dx_ref[...] = bdone[STEPS - 1, 2]
    dy_ref[...] = ddone[STEPS - 1, 2]


def close(x_spots, y_spots, c_ref, dx_ref, dy_ref, out_ref):
    rows = dx_ref[...].reshape(-1, N)
    cols = dy_ref[...].reshape(-1, N)
    cols = jnp.concatenate([cols, jnp.zeros((N - cols.shape[0], N), F32)], 0).T
    for e in range(ELEMENTS):
        x, y = x_spots[e], y_spots[e]
        out_ref[e, 0] = c_ref[e, 0] + rows[x : x + 1] + cols[:, y : y + 1]


def solution(mesh):
    beams, dets = mesh.shape["beam"], mesh.shape["det"]

    def shards(conc, inc, sig, yld, rate, axis, m1, live1, m2, live2):
        step_x = 1.0 / (conc.shape[2] * beams)
        step_y = 1.0 / (conc.shape[3] * dets)

        def body(*refs):
            kernel(step_x, step_y, *refs)

        def exchange(count):
            tiles = pltpu.VMEM((STEPS, 3, count, 8, N), F32)
            return [tiles] * 4 + [pltpu.SemaphoreType.DMA((STEPS, 3, 2, 2))]

        def spots(tiles):
            per = -(-ELEMENTS // tiles)
            return [8 * (e // per) + e % per for e in range(ELEMENTS)]

        field = (N, N)
        anywhere = pl.BlockSpec(memory_space=pl.ANY)
        vmem = pl.BlockSpec(memory_space=pltpu.VMEM)
        small = (axis[None], inc, sig, yld, rate[None], m1, live1, m2, live2)
        inner, dx, dy = pl.pallas_call(
            body,
            out_shape=[
                jax.ShapeDtypeStruct(conc.shape, F32),
                jax.ShapeDtypeStruct((beams, 8, N), F32),
                jax.ShapeDtypeStruct((dets, 8, N), F32),
            ],
            in_specs=[anywhere] * (len(small) + 1),
            out_specs=[anywhere, vmem, vmem],
            scratch_shapes=[
                *[pltpu.VMEM(a.shape, a.dtype) for a in small + (conc,)],
                pltpu.SemaphoreType.DMA((len(small),)),
                pltpu.SemaphoreType.DMA((ZS,)),
                pltpu.VMEM((ZS, FIELDS) + field, F32),
                pltpu.VMEM((ZS, LINES) + field, F32),
                pltpu.VMEM((ZS, LINES) + field, F32),
                *[pltpu.VMEM((16 * ZS, N), F32)] * 2,
                pltpu.VMEM((8 * beams, N), F32),
                pltpu.VMEM(field, F32),
                pltpu.VMEM((8 * beams, N), F32),
                pltpu.VMEM((8 * dets, N), F32),
                pltpu.VMEM((8 * beams, N), F32),
                pltpu.VMEM((8 * dets, N), F32),
                *[pltpu.VMEM((16 * ZS, N), F32)] * 2,
                *[pltpu.VMEM((32, N), F32)] * 2,
                pltpu.VMEM((8 * FIELDS, 2 * N), BF16),
                pltpu.VMEM((16 * ELEMENTS, 8 * FIELDS), BF16),
                *[pltpu.VMEM((2 * N, N), BF16)] * 2,
                *[pltpu.VMEM((N, 2 * N), BF16)] * 2,
                pltpu.VMEM((16 * ZS, 8 * beams), F32),
                pltpu.VMEM((16 * ZS, 8 * dets), F32),
                pltpu.VMEM((8 * beams, 16 * ZS), F32),
                pltpu.VMEM((8 * dets, 16 * ZS), F32),
                *exchange(beams),
                *exchange(dets),
            ],
            compiler_params=pltpu.CompilerParams(
                collective_id=0, has_side_effects=True, vmem_limit_bytes=64 * 1024 * 1024
            ),
        )(*small, conc)

        x_tiles, y_tiles = beams // ZS, dets // ZS

        def last(*refs):
            close(spots(x_tiles), spots(y_tiles), *refs)

        block = pl.BlockSpec((ELEMENTS, 1, N, N), lambda z: (0, z, 0, 0))
        return pl.pallas_call(
            last,
            out_shape=jax.ShapeDtypeStruct(conc.shape, F32),
            grid=(ZS,),
            in_specs=[
                block,
                pl.BlockSpec((x_tiles, 8, N), lambda z: (z, 0, 0)),
                pl.BlockSpec((y_tiles, 8, N), lambda z: (z, 0, 0)),
            ],
            out_specs=block,
            compiler_params=pltpu.CompilerParams(vmem_limit_bytes=64 * 1024 * 1024),
        )(inner, dx, dy)

    in_specs = (
        P(None, None, "beam", "det"),
        P(),
        P(),
        P(),
        P(),
        P(),
        P(None, None, "det"),
        P(None, "det"),
        P(None, None, "beam"),
        P(None, "beam"),
    )
    out_specs = P(None, None, "beam", "det")
    return jax.shard_map(shards, mesh=mesh, in_specs=in_specs, out_specs=out_specs, check_vma=False)
```

```python
import math

import jax
import jax.numpy as jnp
from jax import lax
from jax.experimental import pallas as pl
from jax.experimental.pallas import tpu as pltpu
from jax.sharding import PartitionSpec as P

STEPS = 2
HIGH = lax.Precision.HIGHEST
MESH = pl.DeviceIdType.MESH
F32 = jnp.float32
BF16 = jnp.bfloat16
ELEMENTS = 10
LINES = 12
ZS = 4
N = 128
FIELDS = 26
GROUPS = 2
PER = ZS // GROUPS
LOG2E = math.log2(math.e)


def split(value):
    high = value.astype(BF16)
    return high, (value - high.astype(F32)).astype(BF16)


def iota(shape, dim):
    return lax.broadcasted_iota(jnp.int32, shape, dim)


def dot(a, b):
    return jnp.dot(a, b, preferred_element_type=F32)


def exact(a, b):
    return jnp.dot(a, b, preferred_element_type=F32, precision=HIGH)


def exact_nt(a, b):
    return lax.dot_general(
        a, b, (((1,), (1,)), ((), ())), preferred_element_type=F32, precision=HIGH
    )


def one_hot(condition):
    return jnp.where(condition, 1.0, 0.0).astype(F32)


def cum_cols(value, table):
    high, low = split(value)
    return dot(jnp.concatenate([high, low], 1), table)


def cum_rows(value, table):
    high, low = split(value)
    return dot(table, jnp.concatenate([high, low], 0))


class Ring:
    def __init__(self, axis, send, recv, back, done, sems):
        self.axis = axis
        self.count = recv.shape[2]
        self.me = lax.axis_index(axis)
        self.send, self.recv, self.back, self.done, self.sems = send, recv, back, done, sems
        self.tiles = self.count // ZS
        self.wide = 8 * self.tiles
        self.run = self.count // GROUPS
        half = self.count // 2
        self.hops = sorted(range(1, self.count), key=lambda d: (abs(d - half), d))

    def peer(self, d):
        return lax.rem(self.me + d, self.count)

    def owns(self, g):
        return (self.me >= g * self.run) & (self.me < (g + 1) * self.run)

    def greet(self, barrier):
        for d in self.hops:
            pl.semaphore_signal(barrier, inc=1, device_id={self.axis: self.peer(d)}, device_id_type=MESH)

    def copy(self, src, dst, step, phase, out, into, peer):
        return pltpu.make_async_remote_copy(
            src_ref=src,
            dst_ref=dst,
            send_sem=self.sems.at[step, phase, out],
            recv_sem=self.sems.at[step, phase, into],
            device_id={self.axis: peer},
            device_id_type=MESH,
        )

    def whole(self, src, dst, step, phase, out, into, tiles):
        some = (step, phase, pl.ds(0, tiles))
        return self.copy(src.at[some], dst.at[some], step, phase, out, into, self.peer(1))

    def start(self, step, phase, g):
        def one(d):
            owner = g * self.run + lax.rem(self.me + d, self.run)
            src, dst = self.send.at[step, phase, owner], self.recv.at[step, phase, self.me]
            self.copy(src, dst, step, phase, 0, 1, owner).start()

        @pl.when(self.owns(g))
        def keep():
            mine = (step, phase, pl.ds(self.me, 1))
            self.recv[mine] = self.send[mine]

        @pl.when(jnp.logical_not(self.owns(g)))
        def first():
            one(0)

        for d in range(1, self.run):
            one(d)

    def middle(self, step, phase, g, mode):
        @pl.when(self.owns(g))
        def owner():
            self.whole(self.send, self.recv, step, phase, 0, 1, self.count - 1).wait_recv()
            total = jnp.zeros((8, N), F32)
            order = range(self.count)
            for t in reversed(order) if mode == "later" else order:
                if mode != "sum":
                    self.back[step, phase, t] = total
                total = total + self.recv[step, phase, t]
            mine = (step, phase, pl.ds(self.me, 1))
            if mode == "sum":
                self.back[step, phase, 0] = total
                self.done[mine] = total[None]
            else:
                self.done[mine] = self.back[mine]
            for d in self.hops:
                peer = self.peer(d)
                src = self.back.at[step, phase, 0 if mode == "sum" else peer]
                self.copy(src, self.done.at[step, phase, self.me], step, phase, 2, 3 + g, peer).start()

    def finish(self, step, phase, g):
        @pl.when(self.owns(g))
        def others():
            self.whole(self.back, self.done, step, phase, 2, 3 + g, self.run - 1).wait_recv()

        @pl.when(jnp.logical_not(self.owns(g)))
        def all_of_them():
            self.whole(self.back, self.done, step, phase, 2, 3 + g, self.run).wait_recv()

    def settle(self, step, phase):
        self.whole(self.send, self.recv, step, phase, 0, 1, self.count - 1).wait_send()
        self.whole(self.back, self.done, step, phase, 2, 3, self.count - 1).wait_send()

    def spot(self, z, row, of):
        per = -(-of // self.tiles)
        return self.wide * (z % PER) + 8 * (row // per) + row % per

    def rows(self, ref, step, phase, g):
        return ref[step, phase, g * self.run : (g + 1) * self.run].reshape(8 * self.run, N)

    def put(self, step, phase, g, spot, value):
        self.send[step, phase, g * self.run + spot // 8, spot % 8 : spot % 8 + 1, :] = value

    def put_all(self, step, phase, g, rows):
        self.send[step, phase, g * self.run : (g + 1) * self.run] = rows.reshape(self.run, 8, N)


def kernel(
    step_x, step_y,
    axis_hbm, inc_hbm, sig_hbm, yld_hbm, rate_hbm, m1_hbm, live1_hbm, m2_hbm, live2_hbm, conc_hbm,
    out_hbm, dx_ref, dy_ref,
    axis_ref, inc_ref, sig_ref, yld_ref, rate_ref, m1_ref, live1_ref, m2_ref, live2_ref, c_ref,
    load_sems, conc_sems,
    f_ref, a1_ref, a2_ref, ex_ref, ey_ref, r1_ref, s2c_ref, mx_ref, my_ref, lx_ref, ly_ref,
    tx_ref, ty_ref, tab_ref, back_ref, mix_ref, unmix_ref, up_ref, down_ref, left_ref, right_ref,
    wax_ref, way_ref, wcx_ref, wcy_ref,
    bsend, brecv, bback, bdone, bsems, dsend, drecv, dback, ddone, dsems,
):
    conc_loads = [
        pltpu.make_async_copy(conc_hbm.at[:, z], c_ref.at[:, z], conc_sems.at[z]) for z in range(ZS)
    ]
    hbm = (axis_hbm, inc_hbm, sig_hbm, yld_hbm, rate_hbm, m1_hbm, live1_hbm, m2_hbm, live2_hbm)
    vmem = (axis_ref, inc_ref, sig_ref, yld_ref, rate_ref, m1_ref, live1_ref, m2_ref, live2_ref)
    loads = [pltpu.make_async_copy(a, b, load_sems.at[k]) for k, (a, b) in enumerate(zip(hbm, vmem))]
    for load in conc_loads + loads:
        load.start()
    beam = Ring("beam", bsend, brecv, bback, bdone, bsems)
    det = Ring("det", dsend, drecv, dback, ddone, dsems)
    barrier = pltpu.get_barrier_semaphore()
    det.greet(barrier)
    beam.greet(barrier)

    for ref in (bsend, dsend, mx_ref, my_ref, lx_ref, ly_ref, tx_ref, ty_ref, tab_ref, back_ref):
        ref[...] = jnp.zeros(ref.shape, F32)

    lane = iota((N, N), 1)

    def members(g):
        return range(g * PER, (g + 1) * PER)

    def send_off(step, phase, g):
        det.start(step, phase, g)
        beam.start(step, phase, g)

    def pass_on(step, phase, g, mode):
        det.middle(step, phase, g, mode)
        beam.middle(step, phase, g, mode)

    def take(step, phase, g):
        det.finish(step, phase, g)
        beam.finish(step, phase, g)

    def total(step, acc, z, e, c):
        beam.put(step, 0, z // PER, beam.spot(z, e, ELEMENTS), jnp.sum(c, 0, keepdims=True))
        return jnp.where(lane == det.spot(z, e, ELEMENTS), jnp.sum(c, 1, keepdims=True), acc)

    def first_totals(g):
        acc = jnp.zeros((N, N), F32)
        for z in members(g):
            conc_loads[z].wait()
            for e in range(ELEMENTS):
                acc = total(0, acc, z, e, c_ref[e, z])
        det.put_all(0, 0, g, acc.T[0 : det.wide * PER])

    first_totals(0)
    pl.semaphore_wait(barrier, beam.count + det.count - 2)
    send_off(0, 0, 0)
    first_totals(1)
    send_off(0, 0, 1)
    for load in loads:
        load.wait()

    def tables():
        first = axis_ref[0:1, 0:1] == 0
        one, two = inc_ref[0:1, :], inc_ref[1:2, :]
        s1 = jnp.where(first, one, two)
        s2 = jnp.where(first, two, one)
        scale = -LOG2E * step_y
        sig, yld, rate = sig_ref[...], yld_ref[...], rate_ref[...]
        cols = pl.ds(0, ELEMENTS)
        tab_ref[0:LINES, cols] = scale * sig
        tab_ref[LINES : LINES + 1, cols] = scale * s2
        tab_ref[LINES + 1 : LINES + 2, cols] = scale * s1
        tab_ref[LINES + 2 : FIELDS, cols] = yld
        back_ref[0:LINES, cols] = yld * rate
        back_ref[LINES : 2 * LINES, cols] = -sig * rate
        back_ref[2 * LINES : 2 * LINES + 1, cols] = -s1 * rate
        back_ref[2 * LINES + 1 : FIELDS, cols] = -s2 * rate

        tab, back = tab_ref[...], back_ref[...]
        wide = 8 * ELEMENTS
        pick = one_hot((iota((8 * FIELDS, 32), 0) >> 3) == iota((8 * FIELDS, 32), 1))
        col = iota((N, 256), 1)
        part = (col >= wide).astype(jnp.int32) + (col >= 2 * wide).astype(jnp.int32)
        spread = one_hot(((col - wide * part) >> 3) == iota((N, 256), 0))
        spread = jnp.where(col < 3 * wide, spread, 0.0)
        full = exact(pick, exact(tab, spread))
        shape = (8 * FIELDS, 256)
        full = jnp.where((iota(shape, 0) & 7) == (iota(shape, 1) & 7), full, 0.0)
        high, low = split(full)
        part = iota(shape, 1)
        mix_ref[...] = jnp.where((part >= wide) & (part < 2 * wide), low.astype(F32), high.astype(F32)).astype(BF16)

        pick = one_hot((iota((wide, N), 0) >> 3) == iota((wide, N), 1))
        shape = (wide, 8 * FIELDS)
        spread = one_hot((iota((32, 8 * FIELDS), 1) >> 3) == iota((32, 8 * FIELDS), 0))
        full = exact(exact_nt(pick, back), spread)
        full = jnp.where((iota(shape, 0) & 7) == (iota(shape, 1) & 7), full, 0.0)
        high, low = split(full)
        unmix_ref[0:wide] = high
        unmix_ref[wide : 2 * wide] = low

        r, m = iota((16 * PER, 32), 0) & 15, iota((16 * PER, 32), 1)
        rates = exact(one_hot((r == m) & (r < LINES + 2)), tab)
        sums_x = exact(one_hot(m == jnp.where(r < LINES, r + LINES, 2 * LINES)), back)
        sums_y = exact(one_hot(m == jnp.where(r < LINES, r + LINES, 2 * LINES + 1)), back)
        r = iota((16 * PER, N), 0) & 15
        sums_x = jnp.where(r <= LINES, -step_x * sums_x, 0.0)
        sums_y = jnp.where(r <= LINES, -step_y * sums_y, 0.0)

        def place(ring):
            shape = (8 * ring.run, N)
            per = -(-ELEMENTS // ring.tiles)
            row = iota(shape, 0) & (ring.wide - 1)
            inside = row & 7
            return one_hot((inside < per) & ((row >> 3) * per + inside == iota(shape, 1)))

        def same(shape, rows, cols):
            shift = lambda n: n.bit_length() - 1
            return (iota(shape, 0) >> shift(rows)) == (iota(shape, 1) >> shift(cols))

        place_x, place_y = place(beam), place(det)
        wax_ref[...] = jnp.where(
            same(wax_ref.shape, 16, beam.wide), exact_nt(rates * (step_x / step_y), place_x), 0.0
        )
        way_ref[...] = jnp.where(same(way_ref.shape, 16, det.wide), exact_nt(rates, place_y), 0.0)
        wcx_ref[...] = jnp.where(same(wcx_ref.shape, beam.wide, 16), exact_nt(place_x, sums_x), 0.0)
        wcy_ref[...] = jnp.where(same(wcy_ref.shape, det.wide, 16), exact_nt(place_y, sums_y), 0.0)

        r, c = iota((2 * N, N), 0) & (N - 1), iota((2 * N, N), 1)
        up_ref[...] = one_hot(r < c).astype(BF16)
        down_ref[...] = (step_y * one_hot(r > c)).astype(BF16)
        r, c = iota((N, 2 * N), 0), iota((N, 2 * N), 1) & (N - 1)
        left_ref[...] = (step_x / step_y * one_hot(c < r)).astype(BF16)
        right_ref[...] = (step_x * one_hot(c > r)).astype(BF16)
        for z in range(ZS):
            live1 = live1_ref[z : z + 1, :].astype(F32)
            live2 = live2_ref[z : z + 1, :].astype(F32)
            for l in range(LINES):
                g, x, y = z // PER, beam.spot(z, l, LINES), det.spot(z, l, LINES)
                lx_ref[g, x : x + 1, :] = live1
                ly_ref[g, y : y + 1, :] = live2
                mx_ref[g, x : x + 1, :] = m1_ref[l, z : z + 1, :]
                my_ref[g, y : y + 1, :] = m2_ref[l, z : z + 1, :]

    tables()
    pass_on(0, 0, 0, "earlier")

    def blocks(g, body):
        def one(z, carry):
            for r0 in range(0, N, 32):
                body(z, r0)
            return carry

        lax.fori_loop(g * PER, (g + 1) * PER, one, 0)

    def mix(z, r0):
        parts = []
        for b in range(4):
            high, low = split(c_ref[:, z, pl.ds(r0 + 8 * b, 8), :].reshape(8 * ELEMENTS, N))
            parts.append(jnp.concatenate([high, high, low, jnp.zeros((16, N), BF16)], 0))
        out = dot(mix_ref[...], jnp.concatenate(parts, 1))
        for b in range(4):
            f_ref[z, :, pl.ds(r0 + 8 * b, 8), :] = out[:, b * N : (b + 1) * N].reshape(FIELDS, 8, N)

    def unmix(z, r0):
        highs, lows = [], []
        for b in range(4):
            rows = pl.ds(r0 + 8 * b, 8)
            w = a1_ref[z, :, rows, :].reshape(8 * LINES, N)
            v = f_ref[z, 0 : LINES + 2, rows, :].reshape(8 * (LINES + 2), N)
            high, low = split(jnp.concatenate([w, v], 0))
            highs.append(high)
            lows.append(low)
        wide = 8 * ELEMENTS
        one = dot(unmix_ref[...], jnp.concatenate(highs, 1))
        two = dot(unmix_ref[0:wide], jnp.concatenate(lows, 1))
        out = one[0:wide] + (one[wide:] + two)
        for b in range(4):
            rows = pl.ds(r0 + 8 * b, 8)
            c_ref[:, z, rows, :] = c_ref[:, z, rows, :] - out[:, b * N : (b + 1) * N].reshape(ELEMENTS, 8, N)

    def attenuate(z, carry):
        tin1 = jnp.exp2(cum_rows(f_ref[z, LINES + 1], left_ref[...]))
        tin2 = jnp.exp2(cum_cols(f_ref[z, LINES], up_ref[...]))
        for l in range(0, LINES, 2):
            high0, low0 = split(f_ref[z, l])
            high1, low1 = split(f_ref[z, l + 1])
            across = jnp.concatenate(
                [jnp.concatenate([high0, low0], 1), jnp.concatenate([high1, low1], 1)], 0
            )
            along = jnp.concatenate(
                [jnp.concatenate([high0, high1], 1), jnp.concatenate([low0, low1], 1)], 0
            )
            over_y = jnp.exp2(dot(across, up_ref[...]))
            over_x = jnp.exp2(dot(left_ref[...], along))
            for k in range(2):
                a1_ref[z, l + k] = tin1 * over_y[k * N : (k + 1) * N]
                a2_ref[z, l + k] = tin2 * over_x[:, k * N : (k + 1) * N]
        return carry

    def times(rows, wide, factors, k):
        parts = [
            rows[wide * z : wide * (z + 1)] * factors[16 * z + k : 16 * z + k + 1] for z in range(PER)
        ]
        return jnp.concatenate(parts, 0)

    def counts(step, g):
        ex = jnp.exp2(exact(wax_ref[...], beam.rows(bdone, step, 0, g)))
        ey = jnp.exp2(exact(way_ref[...], det.rows(ddone, step, 0, g)))
        ex_ref[g], ey_ref[g] = ex, ey
        cols = jnp.concatenate([ey, jnp.zeros((N - 16 * PER, N), F32)], 0).T
        acc = jnp.zeros((N, N), F32)
        for z in members(g):
            k = 16 * (z % PER) + LINES + 1
            enter = step_x * ex[k : k + 1]
            for l in range(LINES):
                q = f_ref[z, LINES + 2 + l]
                k = 16 * (z % PER) + l
                a1 = a1_ref[z, l] * cols[:, k : k + 1]
                a1_ref[z, l] = a1
                beam.put(step, 1, g, beam.spot(z, l, LINES), enter * jnp.sum(q * a1, 0, keepdims=True))
                seen = jnp.sum(q * (a2_ref[z, l] * ex[k : k + 1]), 1, keepdims=True)
                acc = jnp.where(lane == det.spot(z, l, LINES), seen, acc)
        det.put_all(step, 1, g, step_y * times(acc.T, det.wide, ey, LINES))

    def residuals(step, g):
        ex, ey = ex_ref[g], ey_ref[g]
        res1 = lx_ref[g] * (beam.rows(bdone, step, 1, g) - mx_ref[g])
        res2 = ly_ref[g] * (det.rows(ddone, step, 1, g) - my_ref[g])
        sum1 = res1 * beam.rows(bsend, step, 1, g) / step_x
        sum2 = res2 * det.rows(dsend, step, 1, g) / step_y
        r1 = times(res1, beam.wide, ex, LINES + 1)
        r1_ref[g] = r1
        cols = jnp.concatenate([times(res2, det.wide, ey, LINES), jnp.zeros((N - det.wide * PER, N), F32)], 0).T
        s2c_ref[g] = cols
        acc = jnp.zeros((N, N), F32)
        for z in members(g):
            for l in range(LINES):
                q = f_ref[z, LINES + 2 + l]
                k, x, y = 16 * (z % PER) + l, beam.spot(z, l, LINES), det.spot(z, l, LINES)
                seen = jnp.sum(q * (a1_ref[z, l] * r1[x : x + 1]), 1, keepdims=True)
                acc = jnp.where(lane == k, seen, acc)
                seen = jnp.sum(q * (a2_ref[z, l] * cols[:, y : y + 1]), 0, keepdims=True)
                tx_ref[g, k : k + 1, :] = ex[k : k + 1] * seen
        ty_ref[g] = acc.T[0 : 16 * PER]
        for z in range(PER):
            k = 16 * z + LINES
            tx_ref[g, k : k + 1, :] = jnp.sum(sum1[beam.wide * z : beam.wide * (z + 1)], 0, keepdims=True)
            ty_ref[g, k : k + 1, :] = jnp.sum(sum2[det.wide * z : det.wide * (z + 1)], 0, keepdims=True)
        beam.put_all(step, 2, g, exact(wcx_ref[...], tx_ref[g]))
        det.put_all(step, 2, g, exact(wcy_ref[...], ty_ref[g]))

    def weights(z):
        g = z // PER
        ex, r1, cols = ex_ref[g], r1_ref[g], s2c_ref[g]
        sum1 = jnp.zeros((N, N), F32)
        sum2 = jnp.zeros((N, N), F32)
        for l in range(LINES):
            q = f_ref[z, LINES + 2 + l]
            k, x, y = 16 * (z % PER) + l, beam.spot(z, l, LINES), det.spot(z, l, LINES)
            w1 = a1_ref[z, l] * r1[x : x + 1]
            w2 = a2_ref[z, l] * ex[k : k + 1] * cols[:, y : y + 1]
            a1_ref[z, l] = w1 + w2
            p1, p2 = q * w1, q * w2
            sum1, sum2 = sum1 + p1, sum2 + p2
            f_ref[z, l] = cum_cols(p1, down_ref[...]) + cum_rows(p2, right_ref[...])
        f_ref[z, LINES] = cum_rows(sum1, right_ref[...])
        f_ref[z, LINES + 1] = cum_cols(sum2, down_ref[...])

    def update(step, g):
        cols = det.rows(ddone, step, 2, g)
        cols = jnp.concatenate([cols, jnp.zeros((N - cols.shape[0], N), F32)], 0).T
        rows = beam.rows(bdone, step, 2, g)
        acc = jnp.zeros((N, N), F32)
        for z in members(g):
            for e in range(ELEMENTS):
                x, y = beam.spot(z, e, ELEMENTS), det.spot(z, e, ELEMENTS)
                c = c_ref[e, z] + rows[x : x + 1] + cols[:, y : y + 1]
                c_ref[e, z] = c
                acc = total(step + 1, acc, z, e, c)
        det.put_all(step + 1, 0, g, acc.T[0 : det.wide * PER])

    def leave(g):
        stores = [pltpu.make_async_copy(c_ref.at[:, z], out_hbm.at[:, z], conc_sems.at[z]) for z in members(g)]
        return stores

    def turn(step, carry):
        last = step == STEPS - 1
        more = jnp.logical_not(last)
        blocks(0, mix)
        pass_on(step, 0, 1, "earlier")
        lax.fori_loop(0, PER, attenuate, 0)
        take(step, 0, 0)
        counts(step, 0)
        send_off(step, 1, 0)
        blocks(1, mix)
        pass_on(step, 1, 0, "sum")
        lax.fori_loop(PER, ZS, attenuate, 0)
        take(step, 0, 1)
        counts(step, 1)
        send_off(step, 1, 1)
        take(step, 1, 0)
        residuals(step, 0)
        send_off(step, 2, 0)
        weights(0)
        pass_on(step, 1, 1, "sum")
        weights(1)
        pass_on(step, 2, 0, "later")
        take(step, 1, 1)
        residuals(step, 1)
        send_off(step, 2, 1)
        blocks(0, unmix)

        @pl.when(last)
        def part():
            for store in leave(0):
                store.start()

        take(step, 2, 0)

        @pl.when(more)
        def again():
            update(step, 0)
            send_off(step + 1, 0, 0)

        weights(2)
        pass_on(step, 2, 1, "later")
        weights(3)

        @pl.when(more)
        def early():
            pass_on(step + 1, 0, 0, "earlier")

        blocks(1, unmix)
        take(step, 2, 1)

        @pl.when(more)
        def once_more():
            update(step, 1)
            send_off(step + 1, 0, 1)

        @pl.when(last)
        def finish():
            for store in leave(1):
                store.start()
            for store in leave(0) + leave(1):
                store.wait()

        for phase in range(3):
            det.settle(step, phase)
            beam.settle(step, phase)
        return carry

    lax.fori_loop(0, STEPS, turn, 0)
    dx_ref[...] = bdone[STEPS - 1, 2]
    dy_ref[...] = ddone[STEPS - 1, 2]


def close(x_spots, y_spots, c_ref, dx_ref, dy_ref, out_ref):
    rows = dx_ref[...].reshape(-1, N)
    cols = dy_ref[...].reshape(-1, N)
    cols = jnp.concatenate([cols, jnp.zeros((N - cols.shape[0], N), F32)], 0).T
    for e in range(ELEMENTS):
        x, y = x_spots[e], y_spots[e]
        out_ref[e, 0] = c_ref[e, 0] + rows[x : x + 1] + cols[:, y : y + 1]


def solution(mesh):
    beams, dets = mesh.shape["beam"], mesh.shape["det"]

    def shards(conc, inc, sig, yld, rate, axis, m1, live1, m2, live2):
        step_x = 1.0 / (conc.shape[2] * beams)
        step_y = 1.0 / (conc.shape[3] * dets)

        def body(*refs):
            kernel(step_x, step_y, *refs)

        def exchange(count):
            tiles = pltpu.VMEM((STEPS, 3, count, 8, N), F32)
            return [tiles] * 4 + [pltpu.SemaphoreType.DMA((STEPS, 3, 3 + GROUPS))]

        def per_group(rows):
            return pltpu.VMEM((GROUPS, rows, N), F32)

        def spots(tiles):
            per = -(-ELEMENTS // tiles)
            return [8 * (e // per) + e % per for e in range(ELEMENTS)]

        field = (N, N)
        anywhere = pl.BlockSpec(memory_space=pl.ANY)
        vmem = pl.BlockSpec(memory_space=pltpu.VMEM)
        small = (axis[None], inc, sig, yld, rate[None], m1, live1, m2, live2)
        inner, dx, dy = pl.pallas_call(
            body,
            out_shape=[
                jax.ShapeDtypeStruct(conc.shape, F32),
                jax.ShapeDtypeStruct((beams, 8, N), F32),
                jax.ShapeDtypeStruct((dets, 8, N), F32),
            ],
            in_specs=[anywhere] * (len(small) + 1),
            out_specs=[anywhere, vmem, vmem],
            scratch_shapes=[
                *[pltpu.VMEM(a.shape, a.dtype) for a in small + (conc,)],
                pltpu.SemaphoreType.DMA((len(small),)),
                pltpu.SemaphoreType.DMA((ZS,)),
                pltpu.VMEM((ZS, FIELDS) + field, F32),
                pltpu.VMEM((ZS, LINES) + field, F32),
                pltpu.VMEM((ZS, LINES) + field, F32),
                *[per_group(16 * PER)] * 2,
                per_group(8 * beams // GROUPS),
                per_group(N),
                per_group(8 * beams // GROUPS),
                per_group(8 * dets // GROUPS),
                per_group(8 * beams // GROUPS),
                per_group(8 * dets // GROUPS),
                *[per_group(16 * PER)] * 2,
                *[pltpu.VMEM((32, N), F32)] * 2,
                pltpu.VMEM((8 * FIELDS, 2 * N), BF16),
                pltpu.VMEM((16 * ELEMENTS, 8 * FIELDS), BF16),
                *[pltpu.VMEM((2 * N, N), BF16)] * 2,
                *[pltpu.VMEM((N, 2 * N), BF16)] * 2,
                pltpu.VMEM((16 * PER, 8 * beams // GROUPS), F32),
                pltpu.VMEM((16 * PER, 8 * dets // GROUPS), F32),
                pltpu.VMEM((8 * beams // GROUPS, 16 * PER), F32),
                pltpu.VMEM((8 * dets // GROUPS, 16 * PER), F32),
                *exchange(beams),
                *exchange(dets),
            ],
            compiler_params=pltpu.CompilerParams(
                collective_id=0, has_side_effects=True, vmem_limit_bytes=64 * 1024 * 1024
            ),
        )(*small, conc)

        x_tiles, y_tiles = beams // ZS, dets // ZS

        def last(*refs):
            close(spots(x_tiles), spots(y_tiles), *refs)

        block = pl.BlockSpec((ELEMENTS, 1, N, N), lambda z: (0, z, 0, 0))
        return pl.pallas_call(
            last,
            out_shape=jax.ShapeDtypeStruct(conc.shape, F32),
            grid=(ZS,),
            in_specs=[
                block,
                pl.BlockSpec((x_tiles, 8, N), lambda z: (z, 0, 0)),
                pl.BlockSpec((y_tiles, 8, N), lambda z: (z, 0, 0)),
            ],
            out_specs=block,
            compiler_params=pltpu.CompilerParams(vmem_limit_bytes=64 * 1024 * 1024),
        )(inner, dx, dy)

    in_specs = (
        P(None, None, "beam", "det"),
        P(),
        P(),
        P(),
        P(),
        P(),
        P(None, None, "det"),
        P(None, "det"),
        P(None, None, "beam"),
        P(None, "beam"),
    )
    out_specs = P(None, None, "beam", "det")
    return jax.shard_map(shards, mesh=mesh, in_specs=in_specs, out_specs=out_specs, check_vma=False)
```

```python
import math

import jax
import jax.numpy as jnp
from jax import lax
from jax.experimental import pallas as pl
from jax.experimental.pallas import tpu as pltpu
from jax.sharding import PartitionSpec as P

STEPS = 2
HIGH = lax.Precision.HIGHEST
MESH = pl.DeviceIdType.MESH
F32 = jnp.float32
BF16 = jnp.bfloat16
ELEMENTS = 10
LINES = 12
ZS = 4
N = 128
FIELDS = 26
CHUNK = 32
LOG2E = math.log2(math.e)


def split(value):
    high = value.astype(BF16)
    return high, (value - high.astype(F32)).astype(BF16)


def iota(shape, dim):
    return lax.broadcasted_iota(jnp.int32, shape, dim)


def dot(a, b):
    return jnp.dot(a, b, preferred_element_type=F32)


def exact(a, b):
    return jnp.dot(a, b, preferred_element_type=F32, precision=HIGH)


def exact_nt(a, b):
    return lax.dot_general(
        a, b, (((1,), (1,)), ((), ())), preferred_element_type=F32, precision=HIGH
    )


def one_hot(condition):
    return jnp.where(condition, 1.0, 0.0).astype(F32)


class Ring:
    def __init__(self, axis, send, recv, back, done, sems):
        self.axis = axis
        self.count = recv.shape[2]
        self.me = lax.axis_index(axis)
        self.send, self.recv, self.back, self.done, self.sems = send, recv, back, done, sems
        self.tiles = self.count // ZS
        self.wide = 8 * self.tiles
        half = self.count // 2
        self.hops = sorted(range(1, self.count), key=lambda d: (abs(d - half), d))

    def peer(self, d):
        return lax.rem(self.me + d, self.count)

    def greet(self, barrier):
        for d in self.hops:
            pl.semaphore_signal(barrier, inc=1, device_id={self.axis: self.peer(d)}, device_id_type=MESH)

    def copy(self, src, dst, step, phase, leg, peer):
        return pltpu.make_async_remote_copy(
            src_ref=src,
            dst_ref=dst,
            send_sem=self.sems.at[step, phase, leg, 0],
            recv_sem=self.sems.at[step, phase, leg, 1],
            device_id={self.axis: peer},
            device_id_type=MESH,
        )

    def start(self, step, phase):
        mine = (step, phase, pl.ds(self.me, 1))
        self.recv[mine] = self.send[mine]
        for d in self.hops:
            peer = self.peer(d)
            src, dst = self.send.at[step, phase, peer], self.recv.at[step, phase, self.me]
            self.copy(src, dst, step, phase, 0, peer).start()

    def wait(self, src, dst, step, phase, leg):
        several = (step, phase, pl.ds(0, self.count - 1))
        whole = self.copy(src.at[several], dst.at[several], step, phase, leg, self.peer(1))
        whole.wait_send()
        whole.wait_recv()

    def middle(self, step, phase, mode):
        self.wait(self.send, self.recv, step, phase, 0)
        total = jnp.zeros((8, N), F32)
        order = range(self.count)
        for t in reversed(order) if mode == "later" else order:
            if mode != "sum":
                self.back[step, phase, t] = total
            total = total + self.recv[step, phase, t]
        mine = (step, phase, pl.ds(self.me, 1))
        if mode == "sum":
            self.back[step, phase, 0] = total
            self.done[mine] = total[None]
        else:
            self.done[mine] = self.back[mine]
        for d in self.hops:
            peer = self.peer(d)
            src = self.back.at[step, phase, 0 if mode == "sum" else peer]
            self.copy(src, self.done.at[step, phase, self.me], step, phase, 1, peer).start()

    def finish(self, step, phase):
        self.wait(self.back, self.done, step, phase, 1)

    def spot(self, row, of):
        per = -(-of // self.tiles)
        return 8 * (row // per) + row % per

    def rows(self, ref, step, phase):
        return ref[step, phase].reshape(8 * self.count, N)

    def put(self, step, phase, z, spot, value):
        self.send[step, phase, z * self.tiles + spot // 8, spot % 8 : spot % 8 + 1, :] = value

    def put_z(self, step, phase, z, rows):
        self.send[step, phase, z * self.tiles : (z + 1) * self.tiles] = rows.reshape(self.tiles, 8, N)

    def put_all(self, step, phase, rows):
        self.send[step, phase] = rows.reshape(self.count, 8, N)


def kernel(
    step_x, step_y,
    axis_hbm, inc_hbm, sig_hbm, yld_hbm, rate_hbm, m1_hbm, live1_hbm, m2_hbm, live2_hbm, conc_hbm,
    out_hbm, dx_ref, dy_ref,
    axis_ref, inc_ref, sig_ref, yld_ref, rate_ref, m1_ref, live1_ref, m2_ref, live2_ref, c_ref,
    load_sems, conc_sems,
    m_ref, q_ref, a1_ref, a2_ref, p1_ref, p2_ref, v_ref, rows_ref, cols_ref, acc_ref,
    mx_ref, my_ref, lx_ref, ly_ref,
    tx_ref, ty_ref, tab_ref, back_ref, mix_ref, unmix_ref, up_ref, down_ref, left_ref, right_ref,
    wax_ref, way_ref, wcx_ref, wcy_ref,
    bsend, brecv, bback, bdone, bsems, dsend, drecv, dback, ddone, dsems,
):
    def conc_load(z):
        return pltpu.make_async_copy(conc_hbm.at[:, z], c_ref.at[:, z], conc_sems.at[z])

    hbm = (axis_hbm, inc_hbm, sig_hbm, yld_hbm, rate_hbm, m1_hbm, live1_hbm, m2_hbm, live2_hbm)
    vmem = (axis_ref, inc_ref, sig_ref, yld_ref, rate_ref, m1_ref, live1_ref, m2_ref, live2_ref)
    loads = [pltpu.make_async_copy(a, b, load_sems.at[k]) for k, (a, b) in enumerate(zip(hbm, vmem))]
    for load in [conc_load(z) for z in range(ZS)] + loads:
        load.start()
    beam = Ring("beam", bsend, brecv, bback, bdone, bsems)
    det = Ring("det", dsend, drecv, dback, ddone, dsems)
    barrier = pltpu.get_barrier_semaphore()
    det.greet(barrier)
    beam.greet(barrier)

    for ref in (bsend, dsend, cols_ref, mx_ref, my_ref, lx_ref, ly_ref, tx_ref, ty_ref, tab_ref, back_ref):
        ref[...] = jnp.zeros(ref.shape, F32)

    lane = iota((CHUNK, N), 1)

    def over_z(body):
        def one(z, carry):
            body(z)
            return carry

        lax.fori_loop(0, ZS, one, 0)

    def chunks(count, body):
        def one(r, sums):
            new = body(pl.ds(pl.multiple_of(r * CHUNK, CHUNK), CHUNK))
            return tuple(a + jnp.sum(b.reshape(CHUNK // 8, 8, N), 0) for a, b in zip(sums, new))

        sums = lax.fori_loop(0, N // CHUNK, one, (jnp.zeros((8, N), F32),) * count)
        return [jnp.sum(a, 0, keepdims=True) for a in sums]

    def turned(rows):
        return jnp.concatenate([rows, jnp.zeros((N - rows.shape[0], N), F32)], 0).T

    def totals(step, add):
        def one(z):
            if not add:
                conc_load(z).wait()

            def chunk(rows):
                sums = []
                acc = jnp.zeros((CHUNK, N), F32)
                cols = cols_ref[z, rows]
                for e in range(ELEMENTS):
                    x, y = beam.spot(e, ELEMENTS), det.spot(e, ELEMENTS)
                    c = c_ref[e, z, rows]
                    if add:
                        c = c + rows_ref[z, x : x + 1] + cols[:, y : y + 1]
                        c_ref[e, z, rows] = c
                    sums.append(c)
                    acc = jnp.where(lane == y, jnp.sum(c, 1, keepdims=True), acc)
                acc_ref[z, rows] = acc
                return sums

            for e, row in enumerate(chunks(ELEMENTS, chunk)):
                beam.put(step, 0, z, beam.spot(e, ELEMENTS), row)

        over_z(one)
        for z in range(ZS):
            det.put_z(step, 0, z, acc_ref[z].T[0 : det.wide])

    totals(0, False)
    pl.semaphore_wait(barrier, beam.count + det.count - 2)
    det.start(0, 0)
    beam.start(0, 0)
    for load in loads:
        load.wait()

    def tables():
        first = axis_ref[0:1, 0:1] == 0
        one, two = inc_ref[0:1, :], inc_ref[1:2, :]
        s1 = jnp.where(first, one, two)
        s2 = jnp.where(first, two, one)
        scale = -LOG2E * step_y
        sig, yld, rate = sig_ref[...], yld_ref[...], rate_ref[...]
        cols = pl.ds(0, ELEMENTS)
        tab_ref[0:LINES, cols] = scale * sig
        tab_ref[LINES : LINES + 1, cols] = scale * s2
        tab_ref[LINES + 1 : LINES + 2, cols] = scale * s1
        tab_ref[LINES + 2 : FIELDS, cols] = yld
        back_ref[0:LINES, cols] = yld * rate
        back_ref[LINES : 2 * LINES, cols] = -sig * rate
        back_ref[2 * LINES : 2 * LINES + 1, cols] = -s1 * rate
        back_ref[2 * LINES + 1 : FIELDS, cols] = -s2 * rate

        tab, back = tab_ref[...], back_ref[...]
        wide = 8 * ELEMENTS
        pick = one_hot((iota((8 * FIELDS, 32), 0) >> 3) == iota((8 * FIELDS, 32), 1))
        col = iota((N, 256), 1)
        part = (col >= wide).astype(jnp.int32) + (col >= 2 * wide).astype(jnp.int32)
        spread = one_hot(((col - wide * part) >> 3) == iota((N, 256), 0))
        spread = jnp.where(col < 3 * wide, spread, 0.0)
        full = exact(pick, exact(tab, spread))
        shape = (8 * FIELDS, 256)
        full = jnp.where((iota(shape, 0) & 7) == (iota(shape, 1) & 7), full, 0.0)
        high, low = split(full)
        part = iota(shape, 1)
        mix_ref[...] = jnp.where((part >= wide) & (part < 2 * wide), low.astype(F32), high.astype(F32)).astype(BF16)

        pick = one_hot((iota((wide, N), 0) >> 3) == iota((wide, N), 1))
        shape = (wide, 8 * FIELDS)
        spread = one_hot((iota((32, 8 * FIELDS), 1) >> 3) == iota((32, 8 * FIELDS), 0))
        full = exact(exact_nt(pick, back), spread)
        full = jnp.where((iota(shape, 0) & 7) == (iota(shape, 1) & 7), full, 0.0)
        high, low = split(full)
        unmix_ref[0:wide] = high
        unmix_ref[wide : 2 * wide] = low

        r, m = iota((16 * ZS, 32), 0) & 15, iota((16 * ZS, 32), 1)
        rates = exact(one_hot((r == m) & (r < LINES + 2)), tab)
        sums_x = exact(one_hot(m == jnp.where(r < LINES, r + LINES, 2 * LINES)), back)
        sums_y = exact(one_hot(m == jnp.where(r < LINES, r + LINES, 2 * LINES + 1)), back)
        r = iota((16 * ZS, N), 0) & 15
        sums_x = jnp.where(r <= LINES, -step_x * sums_x, 0.0)
        sums_y = jnp.where(r <= LINES, -step_y * sums_y, 0.0)

        def place(ring):
            shape = (8 * ring.count, N)
            per = -(-ELEMENTS // ring.tiles)
            row = iota(shape, 0) & (ring.wide - 1)
            inside = row & 7
            return one_hot((inside < per) & ((row >> 3) * per + inside == iota(shape, 1)))

        def same(shape, rows, cols):
            shift = lambda n: n.bit_length() - 1
            return (iota(shape, 0) >> shift(rows)) == (iota(shape, 1) >> shift(cols))

        place_x, place_y = place(beam), place(det)
        wax_ref[...] = jnp.where(
            same(wax_ref.shape, 16, beam.wide), exact_nt(rates * (step_x / step_y), place_x), 0.0
        )
        way_ref[...] = jnp.where(same(way_ref.shape, 16, det.wide), exact_nt(rates, place_y), 0.0)
        wcx_ref[...] = jnp.where(same(wcx_ref.shape, beam.wide, 16), exact_nt(place_x, sums_x), 0.0)
        wcy_ref[...] = jnp.where(same(wcy_ref.shape, det.wide, 16), exact_nt(place_y, sums_y), 0.0)

        r, c = iota((2 * N, N), 0) & (N - 1), iota((2 * N, N), 1)
        up_ref[...] = one_hot(r < c).astype(BF16)
        down_ref[...] = (step_y * one_hot(r > c)).astype(BF16)
        r, c = iota((N, 2 * N), 0), iota((N, 2 * N), 1) & (N - 1)
        left_ref[...] = (step_x / step_y * one_hot(c < r)).astype(BF16)
        right_ref[...] = (step_x * one_hot(c > r)).astype(BF16)
        for z in range(ZS):
            live1 = live1_ref[z : z + 1, :].astype(F32)
            live2 = live2_ref[z : z + 1, :].astype(F32)
            for l in range(LINES):
                x, y = beam.wide * z + beam.spot(l, LINES), det.wide * z + det.spot(l, LINES)
                lx_ref[x : x + 1, :] = live1
                ly_ref[y : y + 1, :] = live2
                mx_ref[x : x + 1, :] = m1_ref[l, z : z + 1, :]
                my_ref[y : y + 1, :] = m2_ref[l, z : z + 1, :]

    tables()

    def groups(body):
        def one(n, carry):
            r0 = (n % 4) * 32
            for b in range(2):
                body(n // 4, pl.multiple_of(r0 + 16 * b, 16))
            return carry

        lax.fori_loop(0, 4 * ZS, one, 0)

    def mix(z, r0):
        parts = []
        for b in range(2):
            high, low = split(c_ref[:, z, pl.ds(r0 + 8 * b, 8), :].reshape(8 * ELEMENTS, N))
            parts.append(jnp.concatenate([high, high, low, jnp.zeros((16, N), BF16)], 0))
        out = dot(mix_ref[...], jnp.concatenate(parts, 1))
        rows = pl.ds(r0, 16)
        for f in range(FIELDS):
            field = jnp.concatenate([out[8 * f : 8 * f + 8, b * N : (b + 1) * N] for b in range(2)], 0)
            if f < LINES + 2:
                high, low = split(field)
                m_ref[z, f, rows, 0:N] = high
                m_ref[z, f, rows, N : 2 * N] = low
            else:
                q_ref[z, f - LINES - 2, rows, :] = field

    def unmix(z, r0):
        highs, lows = [], []
        for b in range(2):
            rows = pl.ds(r0 + 8 * b, 8)
            w = a1_ref[z, 0:LINES, rows, :].reshape(8 * LINES, N)
            v = v_ref[z, :, rows, :].reshape(8 * (LINES + 2), N)
            high, low = split(jnp.concatenate([w, v], 0))
            highs.append(high)
            lows.append(low)
        wide = 8 * ELEMENTS
        one = dot(unmix_ref[...], jnp.concatenate(highs, 1))
        two = dot(unmix_ref[0:wide], jnp.concatenate(lows, 1))
        out = one[0:wide] + (one[wide:] + two)
        for b in range(2):
            rows = pl.ds(r0 + 8 * b, 8)
            c_ref[:, z, rows, :] = c_ref[:, z, rows, :] - out[:, b * N : (b + 1) * N].reshape(ELEMENTS, 8, N)

    def stacked(ref, z, fields):
        value = [ref[z, f] for f in fields]
        high = jnp.concatenate([v[:, 0:N] for v in value], 1)
        low = jnp.concatenate([v[:, N : 2 * N] for v in value], 1)
        return jnp.concatenate([high, low], 0)

    def prefixes(z):
        for l in range(0, LINES, 2):
            out = dot(m_ref[z, l : l + 2].reshape(2 * N, 2 * N), up_ref[...])
            a1_ref[z, l : l + 2] = out.reshape(2, N, N)
            out = dot(left_ref[...], stacked(m_ref, z, (l, l + 1)))
            a2_ref[z, l] = out[:, 0:N]
            a2_ref[z, l + 1] = out[:, N : 2 * N]
        a1_ref[z, LINES] = dot(m_ref[z, LINES], up_ref[...])
        a2_ref[z, LINES] = dot(left_ref[...], stacked(m_ref, z, (LINES + 1,)))

    def suffixes(z):
        for l in range(0, LINES, 2):
            over_y = dot(p1_ref[z, l : l + 2].reshape(2 * N, 2 * N), down_ref[...])
            over_x = dot(right_ref[...], stacked(p2_ref, z, (l, l + 1)))
            v_ref[z, l] = over_y[0:N] + over_x[:, 0:N]
            v_ref[z, l + 1] = over_y[N : 2 * N] + over_x[:, N : 2 * N]
        v_ref[z, LINES] = dot(right_ref[...], stacked(p2_ref, z, (LINES,)))
        v_ref[z, LINES + 1] = dot(p1_ref[z, LINES], down_ref[...])

    def counts(step):
        enter_x = exact(wax_ref[...], beam.rows(bdone, step, 0))
        enter_y = exact(way_ref[...], det.rows(ddone, step, 0))
        rows_ref[:, 0:16] = enter_x.reshape(ZS, 16, N)
        for z in range(ZS):
            cols_ref[z] = turned(enter_y[16 * z : 16 * (z + 1)])

        def one(z):
            def chunk(rows):
                cols = cols_ref[z, rows]
                tin1 = jnp.exp2(a2_ref[z, LINES, rows] + rows_ref[z, LINES + 1 : LINES + 2])
                tin2 = jnp.exp2(a1_ref[z, LINES, rows] + cols[:, LINES : LINES + 1])
                sums = []
                acc = jnp.zeros((CHUNK, N), F32)
                for l in range(LINES):
                    a1 = tin1 * jnp.exp2(a1_ref[z, l, rows] + cols[:, l : l + 1])
                    a2 = tin2 * jnp.exp2(a2_ref[z, l, rows] + rows_ref[z, l : l + 1])
                    a1_ref[z, l, rows] = a1
                    a2_ref[z, l, rows] = a2
                    q = q_ref[z, l, rows]
                    sums.append(q * a1)
                    acc = jnp.where(lane == det.spot(l, LINES), jnp.sum(q * a2, 1, keepdims=True), acc)
                acc_ref[z, rows] = acc
                return sums

            for l, row in enumerate(chunks(LINES, chunk)):
                beam.put(step, 1, z, beam.spot(l, LINES), step_x * row)

        over_z(one)
        for z in range(ZS):
            det.put_z(step, 1, z, step_y * acc_ref[z].T[0 : det.wide])

    def residuals(step):
        res1 = lx_ref[...] * (beam.rows(bdone, step, 1) - mx_ref[...])
        res2 = ly_ref[...] * (det.rows(ddone, step, 1) - my_ref[...])
        sum1 = res1 * beam.rows(bsend, step, 1) / step_x
        sum2 = res2 * det.rows(dsend, step, 1) / step_y
        rows_ref[:, 0 : beam.wide] = res1.reshape(ZS, beam.wide, N)
        for z in range(ZS):
            cols_ref[z] = turned(res2[det.wide * z : det.wide * (z + 1)])

        def one(z):
            def chunk(rows):
                cols = cols_ref[z, rows]
                sums = []
                acc = jnp.zeros((CHUNK, N), F32)
                all1 = jnp.zeros((CHUNK, N), F32)
                all2 = jnp.zeros((CHUNK, N), F32)

                def keep(ref, f, value):
                    high, low = split(value)
                    ref[z, f, rows, 0:N] = high
                    ref[z, f, rows, N : 2 * N] = low

                for l in range(LINES):
                    x, y = beam.spot(l, LINES), det.spot(l, LINES)
                    w1 = a1_ref[z, l, rows] * rows_ref[z, x : x + 1]
                    w2 = a2_ref[z, l, rows] * cols[:, y : y + 1]
                    a1_ref[z, l, rows] = w1 + w2
                    q = q_ref[z, l, rows]
                    p1, p2 = q * w1, q * w2
                    all1, all2 = all1 + p1, all2 + p2
                    sums.append(p2)
                    acc = jnp.where(lane == l, jnp.sum(p1, 1, keepdims=True), acc)
                    keep(p1_ref, l, p1)
                    keep(p2_ref, l, p2)
                keep(p1_ref, LINES, all2)
                keep(p2_ref, LINES, all1)
                acc_ref[z, rows] = acc
                return sums

            for l, row in enumerate(chunks(LINES, chunk)):
                tx_ref[z, l : l + 1] = row

        over_z(one)
        for z in range(ZS):
            ty_ref[z] = acc_ref[z].T[0:16]
            k = slice(LINES, LINES + 1)
            tx_ref[z, k] = jnp.sum(sum1[beam.wide * z : beam.wide * (z + 1)], 0, keepdims=True)
            ty_ref[z, k] = jnp.sum(sum2[det.wide * z : det.wide * (z + 1)], 0, keepdims=True)
        beam.put_all(step, 2, exact(wcx_ref[...], tx_ref[...].reshape(16 * ZS, N)))
        det.put_all(step, 2, exact(wcy_ref[...], ty_ref[...].reshape(16 * ZS, N)))

    def update(step):
        rows_ref[:, 0 : beam.wide] = beam.rows(bdone, step, 2).reshape(ZS, beam.wide, N)
        enter = det.rows(ddone, step, 2)
        for z in range(ZS):
            cols_ref[z] = turned(enter[det.wide * z : det.wide * (z + 1)])
        totals(step + 1, True)

    def turn(step, carry):
        last = step == STEPS - 1
        groups(mix)
        det.middle(step, 0, "earlier")
        beam.middle(step, 0, "earlier")
        over_z(prefixes)
        det.finish(step, 0)
        beam.finish(step, 0)
        counts(step)
        det.start(step, 1)
        beam.start(step, 1)
        det.middle(step, 1, "sum")
        beam.middle(step, 1, "sum")
        det.finish(step, 1)
        beam.finish(step, 1)
        residuals(step)
        det.start(step, 2)
        beam.start(step, 2)
        over_z(suffixes)
        det.middle(step, 2, "later")
        beam.middle(step, 2, "later")
        groups(unmix)

        def stores():
            return [pltpu.make_async_copy(c_ref.at[:, z], out_hbm.at[:, z], conc_sems.at[z]) for z in range(ZS)]

        @pl.when(last)
        def leave():
            for store in stores():
                store.start()

        det.finish(step, 2)
        beam.finish(step, 2)

        @pl.when(last)
        def left():
            for store in stores():
                store.wait()

        @pl.when(jnp.logical_not(last))
        def go_on():
            update(step)
            det.start(step + 1, 0)
            beam.start(step + 1, 0)

        return carry

    lax.fori_loop(0, STEPS, turn, 0)
    dx_ref[...] = bdone[STEPS - 1, 2]
    dy_ref[...] = ddone[STEPS - 1, 2]


def close(x_spots, y_spots, c_ref, dx_ref, dy_ref, out_ref):
    rows = dx_ref[...].reshape(-1, N)
    cols = dy_ref[...].reshape(-1, N)
    cols = jnp.concatenate([cols, jnp.zeros((N - cols.shape[0], N), F32)], 0).T
    for e in range(ELEMENTS):
        x, y = x_spots[e], y_spots[e]
        out_ref[e, 0] = c_ref[e, 0] + rows[x : x + 1] + cols[:, y : y + 1]


def solution(mesh):
    beams, dets = mesh.shape["beam"], mesh.shape["det"]

    def shards(conc, inc, sig, yld, rate, axis, m1, live1, m2, live2):
        step_x = 1.0 / (conc.shape[2] * beams)
        step_y = 1.0 / (conc.shape[3] * dets)

        def body(*refs):
            kernel(step_x, step_y, *refs)

        def exchange(count):
            tiles = pltpu.VMEM((STEPS, 3, count, 8, N), F32)
            return [tiles] * 4 + [pltpu.SemaphoreType.DMA((STEPS, 3, 2, 2))]

        def spots(tiles):
            per = -(-ELEMENTS // tiles)
            return [8 * (e // per) + e % per for e in range(ELEMENTS)]

        field = (N, N)
        anywhere = pl.BlockSpec(memory_space=pl.ANY)
        vmem = pl.BlockSpec(memory_space=pltpu.VMEM)
        small = (axis[None], inc, sig, yld, rate[None], m1, live1, m2, live2)
        inner, dx, dy = pl.pallas_call(
            body,
            out_shape=[
                jax.ShapeDtypeStruct(conc.shape, F32),
                jax.ShapeDtypeStruct((beams, 8, N), F32),
                jax.ShapeDtypeStruct((dets, 8, N), F32),
            ],
            in_specs=[anywhere] * (len(small) + 1),
            out_specs=[anywhere, vmem, vmem],
            scratch_shapes=[
                *[pltpu.VMEM(a.shape, a.dtype) for a in small + (conc,)],
                pltpu.SemaphoreType.DMA((len(small),)),
                pltpu.SemaphoreType.DMA((ZS,)),
                pltpu.VMEM((ZS, LINES + 2, N, 2 * N), BF16),
                pltpu.VMEM((ZS, LINES) + field, F32),
                *[pltpu.VMEM((ZS, LINES + 1) + field, F32)] * 2,
                *[pltpu.VMEM((ZS, LINES + 1, N, 2 * N), BF16)] * 2,
                pltpu.VMEM((ZS, LINES + 2) + field, F32),
                pltpu.VMEM((ZS, 16, N), F32),
                *[pltpu.VMEM((ZS,) + field, F32)] * 2,
                pltpu.VMEM((8 * beams, N), F32),
                pltpu.VMEM((8 * dets, N), F32),
                pltpu.VMEM((8 * beams, N), F32),
                pltpu.VMEM((8 * dets, N), F32),
                *[pltpu.VMEM((ZS, 16, N), F32)] * 2,
                *[pltpu.VMEM((32, N), F32)] * 2,
                pltpu.VMEM((8 * FIELDS, 2 * N), BF16),
                pltpu.VMEM((16 * ELEMENTS, 8 * FIELDS), BF16),
                *[pltpu.VMEM((2 * N, N), BF16)] * 2,
                *[pltpu.VMEM((N, 2 * N), BF16)] * 2,
                pltpu.VMEM((16 * ZS, 8 * beams), F32),
                pltpu.VMEM((16 * ZS, 8 * dets), F32),
                pltpu.VMEM((8 * beams, 16 * ZS), F32),
                pltpu.VMEM((8 * dets, 16 * ZS), F32),
                *exchange(beams),
                *exchange(dets),
            ],
            compiler_params=pltpu.CompilerParams(
                collective_id=0, has_side_effects=True, vmem_limit_bytes=64 * 1024 * 1024
            ),
        )(*small, conc)

        x_tiles, y_tiles = beams // ZS, dets // ZS

        def last(*refs):
            close(spots(x_tiles), spots(y_tiles), *refs)

        block = pl.BlockSpec((ELEMENTS, 1, N, N), lambda z: (0, z, 0, 0))
        return pl.pallas_call(
            last,
            out_shape=jax.ShapeDtypeStruct(conc.shape, F32),
            grid=(ZS,),
            in_specs=[
                block,
                pl.BlockSpec((x_tiles, 8, N), lambda z: (z, 0, 0)),
                pl.BlockSpec((y_tiles, 8, N), lambda z: (z, 0, 0)),
            ],
            out_specs=block,
            compiler_params=pltpu.CompilerParams(vmem_limit_bytes=64 * 1024 * 1024),
        )(inner, dx, dy)

    in_specs = (
        P(None, None, "beam", "det"),
        P(),
        P(),
        P(),
        P(),
        P(),
        P(None, None, "det"),
        P(None, "det"),
        P(None, None, "beam"),
        P(None, "beam"),
    )
    out_specs = P(None, None, "beam", "det")
    return jax.shard_map(shards, mesh=mesh, in_specs=in_specs, out_specs=out_specs, check_vma=False)
```

```python
import math

import jax
import jax.numpy as jnp
from jax import lax
from jax.experimental import pallas as pl
from jax.experimental.pallas import tpu as pltpu
from jax.sharding import PartitionSpec as P

STEPS = 2
HIGH = lax.Precision.HIGHEST
MESH = pl.DeviceIdType.MESH
F32 = jnp.float32
BF16 = jnp.bfloat16
ELEMENTS = 10
LINES = 12
ZS = 4
N = 128
FIELDS = 26
CHUNK = 64
LOG2E = math.log2(math.e)


def split(value):
    high = value.astype(BF16)
    return high, (value - high.astype(F32)).astype(BF16)


def iota(shape, dim):
    return lax.broadcasted_iota(jnp.int32, shape, dim)


def dot(a, b):
    return jnp.dot(a, b, preferred_element_type=F32)


def exact(a, b):
    return jnp.dot(a, b, preferred_element_type=F32, precision=HIGH)


def exact_nt(a, b):
    return lax.dot_general(
        a, b, (((1,), (1,)), ((), ())), preferred_element_type=F32, precision=HIGH
    )


def one_hot(condition):
    return jnp.where(condition, 1.0, 0.0).astype(F32)


class Ring:
    def __init__(self, axis, send, recv, back, done, sems):
        self.axis = axis
        self.count = recv.shape[1]
        self.me = lax.axis_index(axis)
        self.send, self.recv, self.back, self.done, self.sems = send, recv, back, done, sems
        self.tiles = self.count // ZS
        self.wide = 8 * self.tiles
        half = self.count // 2
        self.hops = sorted(range(1, self.count), key=lambda d: (abs(d - half), d))

    def peer(self, d):
        return lax.rem(self.me + d, self.count)

    def greet(self, barrier):
        for d in self.hops:
            pl.semaphore_signal(barrier, inc=1, device_id={self.axis: self.peer(d)}, device_id_type=MESH)

    def copy(self, src, dst, phase, leg, peer):
        return pltpu.make_async_remote_copy(
            src_ref=src,
            dst_ref=dst,
            send_sem=self.sems.at[phase, leg, 0],
            recv_sem=self.sems.at[phase, leg, 1],
            device_id={self.axis: peer},
            device_id_type=MESH,
        )

    def start(self, phase):
        mine = (phase, pl.ds(self.me, 1))
        self.recv[mine] = self.send[mine]
        for d in self.hops:
            peer = self.peer(d)
            src, dst = self.send.at[phase, peer], self.recv.at[phase, self.me]
            self.copy(src, dst, phase, 0, peer).start()

    def wait(self, src, dst, phase, leg):
        several = (phase, pl.ds(0, self.count - 1))
        whole = self.copy(src.at[several], dst.at[several], phase, leg, self.peer(1))
        whole.wait_send()
        whole.wait_recv()

    def middle(self, phase, mode):
        self.wait(self.send, self.recv, phase, 0)
        total = jnp.zeros((8, N), F32)
        order = range(self.count)
        for t in reversed(order) if mode == "later" else order:
            if mode != "sum":
                self.back[phase, t] = total
            total = total + self.recv[phase, t]
        mine = (phase, pl.ds(self.me, 1))
        if mode == "sum":
            self.back[phase, 0] = total
            self.done[mine] = total[None]
        else:
            self.done[mine] = self.back[mine]
        for d in self.hops:
            peer = self.peer(d)
            src = self.back.at[phase, 0 if mode == "sum" else peer]
            self.copy(src, self.done.at[phase, self.me], phase, 1, peer).start()

    def finish(self, phase):
        self.wait(self.back, self.done, phase, 1)

    def spot(self, row, of):
        per = -(-of // self.tiles)
        return 8 * (row // per) + row % per

    def rows(self, ref, phase):
        return ref[phase].reshape(8 * self.count, N)

    def put(self, phase, z, spot, value):
        self.send[phase, z * self.tiles + spot // 8, spot % 8 : spot % 8 + 1, :] = value

    def put_z(self, phase, z, rows):
        self.send[phase, z * self.tiles : (z + 1) * self.tiles] = rows.reshape(self.tiles, 8, N)

    def put_all(self, phase, rows):
        self.send[phase] = rows.reshape(self.count, 8, N)


def kernel(
    step_x, step_y,
    axis_hbm, inc_hbm, sig_hbm, yld_hbm, rate_hbm, m1_hbm, live1_hbm, m2_hbm, live2_hbm, conc_hbm,
    out_hbm, dx_ref, dy_ref,
    axis_ref, inc_ref, sig_ref, yld_ref, rate_ref, m1_ref, live1_ref, m2_ref, live2_ref, c_ref,
    load_sems, conc_sems,
    m_ref, q_ref, e1_ref, e2_ref, a1_ref, a2_ref, w_ref, p1_ref, p2_ref, v_ref, d_ref, rows_ref, cols_ref, acc_ref,
    mx_ref, my_ref, lx_ref, ly_ref,
    tx_ref, ty_ref, tab_ref, back_ref, mix_ref, unmix_ref, up_ref, down_ref, left_ref, right_ref,
    wax_ref, way_ref, wcx_ref, wcy_ref,
    bsend, brecv, bback, bdone, bsems, dsend, drecv, dback, ddone, dsems,
):
    def conc_load(z):
        return pltpu.make_async_copy(conc_hbm.at[:, z], c_ref.at[:, z], conc_sems.at[z])

    hbm = (axis_hbm, inc_hbm, sig_hbm, yld_hbm, rate_hbm, m1_hbm, live1_hbm, m2_hbm, live2_hbm)
    vmem = (axis_ref, inc_ref, sig_ref, yld_ref, rate_ref, m1_ref, live1_ref, m2_ref, live2_ref)
    loads = [pltpu.make_async_copy(a, b, load_sems.at[k]) for k, (a, b) in enumerate(zip(hbm, vmem))]
    for load in [conc_load(z) for z in range(ZS)] + loads:
        load.start()
    beam = Ring("beam", bsend, brecv, bback, bdone, bsems)
    det = Ring("det", dsend, drecv, dback, ddone, dsems)
    barrier = pltpu.get_barrier_semaphore()
    det.greet(barrier)
    beam.greet(barrier)

    for ref in (bsend, dsend, cols_ref, mx_ref, my_ref, lx_ref, ly_ref, tx_ref, ty_ref, tab_ref, back_ref):
        ref[...] = jnp.zeros(ref.shape, F32)

    lane = iota((CHUNK, N), 1)

    def over_z(body):
        for z in range(ZS):
            body(z)

    def chunks(count, body):
        sums = [jnp.zeros((8, N), F32)] * count
        for r in range(0, N, CHUNK):
            new = body(pl.ds(r, CHUNK))
            sums = [a + jnp.sum(b.reshape(CHUNK // 8, 8, N), 0) for a, b in zip(sums, new)]
        return [jnp.sum(a, 0, keepdims=True) for a in sums]

    def turned(rows):
        return jnp.concatenate([rows, jnp.zeros((N - rows.shape[0], N), F32)], 0).T

    def totals(add):
        def one(z):
            if not add:
                conc_load(z).wait()

            def chunk(rows):
                sums = []
                acc = jnp.zeros((CHUNK, N), F32)
                cols = cols_ref[z, rows]
                for e in range(ELEMENTS):
                    x, y = beam.spot(e, ELEMENTS), det.spot(e, ELEMENTS)
                    c = d_ref[e, z, rows] if add else c_ref[e, z, rows]
                    if add:
                        c = c + rows_ref[z, x : x + 1] + cols[:, y : y + 1]
                        c_ref[e, z, rows] = c
                    sums.append(c)
                    acc = jnp.where(lane == y, jnp.sum(c, 1, keepdims=True), acc)
                acc_ref[z, rows] = acc
                return sums

            for e, row in enumerate(chunks(ELEMENTS, chunk)):
                beam.put(0, z, beam.spot(e, ELEMENTS), row)

        over_z(one)
        for z in range(ZS):
            det.put_z(0, z, acc_ref[z].T[0 : det.wide])

    totals(False)
    pl.semaphore_wait(barrier, beam.count + det.count - 2)
    det.start(0)
    beam.start(0)
    for load in loads:
        load.wait()

    def tables():
        first = axis_ref[0:1, 0:1] == 0
        one, two = inc_ref[0:1, :], inc_ref[1:2, :]
        s1 = jnp.where(first, one, two)
        s2 = jnp.where(first, two, one)
        scale = -LOG2E * step_y
        sig, yld, rate = sig_ref[...], yld_ref[...], rate_ref[...]
        cols = pl.ds(0, ELEMENTS)
        tab_ref[0:LINES, cols] = scale * sig
        tab_ref[LINES : LINES + 1, cols] = scale * s2
        tab_ref[LINES + 1 : LINES + 2, cols] = scale * s1
        tab_ref[LINES + 2 : FIELDS, cols] = yld
        back_ref[0:LINES, cols] = yld * rate
        back_ref[LINES : 2 * LINES, cols] = -sig * rate
        back_ref[2 * LINES : 2 * LINES + 1, cols] = -s1 * rate
        back_ref[2 * LINES + 1 : FIELDS, cols] = -s2 * rate

        tab, back = tab_ref[...], back_ref[...]
        wide = 8 * ELEMENTS
        pick = one_hot((iota((8 * FIELDS, 32), 0) >> 3) == iota((8 * FIELDS, 32), 1))
        col = iota((N, 256), 1)
        part = (col >= wide).astype(jnp.int32) + (col >= 2 * wide).astype(jnp.int32)
        spread = one_hot(((col - wide * part) >> 3) == iota((N, 256), 0))
        spread = jnp.where(col < 3 * wide, spread, 0.0)
        full = exact(pick, exact(tab, spread))
        shape = (8 * FIELDS, 256)
        full = jnp.where((iota(shape, 0) & 7) == (iota(shape, 1) & 7), full, 0.0)
        high, low = split(full)
        part = iota(shape, 1)
        mix_ref[...] = jnp.where((part >= wide) & (part < 2 * wide), low.astype(F32), high.astype(F32)).astype(BF16)

        pick = one_hot((iota((wide, N), 0) >> 3) == iota((wide, N), 1))
        shape = (wide, 8 * FIELDS)
        spread = one_hot((iota((32, 8 * FIELDS), 1) >> 3) == iota((32, 8 * FIELDS), 0))
        full = exact(exact_nt(pick, back), spread)
        full = jnp.where((iota(shape, 0) & 7) == (iota(shape, 1) & 7), full, 0.0)
        high, low = split(full)
        unmix_ref[0:wide] = high
        unmix_ref[wide : 2 * wide] = low

        r, m = iota((16 * ZS, 32), 0) & 15, iota((16 * ZS, 32), 1)
        rates = exact(one_hot((r == m) & (r < LINES + 2)), tab)
        sums_x = exact(one_hot(m == jnp.where(r < LINES, r + LINES, 2 * LINES)), back)
        sums_y = exact(one_hot(m == jnp.where(r < LINES, r + LINES, 2 * LINES + 1)), back)
        r = iota((16 * ZS, N), 0) & 15
        sums_x = jnp.where(r <= LINES, -step_x * sums_x, 0.0)
        sums_y = jnp.where(r <= LINES, -step_y * sums_y, 0.0)

        def place(ring):
            shape = (8 * ring.count, N)
            per = -(-ELEMENTS // ring.tiles)
            row = iota(shape, 0) & (ring.wide - 1)
            inside = row & 7
            return one_hot((inside < per) & ((row >> 3) * per + inside == iota(shape, 1)))

        def same(shape, rows, cols):
            shift = lambda n: n.bit_length() - 1
            return (iota(shape, 0) >> shift(rows)) == (iota(shape, 1) >> shift(cols))

        place_x, place_y = place(beam), place(det)
        wax_ref[...] = jnp.where(
            same(wax_ref.shape, 16, beam.wide), exact_nt(rates * (step_x / step_y), place_x), 0.0
        )
        way_ref[...] = jnp.where(same(way_ref.shape, 16, det.wide), exact_nt(rates, place_y), 0.0)
        wcx_ref[...] = jnp.where(same(wcx_ref.shape, beam.wide, 16), exact_nt(place_x, sums_x), 0.0)
        wcy_ref[...] = jnp.where(same(wcy_ref.shape, det.wide, 16), exact_nt(place_y, sums_y), 0.0)

        r, c = iota((2 * N, N), 0) & (N - 1), iota((2 * N, N), 1)
        up_ref[...] = one_hot(r < c).astype(BF16)
        down_ref[...] = (step_y * one_hot(r > c)).astype(BF16)
        r, c = iota((N, 2 * N), 0), iota((N, 2 * N), 1) & (N - 1)
        left_ref[...] = (step_x / step_y * one_hot(c < r)).astype(BF16)
        right_ref[...] = (step_x * one_hot(c > r)).astype(BF16)
        for z in range(ZS):
            live1 = live1_ref[z : z + 1, :].astype(F32)
            live2 = live2_ref[z : z + 1, :].astype(F32)
            for l in range(LINES):
                x, y = beam.wide * z + beam.spot(l, LINES), det.wide * z + det.spot(l, LINES)
                lx_ref[x : x + 1, :] = live1
                ly_ref[y : y + 1, :] = live2
                mx_ref[x : x + 1, :] = m1_ref[l, z : z + 1, :]
                my_ref[y : y + 1, :] = m2_ref[l, z : z + 1, :]

    tables()

    def groups(body):
        for z in range(ZS):
            for r0 in range(0, N, 32):
                body(z, r0)

    def mix(z, r0):
        parts = []
        for b in range(4):
            high, low = split(c_ref[:, z, pl.ds(r0 + 8 * b, 8), :].reshape(8 * ELEMENTS, N))
            parts.append(jnp.concatenate([high, high, low, jnp.zeros((16, N), BF16)], 0))
        out = dot(mix_ref[...], jnp.concatenate(parts, 1))
        rows = pl.ds(r0, 32)
        for f in range(FIELDS):
            field = jnp.concatenate([out[8 * f : 8 * f + 8, b * N : (b + 1) * N] for b in range(4)], 0)
            if f < LINES + 2:
                high, low = split(field)
                m_ref[z, f, rows, 0:N] = high
                m_ref[z, f, rows, N : 2 * N] = low
            else:
                q_ref[z, f - LINES - 2, rows, :] = field

    def unmix(z, r0):
        highs, lows = [], []
        for b in range(4):
            rows = pl.ds(r0 + 8 * b, 8)
            w = w_ref[z, :, rows, :].reshape(8 * LINES, N)
            v = v_ref[z, :, rows, :].reshape(8 * (LINES + 2), N)
            high, low = split(jnp.concatenate([w, v], 0))
            highs.append(high)
            lows.append(low)
        wide = 8 * ELEMENTS
        one = dot(unmix_ref[...], jnp.concatenate(highs, 1))
        two = dot(unmix_ref[0:wide], jnp.concatenate(lows, 1))
        out = one[0:wide] + (one[wide:] + two)
        for b in range(4):
            rows = pl.ds(r0 + 8 * b, 8)
            d_ref[:, z, rows, :] = c_ref[:, z, rows, :] - out[:, b * N : (b + 1) * N].reshape(ELEMENTS, 8, N)

    def stacked(ref, z, fields):
        value = [ref[z, f] for f in fields]
        high = jnp.concatenate([v[:, 0:N] for v in value], 1)
        low = jnp.concatenate([v[:, N : 2 * N] for v in value], 1)
        return jnp.concatenate([high, low], 0)

    def prefixes(z):
        for l in range(0, LINES, 2):
            out = dot(m_ref[z, l : l + 2].reshape(2 * N, 2 * N), up_ref[...])
            e1_ref[z, l : l + 2] = out.reshape(2, N, N)
            out = dot(left_ref[...], stacked(m_ref, z, (l, l + 1)))
            e2_ref[z, l] = out[:, 0:N]
            e2_ref[z, l + 1] = out[:, N : 2 * N]
        e1_ref[z, LINES] = dot(m_ref[z, LINES], up_ref[...])
        e2_ref[z, LINES] = dot(left_ref[...], stacked(m_ref, z, (LINES + 1,)))

    def suffixes(z):
        for l in range(0, LINES, 2):
            over_y = dot(p1_ref[z, l : l + 2].reshape(2 * N, 2 * N), down_ref[...])
            over_x = dot(right_ref[...], stacked(p2_ref, z, (l, l + 1)))
            v_ref[z, l] = over_y[0:N] + over_x[:, 0:N]
            v_ref[z, l + 1] = over_y[N : 2 * N] + over_x[:, N : 2 * N]
        v_ref[z, LINES] = dot(right_ref[...], stacked(p2_ref, z, (LINES,)))
        v_ref[z, LINES + 1] = dot(p1_ref[z, LINES], down_ref[...])

    def counts():
        enter_x = exact(wax_ref[...], beam.rows(bdone, 0))
        enter_y = exact(way_ref[...], det.rows(ddone, 0))
        rows_ref[:, 0:16] = enter_x.reshape(ZS, 16, N)
        for z in range(ZS):
            cols_ref[z] = turned(enter_y[16 * z : 16 * (z + 1)])

        def one(z):
            def chunk(rows):
                cols = cols_ref[z, rows]
                tin1 = jnp.exp2(e2_ref[z, LINES, rows] + rows_ref[z, LINES + 1 : LINES + 2])
                tin2 = jnp.exp2(e1_ref[z, LINES, rows] + cols[:, LINES : LINES + 1])
                sums = []
                acc = jnp.zeros((CHUNK, N), F32)
                for l in range(LINES):
                    a1 = tin1 * jnp.exp2(e1_ref[z, l, rows] + cols[:, l : l + 1])
                    a2 = tin2 * jnp.exp2(e2_ref[z, l, rows] + rows_ref[z, l : l + 1])
                    a1_ref[z, l, rows] = a1
                    a2_ref[z, l, rows] = a2
                    q = q_ref[z, l, rows]
                    sums.append(q * a1)
                    acc = jnp.where(lane == det.spot(l, LINES), jnp.sum(q * a2, 1, keepdims=True), acc)
                acc_ref[z, rows] = acc
                return sums

            for l, row in enumerate(chunks(LINES, chunk)):
                beam.put(1, z, beam.spot(l, LINES), step_x * row)

        over_z(one)
        for z in range(ZS):
            det.put_z(1, z, step_y * acc_ref[z].T[0 : det.wide])

    def residuals():
        res1 = lx_ref[...] * (beam.rows(bdone, 1) - mx_ref[...])
        res2 = ly_ref[...] * (det.rows(ddone, 1) - my_ref[...])
        sum1 = res1 * beam.rows(bsend, 1) / step_x
        sum2 = res2 * det.rows(dsend, 1) / step_y
        rows_ref[:, 0 : beam.wide] = res1.reshape(ZS, beam.wide, N)
        for z in range(ZS):
            cols_ref[z] = turned(res2[det.wide * z : det.wide * (z + 1)])

        def one(z):
            def chunk(rows):
                cols = cols_ref[z, rows]
                sums = []
                acc = jnp.zeros((CHUNK, N), F32)
                all1 = jnp.zeros((CHUNK, N), F32)
                all2 = jnp.zeros((CHUNK, N), F32)

                def keep(ref, f, value):
                    high, low = split(value)
                    ref[z, f, rows, 0:N] = high
                    ref[z, f, rows, N : 2 * N] = low

                for l in range(LINES):
                    x, y = beam.spot(l, LINES), det.spot(l, LINES)
                    w1 = a1_ref[z, l, rows] * rows_ref[z, x : x + 1]
                    w2 = a2_ref[z, l, rows] * cols[:, y : y + 1]
                    w_ref[z, l, rows] = w1 + w2
                    q = q_ref[z, l, rows]
                    p1, p2 = q * w1, q * w2
                    all1, all2 = all1 + p1, all2 + p2
                    sums.append(p2)
                    acc = jnp.where(lane == l, jnp.sum(p1, 1, keepdims=True), acc)
                    keep(p1_ref, l, p1)
                    keep(p2_ref, l, p2)
                keep(p1_ref, LINES, all2)
                keep(p2_ref, LINES, all1)
                acc_ref[z, rows] = acc
                return sums

            for l, row in enumerate(chunks(LINES, chunk)):
                tx_ref[z, l : l + 1] = row

        over_z(one)
        for z in range(ZS):
            ty_ref[z] = acc_ref[z].T[0:16]
            k = slice(LINES, LINES + 1)
            tx_ref[z, k] = jnp.sum(sum1[beam.wide * z : beam.wide * (z + 1)], 0, keepdims=True)
            ty_ref[z, k] = jnp.sum(sum2[det.wide * z : det.wide * (z + 1)], 0, keepdims=True)
        beam.put_all(2, exact(wcx_ref[...], tx_ref[...].reshape(16 * ZS, N)))
        det.put_all(2, exact(wcy_ref[...], ty_ref[...].reshape(16 * ZS, N)))

    def update():
        rows_ref[:, 0 : beam.wide] = beam.rows(bdone, 2).reshape(ZS, beam.wide, N)
        enter = det.rows(ddone, 2)
        for z in range(ZS):
            cols_ref[z] = turned(enter[det.wide * z : det.wide * (z + 1)])
        totals(True)

    def turn(step, carry):
        last = step == STEPS - 1
        groups(mix)
        det.middle(0, "earlier")
        beam.middle(0, "earlier")
        over_z(prefixes)
        det.finish(0)
        beam.finish(0)
        counts()
        det.start(1)
        beam.start(1)
        det.middle(1, "sum")
        beam.middle(1, "sum")
        det.finish(1)
        beam.finish(1)
        residuals()
        det.start(2)
        beam.start(2)
        over_z(suffixes)
        det.middle(2, "later")
        beam.middle(2, "later")
        groups(unmix)

        def stores():
            return [pltpu.make_async_copy(d_ref.at[:, z], out_hbm.at[:, z], conc_sems.at[z]) for z in range(ZS)]

        @pl.when(last)
        def leave():
            for store in stores():
                store.start()

        det.finish(2)
        beam.finish(2)

        @pl.when(last)
        def left():
            for store in stores():
                store.wait()

        @pl.when(jnp.logical_not(last))
        def go_on():
            update()
            det.start(0)
            beam.start(0)

        return carry

    lax.fori_loop(0, STEPS, turn, 0)
    dx_ref[...] = bdone[2]
    dy_ref[...] = ddone[2]


def close(x_spots, y_spots, c_ref, dx_ref, dy_ref, out_ref):
    rows = dx_ref[...].reshape(-1, N)
    cols = dy_ref[...].reshape(-1, N)
    cols = jnp.concatenate([cols, jnp.zeros((N - cols.shape[0], N), F32)], 0).T
    for e in range(ELEMENTS):
        x, y = x_spots[e], y_spots[e]
        out_ref[e, 0] = c_ref[e, 0] + rows[x : x + 1] + cols[:, y : y + 1]


def solution(mesh):
    beams, dets = mesh.shape["beam"], mesh.shape["det"]

    def shards(conc, inc, sig, yld, rate, axis, m1, live1, m2, live2):
        step_x = 1.0 / (conc.shape[2] * beams)
        step_y = 1.0 / (conc.shape[3] * dets)

        def body(*refs):
            kernel(step_x, step_y, *refs)

        def exchange(count):
            tiles = pltpu.VMEM((3, count, 8, N), F32)
            return [tiles] * 4 + [pltpu.SemaphoreType.DMA((3, 2, 2))]

        def spots(tiles):
            per = -(-ELEMENTS // tiles)
            return [8 * (e // per) + e % per for e in range(ELEMENTS)]

        field = (N, N)
        anywhere = pl.BlockSpec(memory_space=pl.ANY)
        vmem = pl.BlockSpec(memory_space=pltpu.VMEM)
        small = (axis[None], inc, sig, yld, rate[None], m1, live1, m2, live2)
        inner, dx, dy = pl.pallas_call(
            body,
            out_shape=[
                jax.ShapeDtypeStruct(conc.shape, F32),
                jax.ShapeDtypeStruct((beams, 8, N), F32),
                jax.ShapeDtypeStruct((dets, 8, N), F32),
            ],
            in_specs=[anywhere] * (len(small) + 1),
            out_specs=[anywhere, vmem, vmem],
            scratch_shapes=[
                *[pltpu.VMEM(a.shape, a.dtype) for a in small + (conc,)],
                pltpu.SemaphoreType.DMA((len(small),)),
                pltpu.SemaphoreType.DMA((ZS,)),
                pltpu.VMEM((ZS, LINES + 2, N, 2 * N), BF16),
                pltpu.VMEM((ZS, LINES) + field, F32),
                *[pltpu.VMEM((ZS, LINES + 1) + field, F32)] * 2,
                *[pltpu.VMEM((ZS, LINES) + field, F32)] * 3,
                *[pltpu.VMEM((ZS, LINES + 1, N, 2 * N), BF16)] * 2,
                pltpu.VMEM((ZS, LINES + 2) + field, F32),
                pltpu.VMEM(conc.shape, F32),
                pltpu.VMEM((ZS, 16, N), F32),
                *[pltpu.VMEM((ZS,) + field, F32)] * 2,
                pltpu.VMEM((8 * beams, N), F32),
                pltpu.VMEM((8 * dets, N), F32),
                pltpu.VMEM((8 * beams, N), F32),
                pltpu.VMEM((8 * dets, N), F32),
                *[pltpu.VMEM((ZS, 16, N), F32)] * 2,
                *[pltpu.VMEM((32, N), F32)] * 2,
                pltpu.VMEM((8 * FIELDS, 2 * N), BF16),
                pltpu.VMEM((16 * ELEMENTS, 8 * FIELDS), BF16),
                *[pltpu.VMEM((2 * N, N), BF16)] * 2,
                *[pltpu.VMEM((N, 2 * N), BF16)] * 2,
                pltpu.VMEM((16 * ZS, 8 * beams), F32),
                pltpu.VMEM((16 * ZS, 8 * dets), F32),
                pltpu.VMEM((8 * beams, 16 * ZS), F32),
                pltpu.VMEM((8 * dets, 16 * ZS), F32),
                *exchange(beams),
                *exchange(dets),
            ],
            compiler_params=pltpu.CompilerParams(
                collective_id=0, has_side_effects=True, vmem_limit_bytes=64 * 1024 * 1024
            ),
        )(*small, conc)

        x_tiles, y_tiles = beams // ZS, dets // ZS

        def last(*refs):
            close(spots(x_tiles), spots(y_tiles), *refs)

        block = pl.BlockSpec((ELEMENTS, 1, N, N), lambda z: (0, z, 0, 0))
        return pl.pallas_call(
            last,
            out_shape=jax.ShapeDtypeStruct(conc.shape, F32),
            grid=(ZS,),
            in_specs=[
                block,
                pl.BlockSpec((x_tiles, 8, N), lambda z: (z, 0, 0)),
                pl.BlockSpec((y_tiles, 8, N), lambda z: (z, 0, 0)),
            ],
            out_specs=block,
            compiler_params=pltpu.CompilerParams(vmem_limit_bytes=64 * 1024 * 1024),
        )(inner, dx, dy)

    in_specs = (
        P(None, None, "beam", "det"),
        P(),
        P(),
        P(),
        P(),
        P(),
        P(None, None, "det"),
        P(None, "det"),
        P(None, None, "beam"),
        P(None, "beam"),
    )
    out_specs = P(None, None, "beam", "det")
    return jax.shard_map(shards, mesh=mesh, in_specs=in_specs, out_specs=out_specs, check_vma=False)
```

```python
import math

import jax
import jax.numpy as jnp
from jax import lax
from jax.experimental import pallas as pl
from jax.experimental.pallas import tpu as pltpu
from jax.sharding import PartitionSpec as P

STEPS = 2
HIGH = lax.Precision.HIGHEST
MESH = pl.DeviceIdType.MESH
F32 = jnp.float32
BF16 = jnp.bfloat16
ELEMENTS = 10
LINES = 12
ZS = 4
N = 128
FIELDS = 26
CHUNK = 64
AHEAD = 4
ROWS = (ELEMENTS * ZS, LINES * ZS, ELEMENTS * ZS)
LOG2E = math.log2(math.e)


def split(value):
    high = value.astype(BF16)
    return high, (value - high.astype(F32)).astype(BF16)


def iota(shape, dim):
    return lax.broadcasted_iota(jnp.int32, shape, dim)


def dot(a, b):
    return jnp.dot(a, b, preferred_element_type=F32)


def exact(a, b):
    return jnp.dot(a, b, preferred_element_type=F32, precision=HIGH)


def exact_nt(a, b):
    return lax.dot_general(
        a, b, (((1,), (1,)), ((), ())), preferred_element_type=F32, precision=HIGH
    )


def one_hot(condition):
    return jnp.where(condition, 1.0, 0.0).astype(F32)


class Ring:
    def __init__(self, axis, count, send, near, out, far, sems):
        self.axis, self.count = axis, count
        self.send, self.near, self.out, self.far, self.sems = send, near, out, far, sems
        self.slots = count // AHEAD
        self.cores = self.slots // 2
        me = lax.axis_index(axis)
        self.c = lax.rem(me, self.cores)
        self.x = lax.rem(me // self.cores, AHEAD)
        self.y = me // (self.cores * AHEAD)
        self.slot = self.y * self.cores + self.c

    def index(self, y, x, c):
        return (y * AHEAD + x) * self.cores + c

    def near_peers(self):
        slots = [lax.rem(self.slot + d, self.slots) for d in range(1, self.slots)]
        return [self.index(k // self.cores, self.x, lax.rem(k, self.cores)) for k in slots]

    def far_peers(self):
        return [(d, self.index(self.y, lax.rem(self.x + d, AHEAD), self.c)) for d in (2, 1, 3)]

    def greet(self, barrier):
        peers = self.near_peers() + [peer for _, peer in self.far_peers()]
        for peer in peers:
            pl.semaphore_signal(barrier, inc=1, device_id={self.axis: peer}, device_id_type=MESH)
        return len(peers)

    def copy(self, src, dst, phase, leg, peer):
        return pltpu.make_async_remote_copy(
            src_ref=src,
            dst_ref=dst,
            send_sem=self.sems.at[phase, leg, 0],
            recv_sem=self.sems.at[phase, leg, 1],
            device_id={self.axis: peer},
            device_id_type=MESH,
        )

    def start(self, phase):
        rows = pl.ds(0, ROWS[phase])
        self.near[phase, pl.ds(self.slot, 1), rows] = self.send[phase, rows][None]
        for peer in self.near_peers():
            self.copy(self.send.at[phase, rows], self.near.at[phase, self.slot, rows], phase, 0, peer).start()

    def wait(self, ref, phase, leg, count):
        some = ref.at[phase, pl.ds(0, count), pl.ds(0, ROWS[phase])]
        whole = self.copy(some, some, phase, leg, self.near_peers()[0])
        whole.wait_send()
        whole.wait_recv()

    def middle(self, phase, mode):
        rows = pl.ds(0, ROWS[phase])
        self.wait(self.near, phase, 0, self.slots - 1)
        have = [[self.near[phase, y * self.cores + c, rows] for c in range(self.cores)] for y in range(2)]
        sums = [sum(cores[1:], cores[0]) for cores in have]
        if mode == "sum":
            mine = sums[0] + sums[1]
            self.out[phase, 0, rows] = mine
        else:
            earlier = mode == "earlier"

            def chosen(other, own):
                return (other < own if earlier else other > own).astype(F32)

            base = sum(sums[y] * chosen(y, self.y) for y in range(2))
            same = sum(sums[y] * (self.y == y).astype(F32) for y in range(2))
            mine = base
            for y in range(2):
                for c in range(self.cores):
                    mine = mine + have[y][c] * ((self.y == y).astype(F32) * chosen(c, self.c))
            self.out[phase, 0, rows] = base
            self.out[phase, 1, rows] = base + same
        self.far[phase, pl.ds(self.x, 1), rows] = mine[None]
        for d, peer in self.far_peers():
            wrap = (self.x + d) // AHEAD
            which = {"sum": 0, "earlier": 1 - wrap, "later": wrap}[mode]
            self.copy(self.out.at[phase, which, rows], self.far.at[phase, self.x, rows], phase, 1, peer).start()

    def finish(self, phase):
        self.wait(self.far, phase, 1, AHEAD - 1)
        rows = pl.ds(0, ROWS[phase])
        return (self.far[phase, 0, rows] + self.far[phase, 1, rows]) + (
            self.far[phase, 2, rows] + self.far[phase, 3, rows]
        )

    def put(self, phase, row, value):
        self.send[phase, row : row + 1, :] = value


def kernel(
    beams, dets, step_x, step_y,
    axis_hbm, inc_hbm, sig_hbm, yld_hbm, rate_hbm, m1_hbm, live1_hbm, m2_hbm, live2_hbm, conc_hbm,
    out_hbm, dx_ref, dy_ref,
    axis_ref, inc_ref, sig_ref, yld_ref, rate_ref, m1_ref, live1_ref, m2_ref, live2_ref, c_ref,
    load_sems, conc_sems,
    m_ref, q_ref, e1_ref, e2_ref, a1_ref, a2_ref, w_ref, p1_ref, p2_ref, v_ref, d_ref, rows_ref, cols_ref, acc_ref,
    mx_ref, my_ref, lx_ref, ly_ref,
    tx_ref, ty_ref, tab_ref, back_ref, mix_ref, unmix_ref, up_ref, down_ref, left_ref, right_ref,
    wax_ref, way_ref, wcx_ref, wcy_ref,
    bsend, bnear, bout, bfar, bsems, dsend, dnear, dout, dfar, dsems,
):
    def conc_load(z):
        return pltpu.make_async_copy(conc_hbm.at[:, z], c_ref.at[:, z], conc_sems.at[z])

    hbm = (axis_hbm, inc_hbm, sig_hbm, yld_hbm, rate_hbm, m1_hbm, live1_hbm, m2_hbm, live2_hbm)
    vmem = (axis_ref, inc_ref, sig_ref, yld_ref, rate_ref, m1_ref, live1_ref, m2_ref, live2_ref)
    loads = [pltpu.make_async_copy(a, b, load_sems.at[k]) for k, (a, b) in enumerate(zip(hbm, vmem))]
    for load in [conc_load(z) for z in range(ZS)] + loads:
        load.start()
    beam = Ring("beam", beams, bsend, bnear, bout, bfar, bsems)
    det = Ring("det", dets, dsend, dnear, dout, dfar, dsems)
    barrier = pltpu.get_barrier_semaphore()
    greeted = det.greet(barrier) + beam.greet(barrier)

    for ref in (bsend, dsend, cols_ref, mx_ref, my_ref, lx_ref, ly_ref, tx_ref, ty_ref, tab_ref, back_ref):
        ref[...] = jnp.zeros(ref.shape, F32)

    lane = iota((CHUNK, N), 1)

    def over_z(body):
        for z in range(ZS):
            body(z)

    def sweep(body):
        sums = [None] * ZS
        for r in range(0, N, CHUNK):
            acc = jnp.zeros((CHUNK, N), F32)
            for z in range(ZS):
                new, acc = body(z, pl.ds(r, CHUNK), acc)
                new = [jnp.sum(a.reshape(CHUNK // 8, 8, N), 0) for a in new]
                sums[z] = new if r == 0 else [a + b for a, b in zip(sums[z], new)]
            acc_ref[pl.ds(r, CHUNK)] = acc
        return [[jnp.sum(a, 0, keepdims=True) for a in part] for part in sums]

    def turned(rows):
        return jnp.concatenate([rows, jnp.zeros((N - rows.shape[0], N), F32)], 0).T

    def totals(add):
        if add is not None:
            rows_ref[0 : ELEMENTS * ZS] = add

        def body(z, rows, acc):
            if add is None and rows.start == 0:
                conc_load(z).wait()
            sums = []
            cols = cols_ref[rows]
            for e in range(ELEMENTS):
                k = ELEMENTS * z + e
                if add is None:
                    c = c_ref[e, z, rows]
                else:
                    c = d_ref[e, z, rows] + rows_ref[k : k + 1] + cols[:, k : k + 1]
                    c_ref[e, z, rows] = c
                sums.append(c)
                acc = jnp.where(lane == k, jnp.sum(c, 1, keepdims=True), acc)
            return sums, acc

        for z, sums in enumerate(sweep(body)):
            for e, row in enumerate(sums):
                beam.put(0, ELEMENTS * z + e, row)
        dsend[0, 0 : ELEMENTS * ZS] = acc_ref[...].T[0 : ELEMENTS * ZS]

    totals(None)
    pl.semaphore_wait(barrier, greeted)
    det.start(0)
    beam.start(0)
    for load in loads:
        load.wait()

    def tables():
        first = axis_ref[0:1, 0:1] == 0
        one, two = inc_ref[0:1, :], inc_ref[1:2, :]
        s1 = jnp.where(first, one, two)
        s2 = jnp.where(first, two, one)
        scale = -LOG2E * step_y
        sig, yld, rate = sig_ref[...], yld_ref[...], rate_ref[...]
        cols = pl.ds(0, ELEMENTS)
        tab_ref[0:LINES, cols] = scale * sig
        tab_ref[LINES : LINES + 1, cols] = scale * s2
        tab_ref[LINES + 1 : LINES + 2, cols] = scale * s1
        tab_ref[LINES + 2 : FIELDS, cols] = yld
        back_ref[0:LINES, cols] = yld * rate
        back_ref[LINES : 2 * LINES, cols] = -sig * rate
        back_ref[2 * LINES : 2 * LINES + 1, cols] = -s1 * rate
        back_ref[2 * LINES + 1 : FIELDS, cols] = -s2 * rate

        tab, back = tab_ref[...], back_ref[...]
        wide = 8 * ELEMENTS
        pick = one_hot((iota((8 * FIELDS, 32), 0) >> 3) == iota((8 * FIELDS, 32), 1))
        col = iota((N, 256), 1)
        part = (col >= wide).astype(jnp.int32) + (col >= 2 * wide).astype(jnp.int32)
        spread = one_hot(((col - wide * part) >> 3) == iota((N, 256), 0))
        spread = jnp.where(col < 3 * wide, spread, 0.0)
        full = exact(pick, exact(tab, spread))
        shape = (8 * FIELDS, 256)
        full = jnp.where((iota(shape, 0) & 7) == (iota(shape, 1) & 7), full, 0.0)
        high, low = split(full)
        part = iota(shape, 1)
        mix_ref[...] = jnp.where((part >= wide) & (part < 2 * wide), low.astype(F32), high.astype(F32)).astype(BF16)

        pick = one_hot((iota((wide, N), 0) >> 3) == iota((wide, N), 1))
        shape = (wide, 8 * FIELDS)
        spread = one_hot((iota((32, 8 * FIELDS), 1) >> 3) == iota((32, 8 * FIELDS), 0))
        full = exact(exact_nt(pick, back), spread)
        full = jnp.where((iota(shape, 0) & 7) == (iota(shape, 1) & 7), full, 0.0)
        high, low = split(full)
        unmix_ref[0:wide] = high
        unmix_ref[wide : 2 * wide] = low

        r, m = iota((16 * ZS, 32), 0) & 15, iota((16 * ZS, 32), 1)
        rates = exact(one_hot((r == m) & (r < LINES + 2)), tab)
        sums_x = exact(one_hot(m == jnp.where(r < LINES, r + LINES, 2 * LINES)), back)
        sums_y = exact(one_hot(m == jnp.where(r < LINES, r + LINES, 2 * LINES + 1)), back)
        r = iota((16 * ZS, N), 0) & 15
        sums_x = jnp.where(r <= LINES, -step_x * sums_x, 0.0)
        sums_y = jnp.where(r <= LINES, -step_y * sums_y, 0.0)

        def slice_of(shape, dim):
            row = iota(shape, dim)
            return sum((row >= ELEMENTS * z).astype(jnp.int32) for z in range(1, ZS))

        shape = (ELEMENTS * ZS, N)
        place = one_hot(iota(shape, 0) - ELEMENTS * slice_of(shape, 0) == iota(shape, 1))
        shape = wax_ref.shape
        same = (iota(shape, 0) >> 4) == slice_of(shape, 1)
        wax_ref[...] = jnp.where(same, exact_nt(rates * (step_x / step_y), place), 0.0)
        way_ref[...] = jnp.where(same, exact_nt(rates, place), 0.0)
        shape = wcx_ref.shape
        same = slice_of(shape, 0) == (iota(shape, 1) >> 4)
        wcx_ref[...] = jnp.where(same, exact_nt(place, sums_x), 0.0)
        wcy_ref[...] = jnp.where(same, exact_nt(place, sums_y), 0.0)

        r, c = iota((2 * N, N), 0) & (N - 1), iota((2 * N, N), 1)
        up_ref[...] = one_hot(r < c).astype(BF16)
        down_ref[...] = (step_y * one_hot(r > c)).astype(BF16)
        r, c = iota((N, 2 * N), 0), iota((N, 2 * N), 1) & (N - 1)
        left_ref[...] = (step_x / step_y * one_hot(c < r)).astype(BF16)
        right_ref[...] = (step_x * one_hot(c > r)).astype(BF16)
        for z in range(ZS):
            live1 = live1_ref[z : z + 1, :].astype(F32)
            live2 = live2_ref[z : z + 1, :].astype(F32)
            for l in range(LINES):
                k = LINES * z + l
                lx_ref[k : k + 1, :] = live1
                ly_ref[k : k + 1, :] = live2
                mx_ref[k : k + 1, :] = m1_ref[l, z : z + 1, :]
                my_ref[k : k + 1, :] = m2_ref[l, z : z + 1, :]

    tables()

    def groups(body):
        for z in range(ZS):
            for r0 in range(0, N, 32):
                body(z, r0)

    def mix(z, r0):
        parts = []
        for b in range(4):
            high, low = split(c_ref[:, z, pl.ds(r0 + 8 * b, 8), :].reshape(8 * ELEMENTS, N))
            parts.append(jnp.concatenate([high, high, low, jnp.zeros((16, N), BF16)], 0))
        out = dot(mix_ref[...], jnp.concatenate(parts, 1))
        rows = pl.ds(r0, 32)
        for f in range(FIELDS):
            field = jnp.concatenate([out[8 * f : 8 * f + 8, b * N : (b + 1) * N] for b in range(4)], 0)
            if f < LINES + 2:
                high, low = split(field)
                m_ref[z, f, rows, 0:N] = high
                m_ref[z, f, rows, N : 2 * N] = low
            else:
                q_ref[z, f - LINES - 2, rows, :] = field

    def unmix(z, r0):
        highs, lows = [], []
        for b in range(4):
            rows = pl.ds(r0 + 8 * b, 8)
            w = w_ref[z, :, rows, :].reshape(8 * LINES, N)
            v = v_ref[z, :, rows, :].reshape(8 * (LINES + 2), N)
            high, low = split(jnp.concatenate([w, v], 0))
            highs.append(high)
            lows.append(low)
        wide = 8 * ELEMENTS
        one = dot(unmix_ref[...], jnp.concatenate(highs, 1))
        two = dot(unmix_ref[0:wide], jnp.concatenate(lows, 1))
        out = one[0:wide] + (one[wide:] + two)
        for b in range(4):
            rows = pl.ds(r0 + 8 * b, 8)
            d_ref[:, z, rows, :] = c_ref[:, z, rows, :] - out[:, b * N : (b + 1) * N].reshape(ELEMENTS, 8, N)

    def stacked(ref, z, fields):
        value = [ref[z, f] for f in fields]
        high = jnp.concatenate([v[:, 0:N] for v in value], 1)
        low = jnp.concatenate([v[:, N : 2 * N] for v in value], 1)
        return jnp.concatenate([high, low], 0)

    def prefixes(z):
        for l in range(0, LINES, 2):
            out = dot(m_ref[z, l : l + 2].reshape(2 * N, 2 * N), up_ref[...])
            e1_ref[z, l : l + 2] = out.reshape(2, N, N)
            out = dot(left_ref[...], stacked(m_ref, z, (l, l + 1)))
            e2_ref[z, l] = out[:, 0:N]
            e2_ref[z, l + 1] = out[:, N : 2 * N]
        e1_ref[z, LINES] = dot(m_ref[z, LINES], up_ref[...])
        e2_ref[z, LINES] = dot(left_ref[...], stacked(m_ref, z, (LINES + 1,)))

    def suffixes(z):
        for l in range(0, LINES, 2):
            over_y = dot(p1_ref[z, l : l + 2].reshape(2 * N, 2 * N), down_ref[...])
            over_x = dot(right_ref[...], stacked(p2_ref, z, (l, l + 1)))
            v_ref[z, l] = over_y[0:N] + over_x[:, 0:N]
            v_ref[z, l + 1] = over_y[N : 2 * N] + over_x[:, N : 2 * N]
        v_ref[z, LINES] = dot(right_ref[...], stacked(p2_ref, z, (LINES,)))
        v_ref[z, LINES + 1] = dot(p1_ref[z, LINES], down_ref[...])

    def counts(enter_x, enter_y):
        rows_ref[...] = exact(wax_ref[...], enter_x)
        cols_ref[...] = turned(exact(way_ref[...], enter_y))

        def body(z, rows, acc):
            cols = cols_ref[rows]
            k = 16 * z + LINES
            tin1 = jnp.exp2(e2_ref[z, LINES, rows] + rows_ref[k + 1 : k + 2])
            tin2 = jnp.exp2(e1_ref[z, LINES, rows] + cols[:, k : k + 1])
            sums = []
            for l in range(LINES):
                k = 16 * z + l
                a1 = tin1 * jnp.exp2(e1_ref[z, l, rows] + cols[:, k : k + 1])
                a2 = tin2 * jnp.exp2(e2_ref[z, l, rows] + rows_ref[k : k + 1])
                a1_ref[z, l, rows] = a1
                a2_ref[z, l, rows] = a2
                q = q_ref[z, l, rows]
                sums.append(q * a1)
                acc = jnp.where(lane == LINES * z + l, jnp.sum(q * a2, 1, keepdims=True), acc)
            return sums, acc

        for z, sums in enumerate(sweep(body)):
            for l, row in enumerate(sums):
                beam.put(1, LINES * z + l, step_x * row)
        dsend[1] = step_y * acc_ref[...].T[0 : LINES * ZS]

    def residuals(pred1, pred2):
        res1 = lx_ref[...] * (pred1 - mx_ref[...])
        res2 = ly_ref[...] * (pred2 - my_ref[...])
        sum1 = res1 * bsend[1] / step_x
        sum2 = res2 * dsend[1] / step_y
        rows_ref[0 : LINES * ZS] = res1
        cols_ref[...] = turned(res2)

        def body(z, rows, acc):
            cols = cols_ref[rows]
            sums = []
            all1 = jnp.zeros((CHUNK, N), F32)
            all2 = jnp.zeros((CHUNK, N), F32)

            def keep(ref, f, value):
                high, low = split(value)
                ref[z, f, rows, 0:N] = high
                ref[z, f, rows, N : 2 * N] = low

            for l in range(LINES):
                k = LINES * z + l
                w1 = a1_ref[z, l, rows] * rows_ref[k : k + 1]
                w2 = a2_ref[z, l, rows] * cols[:, k : k + 1]
                w_ref[z, l, rows] = w1 + w2
                q = q_ref[z, l, rows]
                p1, p2 = q * w1, q * w2
                all1, all2 = all1 + p1, all2 + p2
                sums.append(p2)
                acc = jnp.where(lane == 16 * z + l, jnp.sum(p1, 1, keepdims=True), acc)
                keep(p1_ref, l, p1)
                keep(p2_ref, l, p2)
            keep(p1_ref, LINES, all2)
            keep(p2_ref, LINES, all1)
            return sums, acc

        for z, sums in enumerate(sweep(body)):
            for l, row in enumerate(sums):
                tx_ref[16 * z + l : 16 * z + l + 1] = row
        ty_ref[...] = acc_ref[...].T[0 : 16 * ZS]
        for z in range(ZS):
            k, part = 16 * z + LINES, slice(LINES * z, LINES * (z + 1))
            tx_ref[k : k + 1] = jnp.sum(sum1[part], 0, keepdims=True)
            ty_ref[k : k + 1] = jnp.sum(sum2[part], 0, keepdims=True)
        bsend[2, 0 : ELEMENTS * ZS] = exact(wcx_ref[...], tx_ref[...])
        dsend[2, 0 : ELEMENTS * ZS] = exact(wcy_ref[...], ty_ref[...])

    def turn(step, carry):
        last = step == STEPS - 1
        groups(mix)
        det.middle(0, "earlier")
        beam.middle(0, "earlier")
        over_z(prefixes)
        enter_y = det.finish(0)
        enter_x = beam.finish(0)
        counts(enter_x, enter_y)
        det.start(1)
        beam.start(1)
        det.middle(1, "sum")
        beam.middle(1, "sum")
        pred2 = det.finish(1)
        pred1 = beam.finish(1)
        residuals(pred1, pred2)
        det.start(2)
        beam.start(2)
        over_z(suffixes)
        det.middle(2, "later")
        beam.middle(2, "later")
        groups(unmix)

        def stores():
            return [pltpu.make_async_copy(d_ref.at[:, z], out_hbm.at[:, z], conc_sems.at[z]) for z in range(ZS)]

        @pl.when(last)
        def leave():
            for store in stores():
                store.start()

        after_y = det.finish(2)
        after_x = beam.finish(2)

        @pl.when(last)
        def left():
            for z in range(ZS):
                part = slice(ELEMENTS * z, ELEMENTS * (z + 1))
                dx_ref[z, 0:ELEMENTS] = after_x[part]
                dy_ref[z, 0:ELEMENTS] = after_y[part]
            for store in stores():
                store.wait()

        @pl.when(jnp.logical_not(last))
        def go_on():
            cols_ref[...] = turned(after_y)
            totals(after_x)
            det.start(0)
            beam.start(0)

        return carry

    lax.fori_loop(0, STEPS, turn, 0)


def close(c_ref, dx_ref, dy_ref, out_ref):
    cols = jnp.concatenate([dy_ref[0], jnp.zeros((N - 16, N), F32)], 0).T
    for e in range(ELEMENTS):
        out_ref[e, 0] = c_ref[e, 0] + dx_ref[0, e : e + 1] + cols[:, e : e + 1]


def solution(mesh):
    beams, dets = mesh.shape["beam"], mesh.shape["det"]

    def shards(conc, inc, sig, yld, rate, axis, m1, live1, m2, live2):
        step_x = 1.0 / (conc.shape[2] * beams)
        step_y = 1.0 / (conc.shape[3] * dets)

        def body(*refs):
            kernel(beams, dets, step_x, step_y, *refs)

        def exchange(count):
            def rows(slots):
                return pltpu.VMEM((3, slots, max(ROWS), N), F32)

            own = pltpu.VMEM((3, max(ROWS), N), F32)
            return [own, rows(count // AHEAD), rows(2), rows(AHEAD), pltpu.SemaphoreType.DMA((3, 2, 2))]

        field = (N, N)
        anywhere = pl.BlockSpec(memory_space=pl.ANY)
        vmem = pl.BlockSpec(memory_space=pltpu.VMEM)
        small = (axis[None], inc, sig, yld, rate[None], m1, live1, m2, live2)
        inner, dx, dy = pl.pallas_call(
            body,
            out_shape=[
                jax.ShapeDtypeStruct(conc.shape, F32),
                jax.ShapeDtypeStruct((ZS, 16, N), F32),
                jax.ShapeDtypeStruct((ZS, 16, N), F32),
            ],
            in_specs=[anywhere] * (len(small) + 1),
            out_specs=[anywhere, vmem, vmem],
            scratch_shapes=[
                *[pltpu.VMEM(a.shape, a.dtype) for a in small + (conc,)],
                pltpu.SemaphoreType.DMA((len(small),)),
                pltpu.SemaphoreType.DMA((ZS,)),
                pltpu.VMEM((ZS, LINES + 2, N, 2 * N), BF16),
                pltpu.VMEM((ZS, LINES) + field, F32),
                *[pltpu.VMEM((ZS, LINES + 1) + field, F32)] * 2,
                *[pltpu.VMEM((ZS, LINES) + field, F32)] * 3,
                *[pltpu.VMEM((ZS, LINES + 1, N, 2 * N), BF16)] * 2,
                pltpu.VMEM((ZS, LINES + 2) + field, F32),
                pltpu.VMEM(conc.shape, F32),
                pltpu.VMEM((16 * ZS, N), F32),
                *[pltpu.VMEM(field, F32)] * 2,
                *[pltpu.VMEM((LINES * ZS, N), F32)] * 4,
                *[pltpu.VMEM((16 * ZS, N), F32)] * 2,
                *[pltpu.VMEM((32, N), F32)] * 2,
                pltpu.VMEM((8 * FIELDS, 2 * N), BF16),
                pltpu.VMEM((16 * ELEMENTS, 8 * FIELDS), BF16),
                *[pltpu.VMEM((2 * N, N), BF16)] * 2,
                *[pltpu.VMEM((N, 2 * N), BF16)] * 2,
                *[pltpu.VMEM((16 * ZS, ELEMENTS * ZS), F32)] * 2,
                *[pltpu.VMEM((ELEMENTS * ZS, 16 * ZS), F32)] * 2,
                *exchange(beams),
                *exchange(dets),
            ],
            compiler_params=pltpu.CompilerParams(
                collective_id=0, has_side_effects=True, vmem_limit_bytes=64 * 1024 * 1024
            ),
        )(*small, conc)

        block = pl.BlockSpec((ELEMENTS, 1, N, N), lambda z: (0, z, 0, 0))
        return pl.pallas_call(
            close,
            out_shape=jax.ShapeDtypeStruct(conc.shape, F32),
            grid=(ZS,),
            in_specs=[
                block,
                pl.BlockSpec((1, 16, N), lambda z: (z, 0, 0)),
                pl.BlockSpec((1, 16, N), lambda z: (z, 0, 0)),
            ],
            out_specs=block,
            compiler_params=pltpu.CompilerParams(vmem_limit_bytes=64 * 1024 * 1024),
        )(inner, dx, dy)

    in_specs = (
        P(None, None, "beam", "det"),
        P(),
        P(),
        P(),
        P(),
        P(),
        P(None, None, "det"),
        P(None, "det"),
        P(None, None, "beam"),
        P(None, "beam"),
    )
    out_specs = P(None, None, "beam", "det")
    return jax.shard_map(shards, mesh=mesh, in_specs=in_specs, out_specs=out_specs, check_vma=False)
```

```python
import math

import jax
import jax.numpy as jnp
from jax import lax
from jax.experimental import pallas as pl
from jax.experimental.pallas import tpu as pltpu
from jax.sharding import PartitionSpec as P

STEPS = 2
HIGH = lax.Precision.HIGHEST
MESH = pl.DeviceIdType.MESH
F32 = jnp.float32
BF16 = jnp.bfloat16
ELEMENTS = 10
LINES = 12
ZS = 4
N = 128
PATHS = LINES + 1
FIELDS = 3 * PATHS + LINES
CHUNK = 64
AHEAD = 4
PARTS = 2 * LINES + 2
ROWS = (ELEMENTS * ZS, LINES * ZS, ELEMENTS * ZS)
LOG2E = math.log2(math.e)


def split(value):
    high = value.astype(BF16)
    return high, (value - high.astype(F32)).astype(BF16)


def iota(shape, dim):
    return lax.broadcasted_iota(jnp.int32, shape, dim)


def dot(a, b):
    return jnp.dot(a, b, preferred_element_type=F32)


def exact(a, b):
    return jnp.dot(a, b, preferred_element_type=F32, precision=HIGH)


def exact_nt(a, b):
    return lax.dot_general(
        a, b, (((1,), (1,)), ((), ())), preferred_element_type=F32, precision=HIGH
    )


def one_hot(condition):
    return jnp.where(condition, 1.0, 0.0).astype(F32)


class Ring:
    def __init__(self, axis, count, send, near, out, far, sems):
        self.axis, self.count = axis, count
        self.send, self.near, self.out, self.far, self.sems = send, near, out, far, sems
        self.slots = count // AHEAD
        self.cores = self.slots // 2
        me = lax.axis_index(axis)
        self.c = lax.rem(me, self.cores)
        self.x = lax.rem(me // self.cores, AHEAD)
        self.y = me // (self.cores * AHEAD)
        self.slot = self.y * self.cores + self.c

    def index(self, y, x, c):
        return (y * AHEAD + x) * self.cores + c

    def near_peers(self):
        slots = [lax.rem(self.slot + d, self.slots) for d in range(1, self.slots)]
        return [self.index(k // self.cores, self.x, lax.rem(k, self.cores)) for k in slots]

    def far_peers(self):
        return [(d, self.index(self.y, lax.rem(self.x + d, AHEAD), self.c)) for d in (2, 1, 3)]

    def greet(self, barrier):
        peers = self.near_peers() + [peer for _, peer in self.far_peers()]
        for peer in peers:
            pl.semaphore_signal(barrier, inc=1, device_id={self.axis: peer}, device_id_type=MESH)
        return len(peers)

    def copy(self, src, dst, phase, leg, peer):
        return pltpu.make_async_remote_copy(
            src_ref=src,
            dst_ref=dst,
            send_sem=self.sems.at[phase, leg, 0],
            recv_sem=self.sems.at[phase, leg, 1],
            device_id={self.axis: peer},
            device_id_type=MESH,
        )

    def start(self, phase):
        rows = pl.ds(0, ROWS[phase])
        self.near[phase, pl.ds(self.slot, 1), rows] = self.send[phase, rows][None]
        for peer in self.near_peers():
            self.copy(self.send.at[phase, rows], self.near.at[phase, self.slot, rows], phase, 0, peer).start()

    def wait(self, ref, phase, leg, count):
        some = ref.at[phase, pl.ds(0, count), pl.ds(0, ROWS[phase])]
        whole = self.copy(some, some, phase, leg, self.near_peers()[0])
        whole.wait_send()
        whole.wait_recv()

    def middle(self, phase, mode):
        rows = pl.ds(0, ROWS[phase])
        self.wait(self.near, phase, 0, self.slots - 1)
        have = [[self.near[phase, y * self.cores + c, rows] for c in range(self.cores)] for y in range(2)]
        sums = [sum(cores[1:], cores[0]) for cores in have]
        if mode == "sum":
            mine = sums[0] + sums[1]
            self.out[phase, 0, rows] = mine
        else:
            earlier = mode == "earlier"

            def chosen(other, own):
                return (other < own if earlier else other > own).astype(F32)

            base = sum(sums[y] * chosen(y, self.y) for y in range(2))
            same = sum(sums[y] * (self.y == y).astype(F32) for y in range(2))
            mine = base
            for y in range(2):
                for c in range(self.cores):
                    mine = mine + have[y][c] * ((self.y == y).astype(F32) * chosen(c, self.c))
            self.out[phase, 0, rows] = base
            self.out[phase, 1, rows] = base + same
        self.far[phase, pl.ds(self.x, 1), rows] = mine[None]
        for d, peer in self.far_peers():
            wrap = (self.x + d) // AHEAD
            which = {"sum": 0, "earlier": 1 - wrap, "later": wrap}[mode]
            self.copy(self.out.at[phase, which, rows], self.far.at[phase, self.x, rows], phase, 1, peer).start()

    def finish(self, phase):
        self.wait(self.far, phase, 1, AHEAD - 1)
        rows = pl.ds(0, ROWS[phase])
        return (self.far[phase, 0, rows] + self.far[phase, 1, rows]) + (
            self.far[phase, 2, rows] + self.far[phase, 3, rows]
        )

    def put(self, phase, row, value):
        self.send[phase, row : row + 1, :] = value


def kernel(
    beams, dets, step_x, step_y,
    axis_hbm, inc_hbm, sig_hbm, yld_hbm, rate_hbm, m1_hbm, live1_hbm, m2_hbm, live2_hbm, conc_hbm,
    out_hbm, dx_ref, dy_ref,
    axis_ref, inc_ref, sig_ref, yld_ref, rate_ref, m1_ref, live1_ref, m2_ref, live2_ref, c_ref,
    load_sems, conc_sems,
    m_ref, q_ref, e1_ref, e2_ref, a1_ref, a2_ref, w_ref, p1_ref, p2_ref, vx_ref, vy_ref, d_ref, rows_ref, cols_ref, acc_ref,
    mx_ref, my_ref, lx_ref, ly_ref,
    tx_ref, ty_ref, tab_ref, back_ref, mix_ref, unmix_ref, up_ref, down_ref, right_ref,
    wax_ref, way_ref, wcx_ref, wcy_ref,
    bsend, bnear, bout, bfar, bsems, dsend, dnear, dout, dfar, dsems,
):
    def conc_load(z):
        return pltpu.make_async_copy(conc_hbm.at[:, z], c_ref.at[:, z], conc_sems.at[z])

    hbm = (axis_hbm, inc_hbm, sig_hbm, yld_hbm, rate_hbm, m1_hbm, live1_hbm, m2_hbm, live2_hbm)
    vmem = (axis_ref, inc_ref, sig_ref, yld_ref, rate_ref, m1_ref, live1_ref, m2_ref, live2_ref)
    loads = [pltpu.make_async_copy(a, b, load_sems.at[k]) for k, (a, b) in enumerate(zip(hbm, vmem))]
    for load in [conc_load(z) for z in range(ZS)] + loads:
        load.start()
    beam = Ring("beam", beams, bsend, bnear, bout, bfar, bsems)
    det = Ring("det", dets, dsend, dnear, dout, dfar, dsems)
    barrier = pltpu.get_barrier_semaphore()
    greeted = det.greet(barrier) + beam.greet(barrier)

    for ref in (bsend, dsend, cols_ref, mx_ref, my_ref, lx_ref, ly_ref, tx_ref, ty_ref, tab_ref, back_ref):
        ref[...] = jnp.zeros(ref.shape, F32)

    lane = iota((CHUNK, N), 1)

    def over_z(body):
        for z in range(ZS):
            body(z)

    def sweep(body):
        sums = [None] * ZS
        for r in range(0, N, CHUNK):
            acc = jnp.zeros((CHUNK, N), F32)
            for z in range(ZS):
                new, acc = body(z, pl.ds(r, CHUNK), acc)
                new = [jnp.sum(a.reshape(CHUNK // 8, 8, N), 0) for a in new]
                sums[z] = new if r == 0 else [a + b for a, b in zip(sums[z], new)]
            acc_ref[pl.ds(r, CHUNK)] = acc
        return [[jnp.sum(a, 0, keepdims=True) for a in part] for part in sums]

    def turned(rows):
        return jnp.concatenate([rows, jnp.zeros((N - rows.shape[0], N), F32)], 0).T

    def totals(add):
        if add is not None:
            rows_ref[0 : ELEMENTS * ZS] = add

        def body(z, rows, acc):
            if add is None and rows.start == 0:
                conc_load(z).wait()
            sums = []
            cols = cols_ref[rows]
            for e in range(ELEMENTS):
                k = ELEMENTS * z + e
                if add is None:
                    c = c_ref[e, z, rows]
                else:
                    c = d_ref[e, z, rows] + rows_ref[k : k + 1] + cols[:, k : k + 1]
                    c_ref[e, z, rows] = c
                sums.append(c)
                acc = jnp.where(lane == k, jnp.sum(c, 1, keepdims=True), acc)
            return sums, acc

        for z, sums in enumerate(sweep(body)):
            for e, row in enumerate(sums):
                beam.put(0, ELEMENTS * z + e, row)
        dsend[0, 0 : ELEMENTS * ZS] = acc_ref[...].T[0 : ELEMENTS * ZS]

    totals(None)
    pl.semaphore_wait(barrier, greeted)
    det.start(0)
    beam.start(0)
    for load in loads:
        load.wait()

    def tables():
        first = axis_ref[0:1, 0:1] == 0
        one, two = inc_ref[0:1, :], inc_ref[1:2, :]
        s1 = jnp.where(first, one, two)
        s2 = jnp.where(first, two, one)
        scale = -LOG2E * step_y
        sig, yld, rate = sig_ref[...], yld_ref[...], rate_ref[...]
        cols = pl.ds(0, ELEMENTS)
        tab_ref[0:LINES, cols] = scale * sig
        tab_ref[LINES:PATHS, cols] = scale * s2
        for k in (PATHS, 2 * PATHS):
            tab_ref[k : k + LINES, cols] = -LOG2E * step_x * sig
            tab_ref[k + LINES : k + PATHS, cols] = -LOG2E * step_x * s1
        tab_ref[3 * PATHS : FIELDS, cols] = yld
        back_ref[0:LINES, cols] = yld * rate
        back_ref[LINES : 2 * LINES, cols] = -sig * rate
        back_ref[2 * LINES : 2 * LINES + 1, cols] = -s1 * rate
        back_ref[2 * LINES + 1 : 2 * LINES + 2, cols] = -s2 * rate

        tab, back = tab_ref[...], back_ref[...]
        wide = 8 * ELEMENTS
        pick = one_hot((iota((8 * FIELDS, 64), 0) >> 3) == iota((8 * FIELDS, 64), 1))
        col = iota((N, 256), 1)
        part = (col >= wide).astype(jnp.int32) + (col >= 2 * wide).astype(jnp.int32)
        spread = one_hot(((col - wide * part) >> 3) == iota((N, 256), 0))
        spread = jnp.where(col < 3 * wide, spread, 0.0)
        full = exact(pick, exact(tab, spread))
        shape = (8 * FIELDS, 256)
        field, gap = iota(shape, 0) >> 3, (iota(shape, 0) & 7) - (iota(shape, 1) & 7)
        within = (field >= PATHS) & (field < 2 * PATHS)
        whole = (field >= 2 * PATHS) & (field < 3 * PATHS)
        full = jnp.where(whole | (within & (gap > 0)) | ((gap == 0) & jnp.logical_not(within)), full, 0.0)
        high, low = split(full)
        part = iota(shape, 1)
        mix_ref[...] = jnp.where((part >= wide) & (part < 2 * wide), low.astype(F32), high.astype(F32)).astype(BF16)

        pick = one_hot((iota((wide, N), 0) >> 3) == iota((wide, N), 1))
        shape = (wide, 8 * PARTS)
        spread = one_hot((iota((32, 8 * PARTS), 1) >> 3) == iota((32, 8 * PARTS), 0))
        full = exact(exact_nt(pick, back), spread)
        full = jnp.where((iota(shape, 0) & 7) == (iota(shape, 1) & 7), full, 0.0)
        high, low = split(full)
        unmix_ref[0:wide] = high
        unmix_ref[wide : 2 * wide] = low

        r, m = iota((16 * ZS, 64), 0) & 15, iota((16 * ZS, 64), 1)
        rates_x = exact(one_hot((r < PATHS) & (m == r + PATHS)), tab)
        rates_y = exact(one_hot((r < PATHS) & (m == r)), tab)
        r, m = iota((16 * ZS, 32), 0) & 15, iota((16 * ZS, 32), 1)
        sums_x = exact(one_hot(m == jnp.where(r < LINES, r + LINES, 2 * LINES)), back)
        sums_y = exact(one_hot(m == jnp.where(r < LINES, r + LINES, 2 * LINES + 1)), back)
        r = iota((16 * ZS, N), 0) & 15
        sums_x = jnp.where(r <= LINES, -step_x * sums_x, 0.0)
        sums_y = jnp.where(r <= LINES, -step_y * sums_y, 0.0)

        def slice_of(shape, dim):
            row = iota(shape, dim)
            return sum((row >= ELEMENTS * z).astype(jnp.int32) for z in range(1, ZS))

        shape = (ELEMENTS * ZS, N)
        place = one_hot(iota(shape, 0) - ELEMENTS * slice_of(shape, 0) == iota(shape, 1))
        shape = wax_ref.shape
        same = (iota(shape, 0) >> 4) == slice_of(shape, 1)
        wax_ref[...] = jnp.where(same, exact_nt(rates_x, place), 0.0)
        way_ref[...] = jnp.where(same, exact_nt(rates_y, place), 0.0)
        shape = wcx_ref.shape
        same = slice_of(shape, 0) == (iota(shape, 1) >> 4)
        wcx_ref[...] = jnp.where(same, exact_nt(place, sums_x), 0.0)
        wcy_ref[...] = jnp.where(same, exact_nt(place, sums_y), 0.0)

        r, c = iota((2 * N, N), 0) & (N - 1), iota((2 * N, N), 1)
        up_ref[...] = one_hot(r < c).astype(BF16)
        down_ref[...] = (step_y * one_hot(r > c)).astype(BF16)
        r, c = iota((N, 2 * N), 0), iota((N, 2 * N), 1) & (N - 1)
        right_ref[...] = (step_x * one_hot(c > r)).astype(BF16)
        for z in range(ZS):
            live1 = live1_ref[z : z + 1, :].astype(F32)
            live2 = live2_ref[z : z + 1, :].astype(F32)
            for l in range(LINES):
                k = LINES * z + l
                lx_ref[k : k + 1, :] = live1
                ly_ref[k : k + 1, :] = live2
                mx_ref[k : k + 1, :] = m1_ref[l, z : z + 1, :]
                my_ref[k : k + 1, :] = m2_ref[l, z : z + 1, :]

    tables()

    def mix(z):
        run = [jnp.zeros((8, N), F32)] * PATHS
        for r0 in range(0, N, 16):
            parts = []
            for b in range(2):
                high, low = split(c_ref[:, z, pl.ds(r0 + 8 * b, 8), :].reshape(8 * ELEMENTS, N))
                parts.append(jnp.concatenate([high, high, low, jnp.zeros((16, N), BF16)], 0))
            out = dot(mix_ref[...], jnp.concatenate(parts, 1))

            def field(f):
                return [out[8 * f : 8 * f + 8, b * N : (b + 1) * N] for b in range(2)]

            rows = pl.ds(r0, 16)
            for l in range(PATHS):
                high, low = split(jnp.concatenate(field(l), 0))
                m_ref[z, l, rows, 0:N] = high
                m_ref[z, l, rows, N : 2 * N] = low
                within, whole = field(PATHS + l), field(2 * PATHS + l)
                for b in range(2):
                    e2_ref[z, l, pl.ds(r0 + 8 * b, 8)] = run[l] + within[b]
                    run[l] = run[l] + whole[b]
            for l in range(LINES):
                q_ref[z, l, rows, :] = jnp.concatenate(field(3 * PATHS + l), 0)

    def unmix(z):
        wide = 8 * ELEMENTS
        for r0 in range(0, N, 16):
            highs, lows = [], []
            for b in range(2):
                rows = pl.ds(r0 + 8 * b, 8)
                w = w_ref[z, :, rows, :].reshape(8 * LINES, N)
                along_x, along_y = vx_ref[z, :, rows, :], vy_ref[z, :, rows, :]
                both = (along_x[0:LINES] + along_y[0:LINES]).reshape(8 * LINES, N)
                high, low = split(jnp.concatenate([w, both, along_x[LINES], along_y[LINES]], 0))
                highs.append(high)
                lows.append(low)
            one = dot(unmix_ref[...], jnp.concatenate(highs, 1))
            two = dot(unmix_ref[0:wide], jnp.concatenate(lows, 1))
            out = one[0:wide] + (one[wide:] + two)
            for b in range(2):
                rows = pl.ds(r0 + 8 * b, 8)
                new = c_ref[:, z, rows, :] - out[:, b * N : (b + 1) * N].reshape(ELEMENTS, 8, N)
                d_ref[:, z, rows, :] = new

    def stacked(ref, z, fields):
        value = [ref[z, f] for f in fields]
        high = jnp.concatenate([v[:, 0:N] for v in value], 1)
        low = jnp.concatenate([v[:, N : 2 * N] for v in value], 1)
        return jnp.concatenate([high, low], 0)

    def prefixes(z):
        e1_ref[z] = dot(m_ref[z].reshape(PATHS * N, 2 * N), up_ref[...]).reshape(PATHS, N, N)

    def suffixes(z):
        vy_ref[z] = dot(p1_ref[z].reshape(PATHS * N, 2 * N), down_ref[...]).reshape(PATHS, N, N)
        for l in range(0, LINES, 2):
            over_x = dot(right_ref[...], stacked(p2_ref, z, (l, l + 1)))
            vx_ref[z, l] = over_x[:, 0:N]
            vx_ref[z, l + 1] = over_x[:, N : 2 * N]
        vx_ref[z, LINES] = dot(right_ref[...], stacked(p2_ref, z, (LINES,)))

    def counts(enter_x, enter_y):
        rows_ref[...] = exact(wax_ref[...], enter_x)
        cols_ref[...] = turned(exact(way_ref[...], enter_y))

        def body(z, rows, acc):
            cols = cols_ref[rows]
            k = 16 * z + LINES
            tin1 = jnp.exp2(e2_ref[z, LINES, rows] + rows_ref[k : k + 1])
            tin2 = jnp.exp2(e1_ref[z, LINES, rows] + cols[:, k : k + 1])
            sums = []
            for l in range(LINES):
                k = 16 * z + l
                a1 = tin1 * jnp.exp2(e1_ref[z, l, rows] + cols[:, k : k + 1])
                a2 = tin2 * jnp.exp2(e2_ref[z, l, rows] + rows_ref[k : k + 1])
                a1_ref[z, l, rows] = a1
                a2_ref[z, l, rows] = a2
                q = q_ref[z, l, rows]
                sums.append(q * a1)
                acc = jnp.where(lane == LINES * z + l, jnp.sum(q * a2, 1, keepdims=True), acc)
            return sums, acc

        for z, sums in enumerate(sweep(body)):
            for l, row in enumerate(sums):
                beam.put(1, LINES * z + l, step_x * row)
        dsend[1] = step_y * acc_ref[...].T[0 : LINES * ZS]

    def residuals(pred1, pred2):
        res1 = lx_ref[...] * (pred1 - mx_ref[...])
        res2 = ly_ref[...] * (pred2 - my_ref[...])
        sum1 = res1 * bsend[1] / step_x
        sum2 = res2 * dsend[1] / step_y
        rows_ref[0 : LINES * ZS] = res1
        cols_ref[...] = turned(res2)

        def body(z, rows, acc):
            cols = cols_ref[rows]
            sums = []
            all1 = jnp.zeros((CHUNK, N), F32)
            all2 = jnp.zeros((CHUNK, N), F32)

            def keep(ref, f, value):
                high, low = split(value)
                ref[z, f, rows, 0:N] = high
                ref[z, f, rows, N : 2 * N] = low

            for l in range(LINES):
                k = LINES * z + l
                w1 = a1_ref[z, l, rows] * rows_ref[k : k + 1]
                w2 = a2_ref[z, l, rows] * cols[:, k : k + 1]
                w_ref[z, l, rows] = w1 + w2
                q = q_ref[z, l, rows]
                p1, p2 = q * w1, q * w2
                all1, all2 = all1 + p1, all2 + p2
                sums.append(p2)
                acc = jnp.where(lane == 16 * z + l, jnp.sum(p1, 1, keepdims=True), acc)
                keep(p1_ref, l, p1)
                keep(p2_ref, l, p2)
            keep(p1_ref, LINES, all2)
            keep(p2_ref, LINES, all1)
            return sums, acc

        for z, sums in enumerate(sweep(body)):
            for l, row in enumerate(sums):
                tx_ref[16 * z + l : 16 * z + l + 1] = row
        ty_ref[...] = acc_ref[...].T[0 : 16 * ZS]
        for z in range(ZS):
            k, part = 16 * z + LINES, slice(LINES * z, LINES * (z + 1))
            tx_ref[k : k + 1] = jnp.sum(sum1[part], 0, keepdims=True)
            ty_ref[k : k + 1] = jnp.sum(sum2[part], 0, keepdims=True)
        bsend[2, 0 : ELEMENTS * ZS] = exact(wcx_ref[...], tx_ref[...])
        dsend[2, 0 : ELEMENTS * ZS] = exact(wcy_ref[...], ty_ref[...])

    def turn(step, carry):
        last = step == STEPS - 1
        over_z(mix)
        det.middle(0, "earlier")
        beam.middle(0, "earlier")
        over_z(prefixes)
        enter_y = det.finish(0)
        enter_x = beam.finish(0)
        counts(enter_x, enter_y)
        det.start(1)
        beam.start(1)
        det.middle(1, "sum")
        beam.middle(1, "sum")
        pred2 = det.finish(1)
        pred1 = beam.finish(1)
        residuals(pred1, pred2)
        det.start(2)
        beam.start(2)
        over_z(suffixes)
        det.middle(2, "later")
        beam.middle(2, "later")
        over_z(unmix)

        def stores():
            return [pltpu.make_async_copy(d_ref.at[:, z], out_hbm.at[:, z], conc_sems.at[z]) for z in range(ZS)]

        @pl.when(last)
        def leave():
            for store in stores():
                store.start()

        after_y = det.finish(2)
        after_x = beam.finish(2)

        @pl.when(last)
        def left():
            for z in range(ZS):
                part = slice(ELEMENTS * z, ELEMENTS * (z + 1))
                dx_ref[z, 0:ELEMENTS] = after_x[part]
                dy_ref[z, 0:ELEMENTS] = after_y[part]
            for store in stores():
                store.wait()

        @pl.when(jnp.logical_not(last))
        def go_on():
            cols_ref[...] = turned(after_y)
            totals(after_x)
            det.start(0)
            beam.start(0)

        return carry

    lax.fori_loop(0, STEPS, turn, 0)


def close(c_hbm, dx_hbm, dy_hbm, out_hbm, c_ref, dx_ref, dy_ref, sems):
    loads = [pltpu.make_async_copy(a, b, sems.at[k]) for k, (a, b) in enumerate(((dx_hbm, dx_ref), (dy_hbm, dy_ref)))]
    loads += [pltpu.make_async_copy(c_hbm.at[:, z], c_ref.at[:, z], sems.at[2 + z]) for z in range(ZS)]
    for load in loads:
        load.start()
    loads[0].wait()
    loads[1].wait()
    stores = []
    for z in range(ZS):
        cols = jnp.concatenate([dy_ref[z], jnp.zeros((N - 16, N), F32)], 0).T
        loads[2 + z].wait()
        for e in range(ELEMENTS):
            c_ref[e, z] = c_ref[e, z] + dx_ref[z, e : e + 1] + cols[:, e : e + 1]
        stores.append(pltpu.make_async_copy(c_ref.at[:, z], out_hbm.at[:, z], sems.at[2 + z]))
        stores[z].start()
    for store in stores:
        store.wait()


def solution(mesh):
    beams, dets = mesh.shape["beam"], mesh.shape["det"]

    def shards(conc, inc, sig, yld, rate, axis, m1, live1, m2, live2):
        step_x = 1.0 / (conc.shape[2] * beams)
        step_y = 1.0 / (conc.shape[3] * dets)

        def body(*refs):
            kernel(beams, dets, step_x, step_y, *refs)

        def exchange(count):
            def rows(slots):
                return pltpu.VMEM((3, slots, max(ROWS), N), F32)

            own = pltpu.VMEM((3, max(ROWS), N), F32)
            return [own, rows(count // AHEAD), rows(2), rows(AHEAD), pltpu.SemaphoreType.DMA((3, 2, 2))]

        field = (N, N)
        anywhere = pl.BlockSpec(memory_space=pl.ANY)
        vmem = pl.BlockSpec(memory_space=pltpu.VMEM)
        small = (axis[None], inc, sig, yld, rate[None], m1, live1, m2, live2)
        inner, dx, dy = pl.pallas_call(
            body,
            out_shape=[
                jax.ShapeDtypeStruct(conc.shape, F32),
                jax.ShapeDtypeStruct((ZS, 16, N), F32),
                jax.ShapeDtypeStruct((ZS, 16, N), F32),
            ],
            in_specs=[anywhere] * (len(small) + 1),
            out_specs=[anywhere, vmem, vmem],
            scratch_shapes=[
                *[pltpu.VMEM(a.shape, a.dtype) for a in small + (conc,)],
                pltpu.SemaphoreType.DMA((len(small),)),
                pltpu.SemaphoreType.DMA((ZS,)),
                pltpu.VMEM((ZS, PATHS, N, 2 * N), BF16),
                pltpu.VMEM((ZS, LINES) + field, F32),
                *[pltpu.VMEM((ZS, LINES + 1) + field, F32)] * 2,
                *[pltpu.VMEM((ZS, LINES) + field, F32)] * 3,
                *[pltpu.VMEM((ZS, LINES + 1, N, 2 * N), BF16)] * 2,
                *[pltpu.VMEM((ZS, PATHS) + field, F32)] * 2,
                pltpu.VMEM(conc.shape, F32),
                pltpu.VMEM((16 * ZS, N), F32),
                *[pltpu.VMEM(field, F32)] * 2,
                *[pltpu.VMEM((LINES * ZS, N), F32)] * 4,
                *[pltpu.VMEM((16 * ZS, N), F32)] * 2,
                pltpu.VMEM((64, N), F32),
                pltpu.VMEM((32, N), F32),
                pltpu.VMEM((8 * FIELDS, 2 * N), BF16),
                pltpu.VMEM((16 * ELEMENTS, 8 * PARTS), BF16),
                *[pltpu.VMEM((2 * N, N), BF16)] * 2,
                pltpu.VMEM((N, 2 * N), BF16),
                *[pltpu.VMEM((16 * ZS, ELEMENTS * ZS), F32)] * 2,
                *[pltpu.VMEM((ELEMENTS * ZS, 16 * ZS), F32)] * 2,
                *exchange(beams),
                *exchange(dets),
            ],
            compiler_params=pltpu.CompilerParams(
                collective_id=0, has_side_effects=True, vmem_limit_bytes=64 * 1024 * 1024
            ),
        )(*small, conc)

        return pl.pallas_call(
            close,
            out_shape=jax.ShapeDtypeStruct(conc.shape, F32),
            in_specs=[anywhere] * 3,
            out_specs=anywhere,
            scratch_shapes=[
                pltpu.VMEM(conc.shape, F32),
                *[pltpu.VMEM((ZS, 16, N), F32)] * 2,
                pltpu.SemaphoreType.DMA((2 + ZS,)),
            ],
            compiler_params=pltpu.CompilerParams(vmem_limit_bytes=64 * 1024 * 1024),
        )(inner, dx, dy)

    in_specs = (
        P(None, None, "beam", "det"),
        P(),
        P(),
        P(),
        P(),
        P(),
        P(None, None, "det"),
        P(None, "det"),
        P(None, None, "beam"),
        P(None, "beam"),
    )
    out_specs = P(None, None, "beam", "det")
    return jax.shard_map(shards, mesh=mesh, in_specs=in_specs, out_specs=out_specs, check_vma=False)
```

```python
import math

import jax
import jax.numpy as jnp
from jax import lax
from jax.experimental import pallas as pl
from jax.experimental.pallas import tpu as pltpu
from jax.sharding import PartitionSpec as P

STEPS = 2
HIGH = lax.Precision.HIGHEST
MESH = pl.DeviceIdType.MESH
F32 = jnp.float32
BF16 = jnp.bfloat16
ELEMENTS = 10
LINES = 12
ZS = 4
N = 128
PATHS = LINES + 1
FIELDS = 3 * PATHS + LINES
CHUNK = 64
AHEAD = 4
PARTS = 2 * LINES + 2
ROWS = (ELEMENTS * ZS, LINES * ZS, ELEMENTS * ZS)
LOG2E = math.log2(math.e)


def split(value):
    high = value.astype(BF16)
    return high, (value - high.astype(F32)).astype(BF16)


def iota(shape, dim):
    return lax.broadcasted_iota(jnp.int32, shape, dim)


def dot(a, b):
    return jnp.dot(a, b, preferred_element_type=F32)


def exact(a, b):
    return jnp.dot(a, b, preferred_element_type=F32, precision=HIGH)


def exact_nt(a, b):
    return lax.dot_general(
        a, b, (((1,), (1,)), ((), ())), preferred_element_type=F32, precision=HIGH
    )


def triple(table):
    high, low = split(table)
    return jnp.concatenate([high, high, low], 1)


def rows_of(value):
    high, low = split(jnp.concatenate([value, jnp.zeros((-value.shape[0] % 128, value.shape[1]), F32)], 0))
    return jnp.concatenate([high, low, high], 0)


def one_hot(condition):
    return jnp.where(condition, 1.0, 0.0).astype(F32)


class Ring:
    def __init__(self, axis, count, send, near, out, far, sems):
        self.axis, self.count = axis, count
        self.send, self.near, self.out, self.far, self.sems = send, near, out, far, sems
        self.slots = count // AHEAD
        self.cores = self.slots // 2
        me = lax.axis_index(axis)
        self.c = lax.rem(me, self.cores)
        self.x = lax.rem(me // self.cores, AHEAD)
        self.y = me // (self.cores * AHEAD)
        self.slot = self.y * self.cores + self.c

    def index(self, y, x, c):
        return (y * AHEAD + x) * self.cores + c

    def near_peers(self):
        slots = [lax.rem(self.slot + d, self.slots) for d in range(1, self.slots)]
        return [self.index(k // self.cores, self.x, lax.rem(k, self.cores)) for k in slots]

    def far_peers(self):
        return [(d, self.index(self.y, lax.rem(self.x + d, AHEAD), self.c)) for d in (2, 1, 3)]

    def greet(self, barrier):
        peers = self.near_peers() + [peer for _, peer in self.far_peers()]
        for peer in peers:
            pl.semaphore_signal(barrier, inc=1, device_id={self.axis: peer}, device_id_type=MESH)
        return len(peers)

    def copy(self, src, dst, phase, leg, peer):
        return pltpu.make_async_remote_copy(
            src_ref=src,
            dst_ref=dst,
            send_sem=self.sems.at[phase, leg, 0],
            recv_sem=self.sems.at[phase, leg, 1],
            device_id={self.axis: peer},
            device_id_type=MESH,
        )

    def start(self, phase):
        rows = pl.ds(0, ROWS[phase])
        self.near[phase, pl.ds(self.slot, 1), rows] = self.send[phase, rows][None]
        for peer in self.near_peers():
            self.copy(self.send.at[phase, rows], self.near.at[phase, self.slot, rows], phase, 0, peer).start()

    def wait(self, ref, phase, leg, count):
        some = ref.at[phase, pl.ds(0, count), pl.ds(0, ROWS[phase])]
        whole = self.copy(some, some, phase, leg, self.near_peers()[0])
        whole.wait_send()
        whole.wait_recv()

    def middle(self, phase, mode):
        rows = pl.ds(0, ROWS[phase])
        self.wait(self.near, phase, 0, self.slots - 1)
        have = [[self.near[phase, y * self.cores + c, rows] for c in range(self.cores)] for y in range(2)]
        sums = [sum(cores[1:], cores[0]) for cores in have]
        if mode == "sum":
            mine = sums[0] + sums[1]
            self.out[phase, 0, rows] = mine
        else:
            earlier = mode == "earlier"

            def chosen(other, own):
                return (other < own if earlier else other > own).astype(F32)

            base = sum(sums[y] * chosen(y, self.y) for y in range(2))
            same = sum(sums[y] * (self.y == y).astype(F32) for y in range(2))
            mine = base
            for y in range(2):
                for c in range(self.cores):
                    mine = mine + have[y][c] * ((self.y == y).astype(F32) * chosen(c, self.c))
            self.out[phase, 0, rows] = base
            self.out[phase, 1, rows] = base + same
        self.far[phase, pl.ds(self.x, 1), rows] = mine[None]
        for d, peer in self.far_peers():
            wrap = (self.x + d) // AHEAD
            which = {"sum": 0, "earlier": 1 - wrap, "later": wrap}[mode]
            self.copy(self.out.at[phase, which, rows], self.far.at[phase, self.x, rows], phase, 1, peer).start()

    def finish(self, phase):
        self.wait(self.far, phase, 1, AHEAD - 1)
        rows = pl.ds(0, ROWS[phase])
        return (self.far[phase, 0, rows] + self.far[phase, 1, rows]) + (
            self.far[phase, 2, rows] + self.far[phase, 3, rows]
        )

    def put(self, phase, row, value):
        self.send[phase, row : row + 1, :] = value


def kernel(
    beams, dets, step_x, step_y,
    axis_hbm, inc_hbm, sig_hbm, yld_hbm, rate_hbm, m1_hbm, live1_hbm, m2_hbm, live2_hbm, conc_hbm,
    out_hbm, dx_ref, dy_ref,
    axis_ref, inc_ref, sig_ref, yld_ref, rate_ref, m1_ref, live1_ref, m2_ref, live2_ref, c_ref,
    load_sems, conc_sems,
    m_ref, q_ref, e1_ref, e2_ref, a1_ref, a2_ref, w_ref, p1_ref, p2_ref, vx_ref, vy_ref, d_ref, rows_ref, cols_ref, acc_ref,
    mx_ref, my_ref, lx_ref, ly_ref,
    tx_ref, ty_ref, tab_ref, back_ref, mix_ref, unmix_ref, up_ref, down_ref, right_ref,
    wax_ref, way_ref, wcx_ref, wcy_ref,
    bsend, bnear, bout, bfar, bsems, dsend, dnear, dout, dfar, dsems,
):
    def conc_load(z):
        return pltpu.make_async_copy(conc_hbm.at[:, z], c_ref.at[:, z], conc_sems.at[z])

    hbm = (axis_hbm, inc_hbm, sig_hbm, yld_hbm, rate_hbm, m1_hbm, live1_hbm, m2_hbm, live2_hbm)
    vmem = (axis_ref, inc_ref, sig_ref, yld_ref, rate_ref, m1_ref, live1_ref, m2_ref, live2_ref)
    loads = [pltpu.make_async_copy(a, b, load_sems.at[k]) for k, (a, b) in enumerate(zip(hbm, vmem))]
    for load in [conc_load(z) for z in range(ZS)] + loads:
        load.start()
    beam = Ring("beam", beams, bsend, bnear, bout, bfar, bsems)
    det = Ring("det", dets, dsend, dnear, dout, dfar, dsems)
    barrier = pltpu.get_barrier_semaphore()
    greeted = det.greet(barrier) + beam.greet(barrier)

    for ref in (bsend, dsend, cols_ref, mx_ref, my_ref, lx_ref, ly_ref, tx_ref, ty_ref, tab_ref, back_ref):
        ref[...] = jnp.zeros(ref.shape, F32)

    lane = iota((CHUNK, N), 1)

    def over_z(body):
        for z in range(ZS):
            body(z)

    def sweep(body):
        sums = [None] * ZS
        for r in range(0, N, CHUNK):
            acc = jnp.zeros((CHUNK, N), F32)
            for z in range(ZS):
                new, acc = body(z, pl.ds(r, CHUNK), acc)
                new = [jnp.sum(a.reshape(CHUNK // 8, 8, N), 0) for a in new]
                sums[z] = new if r == 0 else [a + b for a, b in zip(sums[z], new)]
            acc_ref[pl.ds(r, CHUNK)] = acc
        return [[jnp.sum(a, 0, keepdims=True) for a in part] for part in sums]

    def turned(rows):
        return jnp.concatenate([rows, jnp.zeros((N - rows.shape[0], N), F32)], 0).T

    def totals(add):
        if add is not None:
            rows_ref[0 : ELEMENTS * ZS] = add

        def body(z, rows, acc):
            if add is None and rows.start == 0:
                conc_load(z).wait()
            sums = []
            cols = cols_ref[rows]
            for e in range(ELEMENTS):
                k = ELEMENTS * z + e
                if add is None:
                    c = c_ref[e, z, rows]
                else:
                    c = d_ref[e, z, rows] + rows_ref[k : k + 1] + cols[:, k : k + 1]
                    c_ref[e, z, rows] = c
                sums.append(c)
                acc = jnp.where(lane == k, jnp.sum(c, 1, keepdims=True), acc)
            return sums, acc

        for z, sums in enumerate(sweep(body)):
            for e, row in enumerate(sums):
                beam.put(0, ELEMENTS * z + e, row)
        dsend[0, 0 : ELEMENTS * ZS] = acc_ref[...].T[0 : ELEMENTS * ZS]

    totals(None)
    pl.semaphore_wait(barrier, greeted)
    det.start(0)
    beam.start(0)
    for load in loads:
        load.wait()

    def tables():
        first = axis_ref[0:1, 0:1] == 0
        one, two = inc_ref[0:1, :], inc_ref[1:2, :]
        s1 = jnp.where(first, one, two)
        s2 = jnp.where(first, two, one)
        scale = -LOG2E * step_y
        sig, yld, rate = sig_ref[...], yld_ref[...], rate_ref[...]
        cols = pl.ds(0, ELEMENTS)
        tab_ref[0:LINES, cols] = scale * sig
        tab_ref[LINES:PATHS, cols] = scale * s2
        for k in (PATHS, 2 * PATHS):
            tab_ref[k : k + LINES, cols] = -LOG2E * step_x * sig
            tab_ref[k + LINES : k + PATHS, cols] = -LOG2E * step_x * s1
        tab_ref[3 * PATHS : FIELDS, cols] = yld
        back_ref[0:LINES, cols] = yld * rate
        back_ref[LINES : 2 * LINES, cols] = -sig * rate
        back_ref[2 * LINES : 2 * LINES + 1, cols] = -s1 * rate
        back_ref[2 * LINES + 1 : 2 * LINES + 2, cols] = -s2 * rate

        tab, back = tab_ref[...], back_ref[...]
        wide = 8 * ELEMENTS
        pick = one_hot((iota((8 * FIELDS, 64), 0) >> 3) == iota((8 * FIELDS, 64), 1))
        col = iota((N, 256), 1)
        part = (col >= wide).astype(jnp.int32) + (col >= 2 * wide).astype(jnp.int32)
        spread = one_hot(((col - wide * part) >> 3) == iota((N, 256), 0))
        spread = jnp.where(col < 3 * wide, spread, 0.0)
        full = exact(pick, exact(tab, spread))
        shape = (8 * FIELDS, 256)
        field, gap = iota(shape, 0) >> 3, (iota(shape, 0) & 7) - (iota(shape, 1) & 7)
        within = (field >= PATHS) & (field < 2 * PATHS)
        whole = (field >= 2 * PATHS) & (field < 3 * PATHS)
        full = jnp.where(whole | (within & (gap > 0)) | ((gap == 0) & jnp.logical_not(within)), full, 0.0)
        high, low = split(full)
        part = iota(shape, 1)
        mix_ref[...] = jnp.where((part >= wide) & (part < 2 * wide), low.astype(F32), high.astype(F32)).astype(BF16)

        pick = one_hot((iota((wide, N), 0) >> 3) == iota((wide, N), 1))
        shape = (wide, 8 * PARTS)
        spread = one_hot((iota((32, 8 * PARTS), 1) >> 3) == iota((32, 8 * PARTS), 0))
        full = exact(exact_nt(pick, back), spread)
        full = jnp.where((iota(shape, 0) & 7) == (iota(shape, 1) & 7), full, 0.0)
        high, low = split(full)
        unmix_ref[0:wide] = high
        unmix_ref[wide : 2 * wide] = low

        r, m = iota((16 * ZS, 64), 0) & 15, iota((16 * ZS, 64), 1)
        rates_x = exact(one_hot((r < PATHS) & (m == r + PATHS)), tab)
        rates_y = exact(one_hot((r < PATHS) & (m == r)), tab)
        r, m = iota((16 * ZS, 32), 0) & 15, iota((16 * ZS, 32), 1)
        sums_x = exact(one_hot(m == jnp.where(r < LINES, r + LINES, 2 * LINES)), back)
        sums_y = exact(one_hot(m == jnp.where(r < LINES, r + LINES, 2 * LINES + 1)), back)
        r = iota((16 * ZS, N), 0) & 15
        sums_x = jnp.where(r <= LINES, -step_x * sums_x, 0.0)
        sums_y = jnp.where(r <= LINES, -step_y * sums_y, 0.0)

        def slice_of(shape, dim):
            row = iota(shape, dim)
            return sum((row >= ELEMENTS * z).astype(jnp.int32) for z in range(1, ZS))

        shape = (N, N)
        place = one_hot((iota(shape, 0) - ELEMENTS * slice_of(shape, 0) == iota(shape, 1)) & (iota(shape, 1) < ELEMENTS))
        shape = (16 * ZS, N)
        same = (iota(shape, 0) >> 4) == slice_of(shape, 1)
        wax_ref[...] = triple(jnp.where(same, exact_nt(rates_x, place), 0.0))
        way_ref[...] = triple(jnp.where(same, exact_nt(rates_y, place), 0.0))
        shape = (LINES * ZS, N)
        same = slice_of(shape, 0) == (iota(shape, 1) >> 4)
        fill = jnp.zeros((N - 16 * ZS, N), F32)
        for ref, sums in ((wcx_ref, sums_x), (wcy_ref, sums_y)):
            ref[0 : LINES * ZS] = triple(
                jnp.where(same, exact_nt(place[0 : LINES * ZS], jnp.concatenate([sums, fill], 0)), 0.0)
            )

        r, c = iota((2 * N, N), 0) & (N - 1), iota((2 * N, N), 1)
        up_ref[...] = one_hot(r < c).astype(BF16)
        down_ref[...] = (step_y * one_hot(r > c)).astype(BF16)
        r, c = iota((N, 2 * N), 0), iota((N, 2 * N), 1) & (N - 1)
        right_ref[...] = (step_x * one_hot(c > r)).astype(BF16)
        for z in range(ZS):
            live1 = live1_ref[z : z + 1, :].astype(F32)
            live2 = live2_ref[z : z + 1, :].astype(F32)
            for l in range(LINES):
                k = LINES * z + l
                lx_ref[k : k + 1, :] = live1
                ly_ref[k : k + 1, :] = live2
                mx_ref[k : k + 1, :] = m1_ref[l, z : z + 1, :]
                my_ref[k : k + 1, :] = m2_ref[l, z : z + 1, :]

    tables()
    det.middle(0, "earlier")
    beam.middle(0, "earlier")

    def mix(z):
        run = [jnp.zeros((8, N), F32)] * PATHS
        for r0 in range(0, N, 16):
            parts = []
            for b in range(2):
                high, low = split(c_ref[:, z, pl.ds(r0 + 8 * b, 8), :].reshape(8 * ELEMENTS, N))
                parts.append(jnp.concatenate([high, high, low, jnp.zeros((16, N), BF16)], 0))
            out = dot(mix_ref[...], jnp.concatenate(parts, 1))

            def field(f):
                return [out[8 * f : 8 * f + 8, b * N : (b + 1) * N] for b in range(2)]

            rows = pl.ds(r0, 16)
            for l in range(PATHS):
                high, low = split(jnp.concatenate(field(l), 0))
                m_ref[z, l, rows, 0:N] = high
                m_ref[z, l, rows, N : 2 * N] = low
                within, whole = field(PATHS + l), field(2 * PATHS + l)
                for b in range(2):
                    e2_ref[z, l, pl.ds(r0 + 8 * b, 8)] = run[l] + within[b]
                    run[l] = run[l] + whole[b]
            for l in range(LINES):
                q_ref[z, l, rows, :] = jnp.concatenate(field(3 * PATHS + l), 0)

    def unmix(z):
        wide = 8 * ELEMENTS
        for r0 in range(0, N, 16):
            highs, lows = [], []
            for b in range(2):
                rows = pl.ds(r0 + 8 * b, 8)
                w = w_ref[z, :, rows, :].reshape(8 * LINES, N)
                along_x, along_y = vx_ref[z, :, rows, :], vy_ref[z, :, rows, :]
                both = (along_x[0:LINES] + along_y[0:LINES]).reshape(8 * LINES, N)
                high, low = split(jnp.concatenate([w, both, along_x[LINES], along_y[LINES]], 0))
                highs.append(high)
                lows.append(low)
            one = dot(unmix_ref[...], jnp.concatenate(highs, 1))
            two = dot(unmix_ref[0:wide], jnp.concatenate(lows, 1))
            out = one[0:wide] + (one[wide:] + two)
            for b in range(2):
                rows = pl.ds(r0 + 8 * b, 8)
                new = c_ref[:, z, rows, :] - out[:, b * N : (b + 1) * N].reshape(ELEMENTS, 8, N)
                d_ref[:, z, rows, :] = new

    def stacked(ref, z, fields):
        value = [ref[z, f] for f in fields]
        high = jnp.concatenate([v[:, 0:N] for v in value], 1)
        low = jnp.concatenate([v[:, N : 2 * N] for v in value], 1)
        return jnp.concatenate([high, low], 0)

    def prefixes(z):
        e1_ref[z] = dot(m_ref[z].reshape(PATHS * N, 2 * N), up_ref[...]).reshape(PATHS, N, N)

    def suffixes(z):
        vy_ref[z] = dot(p1_ref[z].reshape(PATHS * N, 2 * N), down_ref[...]).reshape(PATHS, N, N)
        for l in range(0, LINES, 2):
            over_x = dot(right_ref[...], stacked(p2_ref, z, (l, l + 1)))
            vx_ref[z, l] = over_x[:, 0:N]
            vx_ref[z, l + 1] = over_x[:, N : 2 * N]
        vx_ref[z, LINES] = dot(right_ref[...], stacked(p2_ref, z, (LINES,)))

    def counts(enter_x, enter_y):
        rows_ref[...] = dot(wax_ref[...], rows_of(enter_x))
        cols_ref[...] = turned(dot(way_ref[...], rows_of(enter_y)))

        def body(z, rows, acc):
            cols = cols_ref[rows]
            k = 16 * z + LINES
            tin1 = jnp.exp2(e2_ref[z, LINES, rows] + rows_ref[k : k + 1])
            tin2 = jnp.exp2(e1_ref[z, LINES, rows] + cols[:, k : k + 1])
            sums = []
            for l in range(LINES):
                k = 16 * z + l
                a1 = tin1 * jnp.exp2(e1_ref[z, l, rows] + cols[:, k : k + 1])
                a2 = tin2 * jnp.exp2(e2_ref[z, l, rows] + rows_ref[k : k + 1])
                a1_ref[z, l, rows] = a1
                a2_ref[z, l, rows] = a2
                q = q_ref[z, l, rows]
                sums.append(q * a1)
                acc = jnp.where(lane == LINES * z + l, jnp.sum(q * a2, 1, keepdims=True), acc)
            return sums, acc

        for z, sums in enumerate(sweep(body)):
            for l, row in enumerate(sums):
                beam.put(1, LINES * z + l, step_x * row)
        dsend[1] = step_y * acc_ref[...].T[0 : LINES * ZS]

    def residuals(pred1, pred2):
        res1 = lx_ref[...] * (pred1 - mx_ref[...])
        res2 = ly_ref[...] * (pred2 - my_ref[...])
        sum1 = res1 * bsend[1] / step_x
        sum2 = res2 * dsend[1] / step_y
        rows_ref[0 : LINES * ZS] = res1
        cols_ref[...] = turned(res2)

        def body(z, rows, acc):
            cols = cols_ref[rows]
            sums = []
            all1 = jnp.zeros((CHUNK, N), F32)
            all2 = jnp.zeros((CHUNK, N), F32)

            def keep(ref, f, value):
                high, low = split(value)
                ref[z, f, rows, 0:N] = high
                ref[z, f, rows, N : 2 * N] = low

            for l in range(LINES):
                k = LINES * z + l
                w1 = a1_ref[z, l, rows] * rows_ref[k : k + 1]
                w2 = a2_ref[z, l, rows] * cols[:, k : k + 1]
                w_ref[z, l, rows] = w1 + w2
                q = q_ref[z, l, rows]
                p1, p2 = q * w1, q * w2
                all1, all2 = all1 + p1, all2 + p2
                sums.append(p2)
                acc = jnp.where(lane == 16 * z + l, jnp.sum(p1, 1, keepdims=True), acc)
                keep(p1_ref, l, p1)
                keep(p2_ref, l, p2)
            keep(p1_ref, LINES, all2)
            keep(p2_ref, LINES, all1)
            return sums, acc

        for z, sums in enumerate(sweep(body)):
            for l, row in enumerate(sums):
                tx_ref[16 * z + l : 16 * z + l + 1] = row
        ty_ref[...] = acc_ref[...].T[0 : 16 * ZS]
        for z in range(ZS):
            k, part = 16 * z + LINES, slice(LINES * z, LINES * (z + 1))
            tx_ref[k : k + 1] = jnp.sum(sum1[part], 0, keepdims=True)
            ty_ref[k : k + 1] = jnp.sum(sum2[part], 0, keepdims=True)
        bsend[2] = dot(wcx_ref[0 : LINES * ZS], rows_of(tx_ref[...]))
        dsend[2] = dot(wcy_ref[0 : LINES * ZS], rows_of(ty_ref[...]))

    def turn(step, carry):
        last = step == STEPS - 1
        for z in range(ZS):
            mix(z)
            if z == 1:

                @pl.when(step > 0)
                def halfway():
                    det.middle(0, "earlier")
                    beam.middle(0, "earlier")

        over_z(prefixes)
        enter_y = det.finish(0)
        enter_x = beam.finish(0)
        counts(enter_x, enter_y)
        det.start(1)
        beam.start(1)
        det.middle(1, "sum")
        beam.middle(1, "sum")
        pred2 = det.finish(1)
        pred1 = beam.finish(1)
        residuals(pred1, pred2)
        det.start(2)
        beam.start(2)
        over_z(suffixes)
        det.middle(2, "later")
        beam.middle(2, "later")
        over_z(unmix)

        def stores():
            return [pltpu.make_async_copy(d_ref.at[:, z], out_hbm.at[:, z], conc_sems.at[z]) for z in range(ZS)]

        @pl.when(last)
        def leave():
            for store in stores():
                store.start()

        after_y = det.finish(2)
        after_x = beam.finish(2)

        @pl.when(last)
        def left():
            for z in range(ZS):
                part = slice(ELEMENTS * z, ELEMENTS * (z + 1))
                dx_ref[z, 0:ELEMENTS] = after_x[part]
                dy_ref[z, 0:ELEMENTS] = after_y[part]
            for store in stores():
                store.wait()

        @pl.when(jnp.logical_not(last))
        def go_on():
            cols_ref[...] = turned(after_y)
            totals(after_x)
            det.start(0)
            beam.start(0)

        return carry

    lax.fori_loop(0, STEPS, turn, 0)


def close(c_hbm, dx_hbm, dy_hbm, out_hbm, c_ref, dx_ref, dy_ref, sems):
    loads = [pltpu.make_async_copy(a, b, sems.at[k]) for k, (a, b) in enumerate(((dx_hbm, dx_ref), (dy_hbm, dy_ref)))]
    loads += [pltpu.make_async_copy(c_hbm.at[:, z], c_ref.at[:, z], sems.at[2 + z]) for z in range(ZS)]
    for load in loads:
        load.start()
    loads[0].wait()
    loads[1].wait()
    stores = []
    for z in range(ZS):
        cols = jnp.concatenate([dy_ref[z], jnp.zeros((N - 16, N), F32)], 0).T
        loads[2 + z].wait()
        for e in range(ELEMENTS):
            c_ref[e, z] = c_ref[e, z] + dx_ref[z, e : e + 1] + cols[:, e : e + 1]
        stores.append(pltpu.make_async_copy(c_ref.at[:, z], out_hbm.at[:, z], sems.at[2 + z]))
        stores[z].start()
    for store in stores:
        store.wait()


def solution(mesh):
    beams, dets = mesh.shape["beam"], mesh.shape["det"]

    def shards(conc, inc, sig, yld, rate, axis, m1, live1, m2, live2):
        step_x = 1.0 / (conc.shape[2] * beams)
        step_y = 1.0 / (conc.shape[3] * dets)

        def body(*refs):
            kernel(beams, dets, step_x, step_y, *refs)

        def exchange(count):
            def rows(slots):
                return pltpu.VMEM((3, slots, max(ROWS), N), F32)

            own = pltpu.VMEM((3, max(ROWS), N), F32)
            return [own, rows(count // AHEAD), rows(2), rows(AHEAD), pltpu.SemaphoreType.DMA((3, 2, 2))]

        field = (N, N)
        anywhere = pl.BlockSpec(memory_space=pl.ANY)
        vmem = pl.BlockSpec(memory_space=pltpu.VMEM)
        small = (axis[None], inc, sig, yld, rate[None], m1, live1, m2, live2)
        inner, dx, dy = pl.pallas_call(
            body,
            out_shape=[
                jax.ShapeDtypeStruct(conc.shape, F32),
                jax.ShapeDtypeStruct((ZS, 16, N), F32),
                jax.ShapeDtypeStruct((ZS, 16, N), F32),
            ],
            in_specs=[anywhere] * (len(small) + 1),
            out_specs=[anywhere, vmem, vmem],
            scratch_shapes=[
                *[pltpu.VMEM(a.shape, a.dtype) for a in small + (conc,)],
                pltpu.SemaphoreType.DMA((len(small),)),
                pltpu.SemaphoreType.DMA((ZS,)),
                pltpu.VMEM((ZS, PATHS, N, 2 * N), BF16),
                pltpu.VMEM((ZS, LINES) + field, F32),
                *[pltpu.VMEM((ZS, LINES + 1) + field, F32)] * 2,
                *[pltpu.VMEM((ZS, LINES) + field, F32)] * 3,
                *[pltpu.VMEM((ZS, LINES + 1, N, 2 * N), BF16)] * 2,
                *[pltpu.VMEM((ZS, PATHS) + field, F32)] * 2,
                pltpu.VMEM(conc.shape, F32),
                pltpu.VMEM((16 * ZS, N), F32),
                *[pltpu.VMEM(field, F32)] * 2,
                *[pltpu.VMEM((LINES * ZS, N), F32)] * 4,
                *[pltpu.VMEM((16 * ZS, N), F32)] * 2,
                pltpu.VMEM((64, N), F32),
                pltpu.VMEM((32, N), F32),
                pltpu.VMEM((8 * FIELDS, 2 * N), BF16),
                pltpu.VMEM((16 * ELEMENTS, 8 * PARTS), BF16),
                *[pltpu.VMEM((2 * N, N), BF16)] * 2,
                pltpu.VMEM((N, 2 * N), BF16),
                *[pltpu.VMEM((16 * ZS, 3 * N), BF16)] * 4,
                *exchange(beams),
                *exchange(dets),
            ],
            compiler_params=pltpu.CompilerParams(
                collective_id=0, has_side_effects=True, vmem_limit_bytes=64 * 1024 * 1024
            ),
        )(*small, conc)

        return pl.pallas_call(
            close,
            out_shape=jax.ShapeDtypeStruct(conc.shape, F32),
            in_specs=[anywhere] * 3,
            out_specs=anywhere,
            scratch_shapes=[
                pltpu.VMEM(conc.shape, F32),
                *[pltpu.VMEM((ZS, 16, N), F32)] * 2,
                pltpu.SemaphoreType.DMA((2 + ZS,)),
            ],
            compiler_params=pltpu.CompilerParams(vmem_limit_bytes=64 * 1024 * 1024),
        )(inner, dx, dy)

    in_specs = (
        P(None, None, "beam", "det"),
        P(),
        P(),
        P(),
        P(),
        P(),
        P(None, None, "det"),
        P(None, "det"),
        P(None, None, "beam"),
        P(None, "beam"),
    )
    out_specs = P(None, None, "beam", "det")
    return jax.shard_map(shards, mesh=mesh, in_specs=in_specs, out_specs=out_specs, check_vma=False)
```

```python
import math

import jax
import jax.numpy as jnp
from jax import lax
from jax.experimental import pallas as pl
from jax.experimental.pallas import tpu as pltpu
from jax.sharding import PartitionSpec as P

STEPS = 2
HIGH = lax.Precision.HIGHEST
MESH = pl.DeviceIdType.MESH
F32 = jnp.float32
BF16 = jnp.bfloat16
ELEMENTS = 10
LINES = 12
ZS = 4
N = 128
PATHS = LINES + 1
FIELDS = 3 * PATHS + LINES
CHUNK = 64
AHEAD = 4
PARTS = 2 * LINES + 2
GROUPS = 2
PER = ZS // GROUPS
ROWS = LINES * PER
LOG2E = math.log2(math.e)


def split(value):
    high = value.astype(BF16)
    return high, (value - high.astype(F32)).astype(BF16)


def iota(shape, dim):
    return lax.broadcasted_iota(jnp.int32, shape, dim)


def dot(a, b):
    return jnp.dot(a, b, preferred_element_type=F32)


def exact(a, b):
    return jnp.dot(a, b, preferred_element_type=F32, precision=HIGH)


def exact_nt(a, b):
    return lax.dot_general(
        a, b, (((1,), (1,)), ((), ())), preferred_element_type=F32, precision=HIGH
    )


def triple(table):
    high, low = split(table)
    return jnp.concatenate([high, high, low], 1)


def rows_of(value):
    high, low = split(jnp.concatenate([value, jnp.zeros((-value.shape[0] % 128, value.shape[1]), F32)], 0))
    return jnp.concatenate([high, low, high], 0)


def one_hot(condition):
    return jnp.where(condition, 1.0, 0.0).astype(F32)


class Ring:
    def __init__(self, axis, count, send, near, out, far, sems):
        self.axis, self.count = axis, count
        self.send, self.near, self.out, self.far, self.sems = send, near, out, far, sems
        self.slots = count // AHEAD
        self.cores = self.slots // 2
        me = lax.axis_index(axis)
        self.c = lax.rem(me, self.cores)
        self.x = lax.rem(me // self.cores, AHEAD)
        self.y = me // (self.cores * AHEAD)
        self.slot = self.y * self.cores + self.c

    def index(self, y, x, c):
        return (y * AHEAD + x) * self.cores + c

    def near_peers(self):
        slots = [lax.rem(self.slot + d, self.slots) for d in range(1, self.slots)]
        return [self.index(k // self.cores, self.x, lax.rem(k, self.cores)) for k in slots]

    def far_peers(self):
        return [(d, self.index(self.y, lax.rem(self.x + d, AHEAD), self.c)) for d in (2, 1, 3)]

    def greet(self, barrier):
        peers = self.near_peers() + [peer for _, peer in self.far_peers()]
        for peer in peers:
            pl.semaphore_signal(barrier, inc=1, device_id={self.axis: peer}, device_id_type=MESH)
        return len(peers)

    def copy(self, src, dst, phase, g, leg, peer):
        return pltpu.make_async_remote_copy(
            src_ref=src,
            dst_ref=dst,
            send_sem=self.sems.at[phase, g, leg, 0],
            recv_sem=self.sems.at[phase, g, leg, 1],
            device_id={self.axis: peer},
            device_id_type=MESH,
        )

    def start(self, phase, g):
        self.near[phase, g, pl.ds(self.slot, 1)] = self.send[phase, g][None]
        for peer in self.near_peers():
            self.copy(self.send.at[phase, g], self.near.at[phase, g, self.slot], phase, g, 0, peer).start()

    def wait(self, ref, phase, g, leg, count):
        some = ref.at[phase, g, pl.ds(0, count)]
        whole = self.copy(some, some, phase, g, leg, self.near_peers()[0])
        whole.wait_send()
        whole.wait_recv()

    def middle(self, phase, g, mode):
        self.wait(self.near, phase, g, 0, self.slots - 1)
        have = [[self.near[phase, g, y * self.cores + c] for c in range(self.cores)] for y in range(2)]
        sums = [sum(cores[1:], cores[0]) for cores in have]
        if mode == "sum":
            mine = sums[0] + sums[1]
            self.out[phase, g, 0] = mine
        else:
            earlier = mode == "earlier"

            def chosen(other, own):
                return (other < own if earlier else other > own).astype(F32)

            base = sum(sums[y] * chosen(y, self.y) for y in range(2))
            same = sum(sums[y] * (self.y == y).astype(F32) for y in range(2))
            mine = base
            for y in range(2):
                for c in range(self.cores):
                    mine = mine + have[y][c] * ((self.y == y).astype(F32) * chosen(c, self.c))
            self.out[phase, g, 0] = base
            self.out[phase, g, 1] = base + same
        self.far[phase, g, pl.ds(self.x, 1)] = mine[None]
        for d, peer in self.far_peers():
            wrap = (self.x + d) // AHEAD
            which = {"sum": 0, "earlier": 1 - wrap, "later": wrap}[mode]
            self.copy(self.out.at[phase, g, which], self.far.at[phase, g, self.x], phase, g, 1, peer).start()

    def finish(self, phase, g):
        self.wait(self.far, phase, g, 1, AHEAD - 1)
        far = [self.far[phase, g, x] for x in range(AHEAD)]
        return (far[0] + far[1]) + (far[2] + far[3])

    def put(self, phase, g, row, value):
        self.send[phase, g, row : row + 1, :] = value


def kernel(
    beams, dets, step_x, step_y,
    axis_hbm, inc_hbm, sig_hbm, yld_hbm, rate_hbm, m1_hbm, live1_hbm, m2_hbm, live2_hbm, conc_hbm,
    out_hbm, dx_ref, dy_ref,
    axis_ref, inc_ref, sig_ref, yld_ref, rate_ref, m1_ref, live1_ref, m2_ref, live2_ref, c_ref,
    load_sems, conc_sems,
    m_ref, q_ref, e1_ref, e2_ref, a1_ref, a2_ref, w_ref, p1_ref, p2_ref, vx_ref, vy_ref, d_ref, rows_ref, cols_ref, acc_ref,
    mx_ref, my_ref, lx_ref, ly_ref,
    tx_ref, ty_ref, tab_ref, back_ref, mix_ref, unmix_ref, up_ref, down_ref, right_ref,
    wax_ref, way_ref, wcx_ref, wcy_ref,
    bsend, bnear, bout, bfar, bsems, dsend, dnear, dout, dfar, dsems,
):
    def conc_load(z):
        return pltpu.make_async_copy(conc_hbm.at[:, z], c_ref.at[:, z], conc_sems.at[z])

    hbm = (axis_hbm, inc_hbm, sig_hbm, yld_hbm, rate_hbm, m1_hbm, live1_hbm, m2_hbm, live2_hbm)
    vmem = (axis_ref, inc_ref, sig_ref, yld_ref, rate_ref, m1_ref, live1_ref, m2_ref, live2_ref)
    loads = [pltpu.make_async_copy(a, b, load_sems.at[k]) for k, (a, b) in enumerate(zip(hbm, vmem))]
    for load in [conc_load(z) for z in range(ZS)] + loads:
        load.start()
    beam = Ring("beam", beams, bsend, bnear, bout, bfar, bsems)
    det = Ring("det", dets, dsend, dnear, dout, dfar, dsems)
    barrier = pltpu.get_barrier_semaphore()
    greeted = det.greet(barrier) + beam.greet(barrier)

    for ref in (bsend, dsend, cols_ref, mx_ref, my_ref, lx_ref, ly_ref, tx_ref, ty_ref, tab_ref, back_ref):
        ref[...] = jnp.zeros(ref.shape, F32)

    lane = iota((CHUNK, N), 1)

    def members(g):
        return range(g * PER, (g + 1) * PER)

    def sweep(g, body):
        sums = {}
        for r in range(0, N, CHUNK):
            acc = jnp.zeros((CHUNK, N), F32)
            for z in members(g):
                new, acc = body(z, pl.ds(r, CHUNK), acc)
                new = [jnp.sum(a.reshape(CHUNK // 8, 8, N), 0) for a in new]
                sums[z] = new if r == 0 else [a + b for a, b in zip(sums[z], new)]
            acc_ref[g, pl.ds(r, CHUNK)] = acc
        return [[jnp.sum(a, 0, keepdims=True) for a in sums[z]] for z in members(g)]

    def send_off(phase, g):
        det.start(phase, g)
        beam.start(phase, g)

    def pass_on(phase, g, mode):
        det.middle(phase, g, mode)
        beam.middle(phase, g, mode)

    def take(phase, g):
        across = det.finish(phase, g)
        return beam.finish(phase, g), across

    def turned(rows):
        return jnp.concatenate([rows, jnp.zeros((N - rows.shape[0], N), F32)], 0).T

    def totals(g, add):
        if add is not None:
            rows_ref[g, 0:ROWS] = add

        def body(z, rows, acc):
            if add is None and rows.start == 0:
                conc_load(z).wait()
            sums = []
            cols = cols_ref[g, rows]
            for e in range(ELEMENTS):
                k = ELEMENTS * (z % PER) + e
                if add is None:
                    c = c_ref[e, z, rows]
                else:
                    c = d_ref[e, z, rows] + rows_ref[g, k : k + 1] + cols[:, k : k + 1]
                    c_ref[e, z, rows] = c
                sums.append(c)
                acc = jnp.where(lane == k, jnp.sum(c, 1, keepdims=True), acc)
            return sums, acc

        for z, sums in enumerate(sweep(g, body)):
            for e, row in enumerate(sums):
                beam.put(0, g, ELEMENTS * z + e, row)
        dsend[0, g] = acc_ref[g].T[0:ROWS]

    totals(0, None)
    pl.semaphore_wait(barrier, greeted)
    send_off(0, 0)
    totals(1, None)
    send_off(0, 1)
    for load in loads:
        load.wait()

    def tables():
        first = axis_ref[0:1, 0:1] == 0
        one, two = inc_ref[0:1, :], inc_ref[1:2, :]
        s1 = jnp.where(first, one, two)
        s2 = jnp.where(first, two, one)
        scale = -LOG2E * step_y
        sig, yld, rate = sig_ref[...], yld_ref[...], rate_ref[...]
        cols = pl.ds(0, ELEMENTS)
        tab_ref[0:LINES, cols] = scale * sig
        tab_ref[LINES:PATHS, cols] = scale * s2
        for k in (PATHS, 2 * PATHS):
            tab_ref[k : k + LINES, cols] = -LOG2E * step_x * sig
            tab_ref[k + LINES : k + PATHS, cols] = -LOG2E * step_x * s1
        tab_ref[3 * PATHS : FIELDS, cols] = yld
        back_ref[0:LINES, cols] = yld * rate
        back_ref[LINES : 2 * LINES, cols] = -sig * rate
        back_ref[2 * LINES : 2 * LINES + 1, cols] = -s1 * rate
        back_ref[2 * LINES + 1 : 2 * LINES + 2, cols] = -s2 * rate

        tab, back = tab_ref[...], back_ref[...]
        wide = 8 * ELEMENTS
        pick = one_hot((iota((8 * FIELDS, 64), 0) >> 3) == iota((8 * FIELDS, 64), 1))
        col = iota((N, 256), 1)
        part = (col >= wide).astype(jnp.int32) + (col >= 2 * wide).astype(jnp.int32)
        spread = one_hot(((col - wide * part) >> 3) == iota((N, 256), 0))
        spread = jnp.where(col < 3 * wide, spread, 0.0)
        full = exact(pick, exact(tab, spread))
        shape = (8 * FIELDS, 256)
        field, gap = iota(shape, 0) >> 3, (iota(shape, 0) & 7) - (iota(shape, 1) & 7)
        within = (field >= PATHS) & (field < 2 * PATHS)
        whole = (field >= 2 * PATHS) & (field < 3 * PATHS)
        full = jnp.where(whole | (within & (gap > 0)) | ((gap == 0) & jnp.logical_not(within)), full, 0.0)
        high, low = split(full)
        part = iota(shape, 1)
        mix_ref[...] = jnp.where((part >= wide) & (part < 2 * wide), low.astype(F32), high.astype(F32)).astype(BF16)

        pick = one_hot((iota((wide, N), 0) >> 3) == iota((wide, N), 1))
        shape = (wide, 8 * PARTS)
        spread = one_hot((iota((32, 8 * PARTS), 1) >> 3) == iota((32, 8 * PARTS), 0))
        full = exact(exact_nt(pick, back), spread)
        full = jnp.where((iota(shape, 0) & 7) == (iota(shape, 1) & 7), full, 0.0)
        high, low = split(full)
        unmix_ref[0:wide] = high
        unmix_ref[wide : 2 * wide] = low

        r, m = iota((16 * PER, 64), 0) & 15, iota((16 * PER, 64), 1)
        rates_x = exact(one_hot((r < PATHS) & (m == r + PATHS)), tab)
        rates_y = exact(one_hot((r < PATHS) & (m == r)), tab)
        r, m = iota((16 * PER, 32), 0) & 15, iota((16 * PER, 32), 1)
        sums_x = exact(one_hot(m == jnp.where(r < LINES, r + LINES, 2 * LINES)), back)
        sums_y = exact(one_hot(m == jnp.where(r < LINES, r + LINES, 2 * LINES + 1)), back)
        r = iota((16 * PER, N), 0) & 15
        sums_x = jnp.where(r <= LINES, -step_x * sums_x, 0.0)
        sums_y = jnp.where(r <= LINES, -step_y * sums_y, 0.0)

        def slice_of(shape, dim):
            row = iota(shape, dim)
            return sum((row >= ELEMENTS * z).astype(jnp.int32) for z in range(1, PER))

        shape = (N, N)
        place = one_hot((iota(shape, 0) - ELEMENTS * slice_of(shape, 0) == iota(shape, 1)) & (iota(shape, 1) < ELEMENTS))
        shape = (16 * PER, N)
        same = (iota(shape, 0) >> 4) == slice_of(shape, 1)
        wax_ref[...] = triple(jnp.where(same, exact_nt(rates_x, place), 0.0))
        way_ref[...] = triple(jnp.where(same, exact_nt(rates_y, place), 0.0))
        same = slice_of(shape, 0) == (iota(shape, 1) >> 4)
        fill = jnp.zeros((N - 16 * PER, N), F32)
        for ref, sums in ((wcx_ref, sums_x), (wcy_ref, sums_y)):
            ref[...] = triple(jnp.where(same, exact_nt(place[0 : 16 * PER], jnp.concatenate([sums, fill], 0)), 0.0))

        r, c = iota((2 * N, N), 0) & (N - 1), iota((2 * N, N), 1)
        up_ref[...] = one_hot(r < c).astype(BF16)
        down_ref[...] = (step_y * one_hot(r > c)).astype(BF16)
        r, c = iota((N, 2 * N), 0), iota((N, 2 * N), 1) & (N - 1)
        right_ref[...] = (step_x * one_hot(c > r)).astype(BF16)
        for z in range(ZS):
            live1 = live1_ref[z : z + 1, :].astype(F32)
            live2 = live2_ref[z : z + 1, :].astype(F32)
            for l in range(LINES):
                g, k = z // PER, LINES * (z % PER) + l
                lx_ref[g, k : k + 1, :] = live1
                ly_ref[g, k : k + 1, :] = live2
                mx_ref[g, k : k + 1, :] = m1_ref[l, z : z + 1, :]
                my_ref[g, k : k + 1, :] = m2_ref[l, z : z + 1, :]

    tables()
    pass_on(0, 0, "earlier")

    def mix(z):
        run = [jnp.zeros((8, N), F32)] * PATHS
        for r0 in range(0, N, 16):
            parts = []
            for b in range(2):
                high, low = split(c_ref[:, z, pl.ds(r0 + 8 * b, 8), :].reshape(8 * ELEMENTS, N))
                parts.append(jnp.concatenate([high, high, low, jnp.zeros((16, N), BF16)], 0))
            out = dot(mix_ref[...], jnp.concatenate(parts, 1))

            def field(f):
                return [out[8 * f : 8 * f + 8, b * N : (b + 1) * N] for b in range(2)]

            rows = pl.ds(r0, 16)
            for l in range(PATHS):
                high, low = split(jnp.concatenate(field(l), 0))
                m_ref[z, l, rows, 0:N] = high
                m_ref[z, l, rows, N : 2 * N] = low
                within, whole = field(PATHS + l), field(2 * PATHS + l)
                for b in range(2):
                    e2_ref[z, l, pl.ds(r0 + 8 * b, 8)] = run[l] + within[b]
                    run[l] = run[l] + whole[b]
            for l in range(LINES):
                q_ref[z, l, rows, :] = jnp.concatenate(field(3 * PATHS + l), 0)

    def unmix(z):
        wide = 8 * ELEMENTS
        for r0 in range(0, N, 16):
            highs, lows = [], []
            for b in range(2):
                rows = pl.ds(r0 + 8 * b, 8)
                w = w_ref[z, :, rows, :].reshape(8 * LINES, N)
                along_x, along_y = vx_ref[z, :, rows, :], vy_ref[z, :, rows, :]
                both = (along_x[0:LINES] + along_y[0:LINES]).reshape(8 * LINES, N)
                high, low = split(jnp.concatenate([w, both, along_x[LINES], along_y[LINES]], 0))
                highs.append(high)
                lows.append(low)
            one = dot(unmix_ref[...], jnp.concatenate(highs, 1))
            two = dot(unmix_ref[0:wide], jnp.concatenate(lows, 1))
            out = one[0:wide] + (one[wide:] + two)
            for b in range(2):
                rows = pl.ds(r0 + 8 * b, 8)
                new = c_ref[:, z, rows, :] - out[:, b * N : (b + 1) * N].reshape(ELEMENTS, 8, N)
                d_ref[:, z, rows, :] = new

    def stacked(ref, z, fields):
        value = [ref[z, f] for f in fields]
        high = jnp.concatenate([v[:, 0:N] for v in value], 1)
        low = jnp.concatenate([v[:, N : 2 * N] for v in value], 1)
        return jnp.concatenate([high, low], 0)

    def prefixes(z):
        e1_ref[z] = dot(m_ref[z].reshape(PATHS * N, 2 * N), up_ref[...]).reshape(PATHS, N, N)

    def suffixes(z):
        vy_ref[z] = dot(p1_ref[z].reshape(PATHS * N, 2 * N), down_ref[...]).reshape(PATHS, N, N)
        for l in range(0, LINES, 2):
            over_x = dot(right_ref[...], stacked(p2_ref, z, (l, l + 1)))
            vx_ref[z, l] = over_x[:, 0:N]
            vx_ref[z, l + 1] = over_x[:, N : 2 * N]
        vx_ref[z, LINES] = dot(right_ref[...], stacked(p2_ref, z, (LINES,)))

    def counts(g, enter_x, enter_y):
        rows_ref[g] = dot(wax_ref[...], rows_of(enter_x))
        cols_ref[g] = turned(dot(way_ref[...], rows_of(enter_y)))

        def body(z, rows, acc):
            cols = cols_ref[g, rows]
            k = 16 * (z % PER) + LINES
            tin1 = jnp.exp2(e2_ref[z, LINES, rows] + rows_ref[g, k : k + 1])
            tin2 = jnp.exp2(e1_ref[z, LINES, rows] + cols[:, k : k + 1])
            sums = []
            for l in range(LINES):
                k = 16 * (z % PER) + l
                a1 = tin1 * jnp.exp2(e1_ref[z, l, rows] + cols[:, k : k + 1])
                a2 = tin2 * jnp.exp2(e2_ref[z, l, rows] + rows_ref[g, k : k + 1])
                a1_ref[z, l, rows] = a1
                a2_ref[z, l, rows] = a2
                q = q_ref[z, l, rows]
                sums.append(q * a1)
                acc = jnp.where(lane == LINES * (z % PER) + l, jnp.sum(q * a2, 1, keepdims=True), acc)
            return sums, acc

        for z, sums in enumerate(sweep(g, body)):
            for l, row in enumerate(sums):
                beam.put(1, g, LINES * z + l, step_x * row)
        dsend[1, g] = step_y * acc_ref[g].T[0:ROWS]

    def residuals(g, pred1, pred2):
        res1 = lx_ref[g] * (pred1 - mx_ref[g])
        res2 = ly_ref[g] * (pred2 - my_ref[g])
        sum1 = res1 * bsend[1, g] / step_x
        sum2 = res2 * dsend[1, g] / step_y
        rows_ref[g, 0:ROWS] = res1
        cols_ref[g] = turned(res2)

        def body(z, rows, acc):
            cols = cols_ref[g, rows]
            sums = []
            all1 = jnp.zeros((CHUNK, N), F32)
            all2 = jnp.zeros((CHUNK, N), F32)

            def keep(ref, f, value):
                high, low = split(value)
                ref[z, f, rows, 0:N] = high
                ref[z, f, rows, N : 2 * N] = low

            for l in range(LINES):
                k = LINES * (z % PER) + l
                w1 = a1_ref[z, l, rows] * rows_ref[g, k : k + 1]
                w2 = a2_ref[z, l, rows] * cols[:, k : k + 1]
                w_ref[z, l, rows] = w1 + w2
                q = q_ref[z, l, rows]
                p1, p2 = q * w1, q * w2
                all1, all2 = all1 + p1, all2 + p2
                sums.append(p2)
                acc = jnp.where(lane == 16 * (z % PER) + l, jnp.sum(p1, 1, keepdims=True), acc)
                keep(p1_ref, l, p1)
                keep(p2_ref, l, p2)
            keep(p1_ref, LINES, all2)
            keep(p2_ref, LINES, all1)
            return sums, acc

        for z, sums in enumerate(sweep(g, body)):
            for l, row in enumerate(sums):
                tx_ref[g, 16 * z + l : 16 * z + l + 1] = row
        ty_ref[g] = acc_ref[g].T[0 : 16 * PER]
        for z in range(PER):
            k, part = 16 * z + LINES, slice(LINES * z, LINES * (z + 1))
            tx_ref[g, k : k + 1] = jnp.sum(sum1[part], 0, keepdims=True)
            ty_ref[g, k : k + 1] = jnp.sum(sum2[part], 0, keepdims=True)
        bsend[2, g] = dot(wcx_ref[...], rows_of(tx_ref[g]))[0:ROWS]
        dsend[2, g] = dot(wcy_ref[...], rows_of(ty_ref[g]))[0:ROWS]

    def store(z):
        return pltpu.make_async_copy(d_ref.at[:, z], out_hbm.at[:, z], conc_sems.at[z])

    def end(g, after_x, after_y):
        for z in range(PER):
            part = slice(ELEMENTS * z, ELEMENTS * (z + 1))
            dx_ref[g * PER + z, 0:ELEMENTS] = after_x[part]
            dy_ref[g * PER + z, 0:ELEMENTS] = after_y[part]

    def renew(g, after_x, after_y):
        cols_ref[g] = turned(after_y)
        totals(g, after_x)
        send_off(0, g)

    def turn(step, carry):
        last = step == STEPS - 1
        more = jnp.logical_not(last)

        def each(stage, g):
            for z in members(g):
                stage(z)

        each(mix, 0)
        pass_on(0, 1, "earlier")
        each(prefixes, 0)
        each(mix, 1)
        counts(0, *take(0, 0))
        send_off(1, 0)
        each(prefixes, 1)
        enter = take(0, 1)
        pass_on(1, 0, "sum")
        counts(1, *enter)
        send_off(1, 1)
        residuals(0, *take(1, 0))
        send_off(2, 0)
        pass_on(1, 1, "sum")
        each(suffixes, 0)
        pass_on(2, 0, "later")
        residuals(1, *take(1, 1))
        send_off(2, 1)
        each(unmix, 0)

        @pl.when(last)
        def leave():
            for z in members(0):
                store(z).start()

        after = take(2, 0)

        @pl.when(more)
        def again():
            renew(0, *after)

        @pl.when(last)
        def part():
            end(0, *after)

        pass_on(2, 1, "later")
        each(suffixes, 1)

        @pl.when(more)
        def early():
            pass_on(0, 0, "earlier")

        each(unmix, 1)

        @pl.when(last)
        def leave_too():
            for z in members(1):
                store(z).start()

        rest = take(2, 1)

        @pl.when(more)
        def once_more():
            renew(1, *rest)

        @pl.when(last)
        def finish():
            end(1, *rest)
            for z in range(ZS):
                store(z).wait()

        return carry

    lax.fori_loop(0, STEPS, turn, 0)


def close(c_hbm, dx_hbm, dy_hbm, out_hbm, c_ref, dx_ref, dy_ref, sems):
    loads = [pltpu.make_async_copy(a, b, sems.at[k]) for k, (a, b) in enumerate(((dx_hbm, dx_ref), (dy_hbm, dy_ref)))]
    loads += [pltpu.make_async_copy(c_hbm.at[:, z], c_ref.at[:, z], sems.at[2 + z]) for z in range(ZS)]
    for load in loads:
        load.start()
    loads[0].wait()
    loads[1].wait()
    stores = []
    for z in range(ZS):
        cols = jnp.concatenate([dy_ref[z], jnp.zeros((N - 16, N), F32)], 0).T
        loads[2 + z].wait()
        for e in range(ELEMENTS):
            c_ref[e, z] = c_ref[e, z] + dx_ref[z, e : e + 1] + cols[:, e : e + 1]
        stores.append(pltpu.make_async_copy(c_ref.at[:, z], out_hbm.at[:, z], sems.at[2 + z]))
        stores[z].start()
    for store in stores:
        store.wait()


def solution(mesh):
    beams, dets = mesh.shape["beam"], mesh.shape["det"]

    def shards(conc, inc, sig, yld, rate, axis, m1, live1, m2, live2):
        step_x = 1.0 / (conc.shape[2] * beams)
        step_y = 1.0 / (conc.shape[3] * dets)

        def body(*refs):
            kernel(beams, dets, step_x, step_y, *refs)

        def exchange(count):
            def rows(*slots):
                return pltpu.VMEM((3, GROUPS) + slots + (ROWS, N), F32)

            sems = pltpu.SemaphoreType.DMA((3, GROUPS, 2, 2))
            return [rows(), rows(count // AHEAD), rows(2), rows(AHEAD), sems]

        def grouped(rows):
            return pltpu.VMEM((GROUPS, rows, N), F32)

        field = (N, N)
        anywhere = pl.BlockSpec(memory_space=pl.ANY)
        vmem = pl.BlockSpec(memory_space=pltpu.VMEM)
        small = (axis[None], inc, sig, yld, rate[None], m1, live1, m2, live2)
        inner, dx, dy = pl.pallas_call(
            body,
            out_shape=[
                jax.ShapeDtypeStruct(conc.shape, F32),
                jax.ShapeDtypeStruct((ZS, 16, N), F32),
                jax.ShapeDtypeStruct((ZS, 16, N), F32),
            ],
            in_specs=[anywhere] * (len(small) + 1),
            out_specs=[anywhere, vmem, vmem],
            scratch_shapes=[
                *[pltpu.VMEM(a.shape, a.dtype) for a in small + (conc,)],
                pltpu.SemaphoreType.DMA((len(small),)),
                pltpu.SemaphoreType.DMA((ZS,)),
                pltpu.VMEM((ZS, PATHS, N, 2 * N), BF16),
                pltpu.VMEM((ZS, LINES) + field, F32),
                *[pltpu.VMEM((ZS, LINES + 1) + field, F32)] * 2,
                *[pltpu.VMEM((ZS, LINES) + field, F32)] * 3,
                *[pltpu.VMEM((ZS, LINES + 1, N, 2 * N), BF16)] * 2,
                *[pltpu.VMEM((ZS, PATHS) + field, F32)] * 2,
                pltpu.VMEM(conc.shape, F32),
                grouped(16 * PER),
                *[grouped(N)] * 2,
                *[grouped(ROWS)] * 4,
                *[grouped(16 * PER)] * 2,
                pltpu.VMEM((64, N), F32),
                pltpu.VMEM((32, N), F32),
                pltpu.VMEM((8 * FIELDS, 2 * N), BF16),
                pltpu.VMEM((16 * ELEMENTS, 8 * PARTS), BF16),
                *[pltpu.VMEM((2 * N, N), BF16)] * 2,
                pltpu.VMEM((N, 2 * N), BF16),
                *[pltpu.VMEM((16 * PER, 3 * N), BF16)] * 4,
                *exchange(beams),
                *exchange(dets),
            ],
            compiler_params=pltpu.CompilerParams(
                collective_id=0, has_side_effects=True, vmem_limit_bytes=64 * 1024 * 1024
            ),
        )(*small, conc)

        return pl.pallas_call(
            close,
            out_shape=jax.ShapeDtypeStruct(conc.shape, F32),
            in_specs=[anywhere] * 3,
            out_specs=anywhere,
            scratch_shapes=[
                pltpu.VMEM(conc.shape, F32),
                *[pltpu.VMEM((ZS, 16, N), F32)] * 2,
                pltpu.SemaphoreType.DMA((2 + ZS,)),
            ],
            compiler_params=pltpu.CompilerParams(vmem_limit_bytes=64 * 1024 * 1024),
        )(inner, dx, dy)

    in_specs = (
        P(None, None, "beam", "det"),
        P(),
        P(),
        P(),
        P(),
        P(),
        P(None, None, "det"),
        P(None, "det"),
        P(None, None, "beam"),
        P(None, "beam"),
    )
    out_specs = P(None, None, "beam", "det")
    return jax.shard_map(shards, mesh=mesh, in_specs=in_specs, out_specs=out_specs, check_vma=False)
```

```python
import math

import jax
import jax.numpy as jnp
from jax import lax
from jax.experimental import pallas as pl
from jax.experimental.pallas import tpu as pltpu
from jax.sharding import PartitionSpec as P

STEPS = 2
HIGH = lax.Precision.HIGHEST
MESH = pl.DeviceIdType.MESH
F32 = jnp.float32
BF16 = jnp.bfloat16
ELEMENTS = 10
LINES = 12
ZS = 4
N = 128
PATHS = LINES + 1
FIELDS = 3 * PATHS + LINES
AHEAD = 4
PARTS = 2 * LINES + 2
GROUPS = 2
PER = ZS // GROUPS
ROWS = 16 * PER
LOG2E = math.log2(math.e)


def split(value):
    high = value.astype(BF16)
    return high, (value - high.astype(F32)).astype(BF16)


def iota(shape, dim):
    return lax.broadcasted_iota(jnp.int32, shape, dim)


def dot(a, b):
    return jnp.dot(a, b, preferred_element_type=F32)


def exact(a, b):
    return jnp.dot(a, b, preferred_element_type=F32, precision=HIGH)


def exact_nt(a, b):
    return lax.dot_general(
        a, b, (((1,), (1,)), ((), ())), preferred_element_type=F32, precision=HIGH
    )


def triple(table):
    high, low = split(table)
    return jnp.concatenate([high, high, low], 1)


def rows_of(value):
    high, low = split(jnp.concatenate([value, jnp.zeros((-value.shape[0] % 128, value.shape[1]), F32)], 0))
    return jnp.concatenate([high, low, high], 0)


def one_hot(condition):
    return jnp.where(condition, 1.0, 0.0).astype(F32)


class Ring:
    def __init__(self, axis, count, send, near, out, far, sems):
        self.axis, self.count = axis, count
        self.send, self.near, self.out, self.far, self.sems = send, near, out, far, sems
        self.slots = count // AHEAD
        self.cores = self.slots // 2
        me = lax.axis_index(axis)
        self.c = lax.rem(me, self.cores)
        self.x = lax.rem(me // self.cores, AHEAD)
        self.y = me // (self.cores * AHEAD)
        self.slot = self.y * self.cores + self.c

    def index(self, y, x, c):
        return (y * AHEAD + x) * self.cores + c

    def near_peers(self):
        slots = [lax.rem(self.slot + d, self.slots) for d in range(1, self.slots)]
        return [self.index(k // self.cores, self.x, lax.rem(k, self.cores)) for k in slots]

    def far_peers(self):
        return [(d, self.index(self.y, lax.rem(self.x + d, AHEAD), self.c)) for d in (2, 1, 3)]

    def greet(self, barrier):
        peers = self.near_peers() + [peer for _, peer in self.far_peers()]
        for peer in peers:
            pl.semaphore_signal(barrier, inc=1, device_id={self.axis: peer}, device_id_type=MESH)
        return len(peers)

    def copy(self, src, dst, phase, g, leg, peer):
        return pltpu.make_async_remote_copy(
            src_ref=src,
            dst_ref=dst,
            send_sem=self.sems.at[phase, g, leg, 0],
            recv_sem=self.sems.at[phase, g, leg, 1],
            device_id={self.axis: peer},
            device_id_type=MESH,
        )

    def start(self, phase, g):
        self.near[phase, g, pl.ds(self.slot, 1)] = self.send[phase, g][None]
        for peer in self.near_peers():
            self.copy(self.send.at[phase, g], self.near.at[phase, g, self.slot], phase, g, 0, peer).start()

    def wait(self, ref, phase, g, leg, count):
        some = ref.at[phase, g, pl.ds(0, count)]
        whole = self.copy(some, some, phase, g, leg, self.near_peers()[0])
        whole.wait_send()
        whole.wait_recv()

    def middle(self, phase, g, mode):
        self.wait(self.near, phase, g, 0, self.slots - 1)
        have = [[self.near[phase, g, y * self.cores + c] for c in range(self.cores)] for y in range(2)]
        sums = [sum(cores[1:], cores[0]) for cores in have]
        if mode == "sum":
            mine = sums[0] + sums[1]
            self.out[phase, g, 0] = mine
        else:
            earlier = mode == "earlier"

            def chosen(other, own):
                return (other < own if earlier else other > own).astype(F32)

            base = sum(sums[y] * chosen(y, self.y) for y in range(2))
            same = sum(sums[y] * (self.y == y).astype(F32) for y in range(2))
            mine = base
            for y in range(2):
                for c in range(self.cores):
                    mine = mine + have[y][c] * ((self.y == y).astype(F32) * chosen(c, self.c))
            self.out[phase, g, 0] = base
            self.out[phase, g, 1] = base + same
        self.far[phase, g, pl.ds(self.x, 1)] = mine[None]
        for d, peer in self.far_peers():
            wrap = (self.x + d) // AHEAD
            which = {"sum": 0, "earlier": 1 - wrap, "later": wrap}[mode]
            self.copy(self.out.at[phase, g, which], self.far.at[phase, g, self.x], phase, g, 1, peer).start()

    def finish(self, phase, g):
        self.wait(self.far, phase, g, 1, AHEAD - 1)
        far = [self.far[phase, g, x] for x in range(AHEAD)]
        return (far[0] + far[1]) + (far[2] + far[3])

    def put(self, phase, g, row, value):
        self.send[phase, g, row : row + 1, :] = value


def kernel(
    beams, dets, step_x, step_y,
    axis_hbm, inc_hbm, sig_hbm, yld_hbm, rate_hbm, m1_hbm, live1_hbm, m2_hbm, live2_hbm, conc_hbm,
    out_hbm, dx_ref, dy_ref,
    axis_ref, inc_ref, sig_ref, yld_ref, rate_ref, m1_ref, live1_ref, m2_ref, live2_ref, c_ref,
    load_sems, conc_sems,
    m_ref, q_ref, e1_ref, e2_ref, a1_ref, a2_ref, w_ref, p1_ref, p2_ref, vx_ref, vy_ref, d_ref, rows_ref, cols_ref, spread_ref,
    mx_ref, my_ref, lx_ref, ly_ref,
    tx_ref, ty_ref, tab_ref, back_ref, mix_ref, unmix_ref, up_ref, down_ref, right_ref,
    wcx_ref, wcy_ref,
    bsend, bnear, bout, bfar, bsems, dsend, dnear, dout, dfar, dsems,
):
    def conc_load(z):
        return pltpu.make_async_copy(conc_hbm.at[:, z], c_ref.at[:, z], conc_sems.at[z])

    hbm = (axis_hbm, inc_hbm, sig_hbm, yld_hbm, rate_hbm, m1_hbm, live1_hbm, m2_hbm, live2_hbm)
    vmem = (axis_ref, inc_ref, sig_ref, yld_ref, rate_ref, m1_ref, live1_ref, m2_ref, live2_ref)
    loads = [pltpu.make_async_copy(a, b, load_sems.at[k]) for k, (a, b) in enumerate(zip(hbm, vmem))]
    for load in [conc_load(z) for z in range(ZS)] + loads:
        load.start()
    beam = Ring("beam", beams, bsend, bnear, bout, bfar, bsems)
    det = Ring("det", dets, dsend, dnear, dout, dfar, dsems)
    barrier = pltpu.get_barrier_semaphore()
    greeted = det.greet(barrier) + beam.greet(barrier)

    for ref in (bsend, dsend, mx_ref, my_ref, lx_ref, ly_ref, tx_ref, ty_ref, tab_ref, back_ref):
        ref[...] = jnp.zeros(ref.shape, F32)

    lane = iota((N, N), 1)

    def members(g):
        return range(g * PER, (g + 1) * PER)

    def send_off(phase, g):
        det.start(phase, g)
        beam.start(phase, g)

    def pass_on(phase, g, mode):
        det.middle(phase, g, mode)
        beam.middle(phase, g, mode)

    def take(phase, g):
        across = det.finish(phase, g)
        return beam.finish(phase, g), across

    def turn_over(g, rows):
        high = rows.astype(BF16).astype(F32)
        rest = rows - high
        middle = rest.astype(BF16).astype(F32)
        parts = [high, middle, rest - middle, jnp.zeros((N - 3 * ROWS, N), F32)]
        cols_ref[g] = jnp.concatenate(parts, 0).T.astype(BF16)

    def spread(g, k, count):
        out = dot(cols_ref[g], spread_ref[:, k * N : (k + count) * N])
        return [out[:, n * N : (n + 1) * N] for n in range(count)]

    def row_sum(value):
        return jnp.sum(jnp.sum(value.reshape(N // 8, 8, N), 0), 0, keepdims=True)

    for load in loads:
        load.wait()

    def tables():
        first = axis_ref[0:1, 0:1] == 0
        one, two = inc_ref[0:1, :], inc_ref[1:2, :]
        s1 = jnp.where(first, one, two)
        s2 = jnp.where(first, two, one)
        scale = -LOG2E * step_y
        sig, yld, rate = sig_ref[...], yld_ref[...], rate_ref[...]
        cols = pl.ds(0, ELEMENTS)
        tab_ref[0:LINES, cols] = scale * sig
        tab_ref[LINES:PATHS, cols] = scale * s2
        for k in (PATHS, 2 * PATHS):
            tab_ref[k : k + LINES, cols] = -LOG2E * step_x * sig
            tab_ref[k + LINES : k + PATHS, cols] = -LOG2E * step_x * s1
        tab_ref[3 * PATHS : FIELDS, cols] = yld
        back_ref[0:LINES, cols] = yld * rate
        back_ref[LINES : 2 * LINES, cols] = -sig * rate
        back_ref[2 * LINES : 2 * LINES + 1, cols] = -s1 * rate
        back_ref[2 * LINES + 1 : 2 * LINES + 2, cols] = -s2 * rate

        tab, back = tab_ref[...], back_ref[...]
        wide = 8 * ELEMENTS
        pick = one_hot((iota((8 * FIELDS, 64), 0) >> 3) == iota((8 * FIELDS, 64), 1))
        col = iota((N, 256), 1)
        part = (col >= wide).astype(jnp.int32) + (col >= 2 * wide).astype(jnp.int32)
        spread = one_hot(((col - wide * part) >> 3) == iota((N, 256), 0))
        spread = jnp.where(col < 3 * wide, spread, 0.0)
        full = exact(pick, exact(tab, spread))
        shape = (8 * FIELDS, 256)
        field, gap = iota(shape, 0) >> 3, (iota(shape, 0) & 7) - (iota(shape, 1) & 7)
        within = (field >= PATHS) & (field < 2 * PATHS)
        whole = (field >= 2 * PATHS) & (field < 3 * PATHS)
        full = jnp.where(whole | (within & (gap > 0)) | ((gap == 0) & jnp.logical_not(within)), full, 0.0)
        high, low = split(full)
        part = iota(shape, 1)
        mix_ref[...] = jnp.where((part >= wide) & (part < 2 * wide), low.astype(F32), high.astype(F32)).astype(BF16)

        pick = one_hot((iota((wide, N), 0) >> 3) == iota((wide, N), 1))
        shape = (wide, 8 * PARTS)
        spread = one_hot((iota((32, 8 * PARTS), 1) >> 3) == iota((32, 8 * PARTS), 0))
        full = exact(exact_nt(pick, back), spread)
        full = jnp.where((iota(shape, 0) & 7) == (iota(shape, 1) & 7), full, 0.0)
        high, low = split(full)
        unmix_ref[0:wide] = high
        unmix_ref[wide : 2 * wide] = low

        r, m = iota((16 * PER, 32), 0) & 15, iota((16 * PER, 32), 1)
        sums_x = exact(one_hot(m == jnp.where(r < LINES, r + LINES, 2 * LINES)), back)
        sums_y = exact(one_hot(m == jnp.where(r < LINES, r + LINES, 2 * LINES + 1)), back)
        r = iota((16 * PER, N), 0) & 15
        sums_x = jnp.where(r <= LINES, -step_x * sums_x, 0.0)
        sums_y = jnp.where(r <= LINES, -step_y * sums_y, 0.0)

        shape = (ROWS, N)
        place = one_hot(((iota(shape, 0) & 15) == iota(shape, 1)) & (iota(shape, 1) < ELEMENTS))
        same = (iota(shape, 0) >> 4) == (iota(shape, 1) >> 4)
        fill = jnp.zeros((N - ROWS, N), F32)
        for ref, sums in ((wcx_ref, sums_x), (wcy_ref, sums_y)):
            ref[...] = triple(jnp.where(same, exact_nt(place, jnp.concatenate([sums, fill], 0)), 0.0))
        shape = spread_ref.shape
        k = iota(shape, 0)
        spread_ref[...] = one_hot((k < 3 * ROWS) & ((k & (ROWS - 1)) == (iota(shape, 1) >> 7))).astype(BF16)

        r, c = iota((2 * N, N), 0) & (N - 1), iota((2 * N, N), 1)
        ones = jnp.ones((2 * N, N), F32)
        up_ref[...] = jnp.concatenate([one_hot(r < c), ones], 1).astype(BF16)
        down_ref[...] = jnp.concatenate([step_y * one_hot(r > c), ones], 1).astype(BF16)
        r, c = iota((N, 2 * N), 0), iota((N, 2 * N), 1) & (N - 1)
        right_ref[...] = (step_x * one_hot(c > r)).astype(BF16)
        for z in range(ZS):
            live1 = live1_ref[z : z + 1, :].astype(F32)
            live2 = live2_ref[z : z + 1, :].astype(F32)
            for l in range(LINES):
                g, k = z // PER, 16 * (z % PER) + l
                lx_ref[g, k : k + 1, :] = live1
                ly_ref[g, k : k + 1, :] = live2
                mx_ref[g, k : k + 1, :] = m1_ref[l, z : z + 1, :]
                my_ref[g, k : k + 1, :] = m2_ref[l, z : z + 1, :]

    tables()

    def mix(z):
        run = [jnp.zeros((8, N), F32)] * PATHS
        for r0 in range(0, N, 16):
            parts = []
            for b in range(2):
                high, low = split(c_ref[:, z, pl.ds(r0 + 8 * b, 8), :].reshape(8 * ELEMENTS, N))
                parts.append(jnp.concatenate([high, high, low, jnp.zeros((16, N), BF16)], 0))
            out = dot(mix_ref[...], jnp.concatenate(parts, 1))

            def field(f):
                return [out[8 * f : 8 * f + 8, b * N : (b + 1) * N] for b in range(2)]

            rows = pl.ds(r0, 16)
            for l in range(PATHS):
                high, low = split(jnp.concatenate(field(l), 0))
                m_ref[z, l, rows, 0:N] = high
                m_ref[z, l, rows, N : 2 * N] = low
                within, whole = field(PATHS + l), field(2 * PATHS + l)
                for b in range(2):
                    e2_ref[z, l, pl.ds(r0 + 8 * b, 8)] = run[l] + within[b]
                    run[l] = run[l] + whole[b]
            for l in range(LINES):
                q_ref[z, l, rows, :] = jnp.concatenate(field(3 * PATHS + l), 0)
        for l in range(PATHS):
            beam.put(0, z // PER, 16 * (z % PER) + l, run[l][0:1])

    def unmix(z):
        wide = 8 * ELEMENTS
        for r0 in range(0, N, 16):
            highs, lows = [], []
            for b in range(2):
                rows = pl.ds(r0 + 8 * b, 8)
                w = w_ref[z, :, rows, :].reshape(8 * LINES, N)
                along_x, along_y = vx_ref[z, :, rows, :], vy_ref[z, :, rows, :]
                both = (along_x[0:LINES] + along_y[0:LINES]).reshape(8 * LINES, N)
                high, low = split(jnp.concatenate([w, both, along_x[LINES], along_y[LINES]], 0))
                highs.append(high)
                lows.append(low)
            one = dot(unmix_ref[...], jnp.concatenate(highs, 1))
            two = dot(unmix_ref[0:wide], jnp.concatenate(lows, 1))
            out = one[0:wide] + (one[wide:] + two)
            for b in range(2):
                rows = pl.ds(r0 + 8 * b, 8)
                new = c_ref[:, z, rows, :] - out[:, b * N : (b + 1) * N].reshape(ELEMENTS, 8, N)
                d_ref[:, z, rows, :] = new

    def stacked(ref, z, fields):
        value = [ref[z, f] for f in fields]
        high = jnp.concatenate([v[:, 0:N] for v in value], 1)
        low = jnp.concatenate([v[:, N : 2 * N] for v in value], 1)
        return jnp.concatenate([high, low], 0)

    def prefixes(g):
        acc = jnp.zeros((N, N), F32)
        for z in members(g):
            out = dot(m_ref[z].reshape(PATHS * N, 2 * N), up_ref[...])
            for l in range(PATHS):
                part = out[l * N : (l + 1) * N]
                e1_ref[z, l] = part[:, 0:N]
                acc = jnp.where(lane == 16 * (z % PER) + l, part[:, N : 2 * N], acc)
        dsend[0, g] = acc.T[0:ROWS]

    def suffixes(z):
        for l in range(0, LINES, 2):
            over_x = dot(right_ref[...], stacked(p2_ref, z, (l, l + 1)))
            vx_ref[z, l] = over_x[:, 0:N]
            vx_ref[z, l + 1] = over_x[:, N : 2 * N]
        vx_ref[z, LINES] = dot(right_ref[...], stacked(p2_ref, z, (LINES,)))

    def counts(g, enter_x, enter_y):
        rows_ref[g] = enter_x
        turn_over(g, enter_y)
        acc = jnp.zeros((N, N), F32)
        for z in members(g):
            first = 16 * (z % PER)
            k = first + LINES
            tin1 = jnp.exp2(e2_ref[z, LINES] + rows_ref[g, k : k + 1])
            tin2 = jnp.exp2(e1_ref[z, LINES] + spread(g, k, 1)[0])
            for l in range(LINES):
                k = first + l
                if l % 2 == 0:
                    cols = spread(g, k, 2)
                a1 = tin1 * jnp.exp2(e1_ref[z, l] + cols[l % 2])
                a2 = tin2 * jnp.exp2(e2_ref[z, l] + rows_ref[g, k : k + 1])
                a1_ref[z, l] = a1
                a2_ref[z, l] = a2
                q = q_ref[z, l]
                beam.put(1, g, k, step_x * row_sum(q * a1))
                acc = jnp.where(lane == k, jnp.sum(q * a2, 1, keepdims=True), acc)
        dsend[1, g] = step_y * acc.T[0:ROWS]

    def residuals(g, pred1, pred2):
        res1 = lx_ref[g] * (pred1 - mx_ref[g])
        res2 = ly_ref[g] * (pred2 - my_ref[g])
        sum1 = res1 * bsend[1, g] / step_x
        sum2 = res2 * dsend[1, g] / step_y
        rows_ref[g] = res1
        turn_over(g, res2)

        def keep(ref, z, f, value):
            high, low = split(value)
            ref[z, f, :, 0:N] = high
            ref[z, f, :, N : 2 * N] = low

        acc = jnp.zeros((N, N), F32)
        for z in members(g):
            all1 = jnp.zeros((N, N), F32)
            all2 = jnp.zeros((N, N), F32)
            for l in range(LINES):
                k = 16 * (z % PER) + l
                if l % 2 == 0:
                    cols = spread(g, k, 2)
                w1 = a1_ref[z, l] * rows_ref[g, k : k + 1]
                w2 = a2_ref[z, l] * cols[l % 2]
                w_ref[z, l] = w1 + w2
                q = q_ref[z, l]
                p1, p2 = q * w1, q * w2
                all1, all2 = all1 + p1, all2 + p2
                tx_ref[g, k : k + 1] = row_sum(p2)
                keep(p1_ref, z, l, p1)
                keep(p2_ref, z, l, p2)
            keep(p1_ref, z, LINES, all2)
            keep(p2_ref, z, LINES, all1)
            out = dot(p1_ref[z].reshape(PATHS * N, 2 * N), down_ref[...])
            for l in range(PATHS):
                part = out[l * N : (l + 1) * N]
                vy_ref[z, l] = part[:, 0:N]
                if l < LINES:
                    acc = jnp.where(lane == 16 * (z % PER) + l, part[:, N : 2 * N], acc)
        ty_ref[g] = acc.T[0:ROWS]
        for z in range(PER):
            k, part = 16 * z + LINES, slice(16 * z, 16 * (z + 1))
            tx_ref[g, k : k + 1] = jnp.sum(sum1[part], 0, keepdims=True)
            ty_ref[g, k : k + 1] = jnp.sum(sum2[part], 0, keepdims=True)
        bsend[2, g] = dot(wcx_ref[...], rows_of(tx_ref[g]))
        dsend[2, g] = dot(wcy_ref[...], rows_of(ty_ref[g]))

    def store(z):
        return pltpu.make_async_copy(d_ref.at[:, z], out_hbm.at[:, z], conc_sems.at[z])

    def end(g, after_x, after_y):
        for z in range(PER):
            dx_ref[g * PER + z] = after_x[16 * z : 16 * (z + 1)]
            dy_ref[g * PER + z] = after_y[16 * z : 16 * (z + 1)]

    def renew(g, after_x, after_y):
        rows_ref[g] = after_x
        turn_over(g, after_y)
        for z in members(g):
            for e in range(ELEMENTS):
                k = 16 * (z % PER) + e
                if e % 2 == 0:
                    cols = spread(g, k, 2)
                c_ref[e, z] = d_ref[e, z] + rows_ref[g, k : k + 1] + cols[e % 2]

    def each(stage, g):
        for z in members(g):
            stage(z)

    def opening(g):
        each(mix, g)
        prefixes(g)

    for z in range(ZS):
        conc_load(z).wait()
    opening(0)
    pl.semaphore_wait(barrier, greeted)
    send_off(0, 0)

    def turn(step, carry):
        last = step == STEPS - 1
        more = jnp.logical_not(last)
        each(mix, 1)
        pass_on(0, 0, "earlier")
        prefixes(1)
        send_off(0, 1)
        counts(0, *take(0, 0))
        send_off(1, 0)
        pass_on(0, 1, "earlier")
        pass_on(1, 0, "sum")
        counts(1, *take(0, 1))
        send_off(1, 1)
        residuals(0, *take(1, 0))
        send_off(2, 0)
        pass_on(1, 1, "sum")
        each(suffixes, 0)
        pass_on(2, 0, "later")
        residuals(1, *take(1, 1))
        send_off(2, 1)
        each(unmix, 0)

        @pl.when(last)
        def leave():
            for z in members(0):
                store(z).start()

        after = take(2, 0)

        @pl.when(more)
        def again():
            renew(0, *after)
            opening(0)
            send_off(0, 0)

        @pl.when(last)
        def part():
            end(0, *after)

        pass_on(2, 1, "later")
        each(suffixes, 1)
        each(unmix, 1)

        @pl.when(last)
        def leave_too():
            for z in members(1):
                store(z).start()

        rest = take(2, 1)

        @pl.when(more)
        def once_more():
            renew(1, *rest)

        @pl.when(last)
        def finish():
            end(1, *rest)
            for z in range(ZS):
                store(z).wait()

        return carry

    lax.fori_loop(0, STEPS, turn, 0)


def close(c_hbm, dx_hbm, dy_hbm, out_hbm, c_ref, dx_ref, dy_ref, sems):
    loads = [pltpu.make_async_copy(a, b, sems.at[k]) for k, (a, b) in enumerate(((dx_hbm, dx_ref), (dy_hbm, dy_ref)))]
    loads += [pltpu.make_async_copy(c_hbm.at[:, z], c_ref.at[:, z], sems.at[2 + z]) for z in range(ZS)]
    for load in loads:
        load.start()
    loads[0].wait()
    loads[1].wait()
    stores = []
    for z in range(ZS):
        cols = jnp.concatenate([dy_ref[z], jnp.zeros((N - 16, N), F32)], 0).T
        loads[2 + z].wait()
        for e in range(ELEMENTS):
            c_ref[e, z] = c_ref[e, z] + dx_ref[z, e : e + 1] + cols[:, e : e + 1]
        stores.append(pltpu.make_async_copy(c_ref.at[:, z], out_hbm.at[:, z], sems.at[2 + z]))
        stores[z].start()
    for store in stores:
        store.wait()


def solution(mesh):
    beams, dets = mesh.shape["beam"], mesh.shape["det"]

    def shards(conc, inc, sig, yld, rate, axis, m1, live1, m2, live2):
        step_x = 1.0 / (conc.shape[2] * beams)
        step_y = 1.0 / (conc.shape[3] * dets)

        def body(*refs):
            kernel(beams, dets, step_x, step_y, *refs)

        def exchange(count):
            def rows(*slots):
                return pltpu.VMEM((3, GROUPS) + slots + (ROWS, N), F32)

            sems = pltpu.SemaphoreType.DMA((3, GROUPS, 2, 2))
            return [rows(), rows(count // AHEAD), rows(2), rows(AHEAD), sems]

        def grouped(rows):
            return pltpu.VMEM((GROUPS, rows, N), F32)

        field = (N, N)
        anywhere = pl.BlockSpec(memory_space=pl.ANY)
        vmem = pl.BlockSpec(memory_space=pltpu.VMEM)
        small = (axis[None], inc, sig, yld, rate[None], m1, live1, m2, live2)
        inner, dx, dy = pl.pallas_call(
            body,
            out_shape=[
                jax.ShapeDtypeStruct(conc.shape, F32),
                jax.ShapeDtypeStruct((ZS, 16, N), F32),
                jax.ShapeDtypeStruct((ZS, 16, N), F32),
            ],
            in_specs=[anywhere] * (len(small) + 1),
            out_specs=[anywhere, vmem, vmem],
            scratch_shapes=[
                *[pltpu.VMEM(a.shape, a.dtype) for a in small + (conc,)],
                pltpu.SemaphoreType.DMA((len(small),)),
                pltpu.SemaphoreType.DMA((ZS,)),
                pltpu.VMEM((ZS, PATHS, N, 2 * N), BF16),
                pltpu.VMEM((ZS, LINES) + field, F32),
                *[pltpu.VMEM((ZS, LINES + 1) + field, F32)] * 2,
                *[pltpu.VMEM((ZS, LINES) + field, F32)] * 3,
                *[pltpu.VMEM((ZS, LINES + 1, N, 2 * N), BF16)] * 2,
                *[pltpu.VMEM((ZS, PATHS) + field, F32)] * 2,
                pltpu.VMEM(conc.shape, F32),
                grouped(ROWS),
                pltpu.VMEM((GROUPS, N, N), BF16),
                pltpu.VMEM((N, ROWS * N), BF16),
                *[grouped(ROWS)] * 4,
                *[grouped(ROWS)] * 2,
                pltpu.VMEM((64, N), F32),
                pltpu.VMEM((32, N), F32),
                pltpu.VMEM((8 * FIELDS, 2 * N), BF16),
                pltpu.VMEM((16 * ELEMENTS, 8 * PARTS), BF16),
                *[pltpu.VMEM((2 * N, 2 * N), BF16)] * 2,
                pltpu.VMEM((N, 2 * N), BF16),
                *[pltpu.VMEM((ROWS, 3 * N), BF16)] * 2,
                *exchange(beams),
                *exchange(dets),
            ],
            compiler_params=pltpu.CompilerParams(
                collective_id=0, has_side_effects=True, vmem_limit_bytes=64 * 1024 * 1024
            ),
        )(*small, conc)

        return pl.pallas_call(
            close,
            out_shape=jax.ShapeDtypeStruct(conc.shape, F32),
            in_specs=[anywhere] * 3,
            out_specs=anywhere,
            scratch_shapes=[
                pltpu.VMEM(conc.shape, F32),
                *[pltpu.VMEM((ZS, 16, N), F32)] * 2,
                pltpu.SemaphoreType.DMA((2 + ZS,)),
            ],
            compiler_params=pltpu.CompilerParams(vmem_limit_bytes=64 * 1024 * 1024),
        )(inner, dx, dy)

    in_specs = (
        P(None, None, "beam", "det"),
        P(),
        P(),
        P(),
        P(),
        P(),
        P(None, None, "det"),
        P(None, "det"),
        P(None, None, "beam"),
        P(None, "beam"),
    )
    out_specs = P(None, None, "beam", "det")
    return jax.shard_map(shards, mesh=mesh, in_specs=in_specs, out_specs=out_specs, check_vma=False)
```

```python
import math

import jax
import jax.numpy as jnp
from jax import lax
from jax.experimental import pallas as pl
from jax.experimental.pallas import tpu as pltpu
from jax.sharding import PartitionSpec as P

STEPS = 2
HIGH = lax.Precision.HIGHEST
MESH = pl.DeviceIdType.MESH
F32 = jnp.float32
BF16 = jnp.bfloat16
ELEMENTS = 10
LINES = 12
ZS = 4
N = 128
PATHS = LINES + 1
FIELDS = 3 * PATHS + LINES
AHEAD = 4
PARTS = 2 * LINES + 2
GROUPS = 2
PER = ZS // GROUPS
ROWS = 16 * PER
SIZES = (ROWS, LINES * PER, LINES * PER)
LOG2E = math.log2(math.e)


def split(value):
    high = value.astype(BF16)
    return high, (value - high.astype(F32)).astype(BF16)


def iota(shape, dim):
    return lax.broadcasted_iota(jnp.int32, shape, dim)


def dot(a, b):
    return jnp.dot(a, b, preferred_element_type=F32)


def exact(a, b):
    return jnp.dot(a, b, preferred_element_type=F32, precision=HIGH)


def exact_nt(a, b):
    return lax.dot_general(
        a, b, (((1,), (1,)), ((), ())), preferred_element_type=F32, precision=HIGH
    )


def triple(table):
    high, low = split(table)
    return jnp.concatenate([high, high, low], 1)


def rows_of(value):
    high, low = split(jnp.concatenate([value, jnp.zeros((-value.shape[0] % 128, value.shape[1]), F32)], 0))
    return jnp.concatenate([high, low, high], 0)


def one_hot(condition):
    return jnp.where(condition, 1.0, 0.0).astype(F32)


def spot(z, k):
    return PER * k + z % PER


class Ring:
    def __init__(self, axis, count, send, near, out, far, sems):
        self.axis, self.count = axis, count
        self.send, self.near, self.out, self.far, self.sems = send, near, out, far, sems
        self.slots = count // AHEAD
        self.cores = self.slots // 2
        me = lax.axis_index(axis)
        self.c = lax.rem(me, self.cores)
        self.x = lax.rem(me // self.cores, AHEAD)
        self.y = me // (self.cores * AHEAD)
        self.slot = self.y * self.cores + self.c

    def index(self, y, x, c):
        return (y * AHEAD + x) * self.cores + c

    def near_peers(self):
        slots = [lax.rem(self.slot + d, self.slots) for d in ((2, 1, 3) if self.slots == 4 else (1,))]
        return [self.index(k // self.cores, self.x, lax.rem(k, self.cores)) for k in slots]

    def far_peers(self):
        return [(d, self.index(self.y, lax.rem(self.x + d, AHEAD), self.c)) for d in (2, 1, 3)]

    def greet(self, barrier):
        peers = self.near_peers() + [peer for _, peer in self.far_peers()]
        for peer in peers:
            pl.semaphore_signal(barrier, inc=1, device_id={self.axis: peer}, device_id_type=MESH)
        return len(peers)

    def copy(self, src, dst, phase, g, leg, peer):
        return pltpu.make_async_remote_copy(
            src_ref=src,
            dst_ref=dst,
            send_sem=self.sems.at[phase, g, leg, 0],
            recv_sem=self.sems.at[phase, g, leg, 1],
            device_id={self.axis: peer},
            device_id_type=MESH,
        )

    def start(self, phase, g):
        rows = pl.ds(0, SIZES[phase])
        for peer in self.near_peers():
            src, dst = self.send.at[phase, g, rows], self.near.at[phase, g, self.slot, rows]
            self.copy(src, dst, phase, g, 0, peer).start()
        self.near[phase, g, pl.ds(self.slot, 1), rows] = self.send[phase, g, rows][None]

    def wait(self, ref, phase, g, leg, count):
        some = ref.at[phase, g, pl.ds(0, count), pl.ds(0, SIZES[phase])]
        whole = self.copy(some, some, phase, g, leg, self.near_peers()[0])
        whole.wait_send()
        whole.wait_recv()

    def middle(self, phase, g, mode):
        self.wait(self.near, phase, g, 0, self.slots - 1)
        rows = pl.ds(0, SIZES[phase])
        have = [[self.near[phase, g, y * self.cores + c, rows] for c in range(self.cores)] for y in range(2)]
        sums = [sum(cores[1:], cores[0]) for cores in have]
        if mode == "sum":
            mine = sums[0] + sums[1]
            self.out[phase, g, 0, rows] = mine
        else:
            earlier = mode == "earlier"

            def chosen(other, own):
                return (other < own if earlier else other > own).astype(F32)

            base = sum(sums[y] * chosen(y, self.y) for y in range(2))
            same = sum(sums[y] * (self.y == y).astype(F32) for y in range(2))
            mine = base
            for y in range(2):
                for c in range(self.cores):
                    mine = mine + have[y][c] * ((self.y == y).astype(F32) * chosen(c, self.c))
            self.out[phase, g, 0, rows] = base
            self.out[phase, g, 1, rows] = base + same
        for d, peer in self.far_peers():
            wrap = (self.x + d) // AHEAD
            which = {"sum": 0, "earlier": 1 - wrap, "later": wrap}[mode]
            src, dst = self.out.at[phase, g, which, rows], self.far.at[phase, g, self.x, rows]
            self.copy(src, dst, phase, g, 1, peer).start()
        self.far[phase, g, pl.ds(self.x, 1), rows] = mine[None]

    def finish(self, phase, g):
        self.wait(self.far, phase, g, 1, AHEAD - 1)
        far = [self.far[phase, g, x, pl.ds(0, SIZES[phase])] for x in range(AHEAD)]
        return (far[0] + far[1]) + (far[2] + far[3])

    def put(self, phase, g, row, value):
        self.send[phase, g, row : row + 1, :] = value


def kernel(
    beams, dets, step_x, step_y,
    axis_hbm, inc_hbm, sig_hbm, yld_hbm, rate_hbm, m1_hbm, live1_hbm, m2_hbm, live2_hbm, conc_hbm,
    out_hbm, dx_ref, dy_ref,
    axis_ref, inc_ref, sig_ref, yld_ref, rate_ref, m1_ref, live1_ref, m2_ref, live2_ref, c_ref,
    load_sems, conc_sems,
    m_ref, q_ref, e1_ref, e2_ref, a1_ref, a2_ref, w_ref, p1_ref, p2_ref, vx_ref, vy_ref, d_ref, rows_ref, cols_ref, spread_ref,
    mx_ref, my_ref, lx_ref, ly_ref,
    tx_ref, ty_ref, tab_ref, back_ref, mix_ref, unmix_ref, up_ref, down_ref, right_ref,
    wcx_ref, wcy_ref,
    bsend, bnear, bout, bfar, bsems, dsend, dnear, dout, dfar, dsems,
):
    def conc_load(z):
        return pltpu.make_async_copy(conc_hbm.at[:, z], c_ref.at[:, z], conc_sems.at[z])

    hbm = (axis_hbm, inc_hbm, sig_hbm, yld_hbm, rate_hbm, m1_hbm, live1_hbm, m2_hbm, live2_hbm)
    vmem = (axis_ref, inc_ref, sig_ref, yld_ref, rate_ref, m1_ref, live1_ref, m2_ref, live2_ref)
    loads = [pltpu.make_async_copy(a, b, load_sems.at[k]) for k, (a, b) in enumerate(zip(hbm, vmem))]
    for load in [conc_load(z) for z in range(ZS)] + loads:
        load.start()
    beam = Ring("beam", beams, bsend, bnear, bout, bfar, bsems)
    det = Ring("det", dets, dsend, dnear, dout, dfar, dsems)
    barrier = pltpu.get_barrier_semaphore()
    greeted = det.greet(barrier) + beam.greet(barrier)

    for ref in (bsend, dsend, mx_ref, my_ref, lx_ref, ly_ref, tx_ref, ty_ref, tab_ref, back_ref):
        ref[...] = jnp.zeros(ref.shape, F32)

    lane = iota((N, N), 1)

    def members(g):
        return range(g * PER, (g + 1) * PER)

    def send_off(phase, g):
        det.start(phase, g)
        beam.start(phase, g)

    def pass_on(phase, g, mode):
        det.middle(phase, g, mode)
        beam.middle(phase, g, mode)

    def take(phase, g):
        across = det.finish(phase, g)
        return beam.finish(phase, g), across

    def turn_over(g, rows):
        rows = jnp.concatenate([rows, jnp.zeros((ROWS - rows.shape[0], N), F32)], 0) if rows.shape[0] < ROWS else rows
        high = rows.astype(BF16).astype(F32)
        rest = rows - high
        middle = rest.astype(BF16).astype(F32)
        parts = [high, middle, rest - middle, jnp.zeros((N - 3 * ROWS, N), F32)]
        cols_ref[g] = jnp.concatenate(parts, 0).T.astype(BF16)

    def spread(g, z, k, count):
        k += 16 * (z % PER)
        out = dot(cols_ref[g], spread_ref[:, k * N : (k + count) * N])
        return [out[:, n * N : (n + 1) * N] for n in range(count)]

    def row_sum(value):
        return jnp.sum(jnp.sum(value.reshape(N // 8, 8, N), 0), 0, keepdims=True)

    for load in loads:
        load.wait()

    def tables():
        first = axis_ref[0:1, 0:1] == 0
        one, two = inc_ref[0:1, :], inc_ref[1:2, :]
        s1 = jnp.where(first, one, two)
        s2 = jnp.where(first, two, one)
        scale = -LOG2E * step_y
        sig, yld, rate = sig_ref[...], yld_ref[...], rate_ref[...]
        cols = pl.ds(0, ELEMENTS)
        tab_ref[0:LINES, cols] = scale * sig
        tab_ref[LINES:PATHS, cols] = scale * s2
        for k in (PATHS, 2 * PATHS):
            tab_ref[k : k + LINES, cols] = -LOG2E * step_x * sig
            tab_ref[k + LINES : k + PATHS, cols] = -LOG2E * step_x * s1
        tab_ref[3 * PATHS : FIELDS, cols] = yld
        back_ref[0:LINES, cols] = yld * rate
        back_ref[LINES : 2 * LINES, cols] = -sig * rate
        back_ref[2 * LINES : 2 * LINES + 1, cols] = -s1 * rate
        back_ref[2 * LINES + 1 : 2 * LINES + 2, cols] = -s2 * rate

        tab, back = tab_ref[...], back_ref[...]
        wide = 8 * ELEMENTS
        pick = one_hot((iota((8 * FIELDS, 64), 0) >> 3) == iota((8 * FIELDS, 64), 1))
        col = iota((N, 256), 1)
        part = (col >= wide).astype(jnp.int32) + (col >= 2 * wide).astype(jnp.int32)
        spread = one_hot(((col - wide * part) >> 3) == iota((N, 256), 0))
        spread = jnp.where(col < 3 * wide, spread, 0.0)
        full = exact(pick, exact(tab, spread))
        shape = (8 * FIELDS, 256)
        field, gap = iota(shape, 0) >> 3, (iota(shape, 0) & 7) - (iota(shape, 1) & 7)
        within = (field >= PATHS) & (field < 2 * PATHS)
        whole = (field >= 2 * PATHS) & (field < 3 * PATHS)
        full = jnp.where(whole | (within & (gap > 0)) | ((gap == 0) & jnp.logical_not(within)), full, 0.0)
        high, low = split(full)
        part = iota(shape, 1)
        mix_ref[...] = jnp.where((part >= wide) & (part < 2 * wide), low.astype(F32), high.astype(F32)).astype(BF16)

        pick = one_hot((iota((wide, N), 0) >> 3) == iota((wide, N), 1))
        shape = (wide, 8 * PARTS)
        spread = one_hot((iota((32, 8 * PARTS), 1) >> 3) == iota((32, 8 * PARTS), 0))
        full = exact(exact_nt(pick, back), spread)
        full = jnp.where((iota(shape, 0) & 7) == (iota(shape, 1) & 7), full, 0.0)
        high, low = split(full)
        unmix_ref[0:wide] = high
        unmix_ref[wide : 2 * wide] = low

        r, m = iota((16 * PER, 32), 0) & 15, iota((16 * PER, 32), 1)
        sums_x = exact(one_hot(m == jnp.where(r < LINES, r + LINES, 2 * LINES)), back)
        sums_y = exact(one_hot(m == jnp.where(r < LINES, r + LINES, 2 * LINES + 1)), back)
        r = iota((16 * PER, N), 0) & 15
        sums_x = jnp.where(r <= LINES, -step_x * sums_x, 0.0)
        sums_y = jnp.where(r <= LINES, -step_y * sums_y, 0.0)

        shape = (ROWS, N)
        place = one_hot(((iota(shape, 0) // PER) == iota(shape, 1)) & (iota(shape, 1) < ELEMENTS))
        same = (iota(shape, 0) & (PER - 1)) == (iota(shape, 1) >> 4)
        fill = jnp.zeros((N - ROWS, N), F32)
        for ref, sums in ((wcx_ref, sums_x), (wcy_ref, sums_y)):
            ref[...] = triple(jnp.where(same, exact_nt(place, jnp.concatenate([sums, fill], 0)), 0.0))
        shape = spread_ref.shape
        k = iota(shape, 0)
        wanted = iota(shape, 1) >> 7
        wanted = PER * (wanted & 15) + (wanted >> 4)
        spread_ref[...] = one_hot((k < 3 * ROWS) & ((k & (ROWS - 1)) == wanted)).astype(BF16)

        r, c = iota((2 * N, N), 0) & (N - 1), iota((2 * N, N), 1)
        ones = jnp.ones((2 * N, N), F32)
        up_ref[...] = jnp.concatenate([one_hot(r < c), ones], 1).astype(BF16)
        down_ref[...] = jnp.concatenate([step_y * one_hot(r > c), ones], 1).astype(BF16)
        r, c = iota((N, 2 * N), 0), iota((N, 2 * N), 1) & (N - 1)
        right_ref[...] = (step_x * one_hot(c > r)).astype(BF16)
        for z in range(ZS):
            live1 = live1_ref[z : z + 1, :].astype(F32)
            live2 = live2_ref[z : z + 1, :].astype(F32)
            for l in range(LINES):
                g, k = z // PER, spot(z, l)
                lx_ref[g, k : k + 1, :] = live1
                ly_ref[g, k : k + 1, :] = live2
                mx_ref[g, k : k + 1, :] = m1_ref[l, z : z + 1, :]
                my_ref[g, k : k + 1, :] = m2_ref[l, z : z + 1, :]

    tables()

    def mix(z):
        run = [jnp.zeros((8, N), F32)] * PATHS
        for r0 in range(0, N, 16):
            parts = []
            for b in range(2):
                high, low = split(c_ref[:, z, pl.ds(r0 + 8 * b, 8), :].reshape(8 * ELEMENTS, N))
                parts.append(jnp.concatenate([high, high, low, jnp.zeros((16, N), BF16)], 0))
            out = dot(mix_ref[...], jnp.concatenate(parts, 1))

            def field(f):
                return [out[8 * f : 8 * f + 8, b * N : (b + 1) * N] for b in range(2)]

            rows = pl.ds(r0, 16)
            for l in range(PATHS):
                high, low = split(jnp.concatenate(field(l), 0))
                m_ref[z, l, rows, 0:N] = high
                m_ref[z, l, rows, N : 2 * N] = low
                within, whole = field(PATHS + l), field(2 * PATHS + l)
                for b in range(2):
                    e2_ref[z, l, pl.ds(r0 + 8 * b, 8)] = run[l] + within[b]
                    run[l] = run[l] + whole[b]
            for l in range(LINES):
                q_ref[z, l, rows, :] = jnp.concatenate(field(3 * PATHS + l), 0)
        for l in range(PATHS):
            beam.put(0, z // PER, spot(z, l), run[l][0:1])

    def unmix(z):
        wide = 8 * ELEMENTS
        for r0 in range(0, N, 16):
            highs, lows = [], []
            for b in range(2):
                rows = pl.ds(r0 + 8 * b, 8)
                w = w_ref[z, :, rows, :].reshape(8 * LINES, N)
                along_x, along_y = vx_ref[z, :, rows, :], vy_ref[z, :, rows, :]
                both = (along_x[0:LINES] + along_y[0:LINES]).reshape(8 * LINES, N)
                high, low = split(jnp.concatenate([w, both, along_x[LINES], along_y[LINES]], 0))
                highs.append(high)
                lows.append(low)
            one = dot(unmix_ref[...], jnp.concatenate(highs, 1))
            two = dot(unmix_ref[0:wide], jnp.concatenate(lows, 1))
            out = one[0:wide] + (one[wide:] + two)
            for b in range(2):
                rows = pl.ds(r0 + 8 * b, 8)
                new = c_ref[:, z, rows, :] - out[:, b * N : (b + 1) * N].reshape(ELEMENTS, 8, N)
                d_ref[:, z, rows, :] = new

    def stacked(ref, z, fields):
        value = [ref[z, f] for f in fields]
        high = jnp.concatenate([v[:, 0:N] for v in value], 1)
        low = jnp.concatenate([v[:, N : 2 * N] for v in value], 1)
        return jnp.concatenate([high, low], 0)

    def prefixes(g):
        acc = jnp.zeros((N, N), F32)
        for z in members(g):
            out = dot(m_ref[z].reshape(PATHS * N, 2 * N), up_ref[...])
            for l in range(PATHS):
                part = out[l * N : (l + 1) * N]
                e1_ref[z, l] = part[:, 0:N]
                acc = jnp.where(lane == spot(z, l), part[:, N : 2 * N], acc)
        dsend[0, g] = acc.T[0:ROWS]

    def suffixes(z):
        for l in range(0, LINES, 2):
            over_x = dot(right_ref[...], stacked(p2_ref, z, (l, l + 1)))
            vx_ref[z, l] = over_x[:, 0:N]
            vx_ref[z, l + 1] = over_x[:, N : 2 * N]
        vx_ref[z, LINES] = dot(right_ref[...], stacked(p2_ref, z, (LINES,)))

    def counts(g, enter_x, enter_y):
        rows_ref[g] = enter_x
        turn_over(g, enter_y)
        acc = jnp.zeros((N, N), F32)
        for z in members(g):
            k = spot(z, LINES)
            tin1 = jnp.exp2(e2_ref[z, LINES] + rows_ref[g, k : k + 1])
            tin2 = jnp.exp2(e1_ref[z, LINES] + spread(g, z, LINES, 1)[0])
            for l in range(LINES):
                k = spot(z, l)
                if l % 2 == 0:
                    cols = spread(g, z, l, 2)
                a1 = tin1 * jnp.exp2(e1_ref[z, l] + cols[l % 2])
                a2 = tin2 * jnp.exp2(e2_ref[z, l] + rows_ref[g, k : k + 1])
                a1_ref[z, l] = a1
                a2_ref[z, l] = a2
                q = q_ref[z, l]
                beam.put(1, g, k, step_x * row_sum(q * a1))
                acc = jnp.where(lane == k, jnp.sum(q * a2, 1, keepdims=True), acc)
        dsend[1, g] = step_y * acc.T[0:ROWS]

    def residuals(g, pred1, pred2):
        used = pl.ds(0, LINES * PER)
        res1 = lx_ref[g, used] * (pred1 - mx_ref[g, used])
        res2 = ly_ref[g, used] * (pred2 - my_ref[g, used])
        sum1 = res1 * bsend[1, g, used] / step_x
        sum2 = res2 * dsend[1, g, used] / step_y
        rows_ref[g, used] = res1
        turn_over(g, res2)

        def keep(ref, z, f, value):
            high, low = split(value)
            ref[z, f, :, 0:N] = high
            ref[z, f, :, N : 2 * N] = low

        acc = jnp.zeros((N, N), F32)
        for z in members(g):
            all1 = jnp.zeros((N, N), F32)
            all2 = jnp.zeros((N, N), F32)
            for l in range(LINES):
                k = 16 * (z % PER) + l
                if l % 2 == 0:
                    cols = spread(g, z, l, 2)
                w1 = a1_ref[z, l] * rows_ref[g, spot(z, l) : spot(z, l) + 1]
                w2 = a2_ref[z, l] * cols[l % 2]
                w_ref[z, l] = w1 + w2
                q = q_ref[z, l]
                p1, p2 = q * w1, q * w2
                all1, all2 = all1 + p1, all2 + p2
                tx_ref[g, k : k + 1] = row_sum(p2)
                keep(p1_ref, z, l, p1)
                keep(p2_ref, z, l, p2)
            keep(p1_ref, z, LINES, all2)
            keep(p2_ref, z, LINES, all1)
            out = dot(p1_ref[z].reshape(PATHS * N, 2 * N), down_ref[...])
            for l in range(PATHS):
                part = out[l * N : (l + 1) * N]
                vy_ref[z, l] = part[:, 0:N]
                if l < LINES:
                    acc = jnp.where(lane == 16 * (z % PER) + l, part[:, N : 2 * N], acc)
        ty_ref[g] = acc.T[0:ROWS]
        for z in range(PER):
            k = 16 * z + LINES
            own = (iota((LINES * PER, N), 0) & (PER - 1)) == z
            tx_ref[g, k : k + 1] = jnp.sum(jnp.where(own, sum1, 0.0), 0, keepdims=True)
            ty_ref[g, k : k + 1] = jnp.sum(jnp.where(own, sum2, 0.0), 0, keepdims=True)
        bsend[2, g] = dot(wcx_ref[...], rows_of(tx_ref[g]))
        dsend[2, g] = dot(wcy_ref[...], rows_of(ty_ref[g]))

    def store(z):
        return pltpu.make_async_copy(d_ref.at[:, z], out_hbm.at[:, z], conc_sems.at[z])

    def end(g, after_x, after_y):
        dx_ref[g], dy_ref[g] = after_x, after_y

    def renew(g, after_x, after_y):
        rows_ref[g, 0 : SIZES[2]] = after_x
        turn_over(g, after_y)
        for z in members(g):
            for e in range(ELEMENTS):
                k = spot(z, e)
                if e % 2 == 0:
                    cols = spread(g, z, e, 2)
                c_ref[e, z] = d_ref[e, z] + rows_ref[g, k : k + 1] + cols[e % 2]

    def each(stage, g):
        for z in members(g):
            stage(z)

    def opening(g):
        each(mix, g)
        prefixes(g)

    for z in range(ZS):
        conc_load(z).wait()
    opening(0)
    pl.semaphore_wait(barrier, greeted)
    send_off(0, 0)

    def turn(step, carry):
        last = step == STEPS - 1
        more = jnp.logical_not(last)
        each(mix, 1)

        @pl.when(step == 0)
        def late():
            pass_on(0, 0, "earlier")

        prefixes(1)
        send_off(0, 1)
        counts(0, *take(0, 0))
        send_off(1, 0)
        pass_on(0, 1, "earlier")
        pass_on(1, 0, "sum")
        counts(1, *take(0, 1))
        send_off(1, 1)
        residuals(0, *take(1, 0))
        send_off(2, 0)
        pass_on(1, 1, "sum")
        each(suffixes, 0)
        pass_on(2, 0, "later")
        residuals(1, *take(1, 1))
        send_off(2, 1)
        each(unmix, 0)

        @pl.when(last)
        def leave():
            for z in members(0):
                store(z).start()

        after = take(2, 0)

        @pl.when(more)
        def again():
            renew(0, *after)
            opening(0)
            send_off(0, 0)

        @pl.when(last)
        def part():
            end(0, *after)

        pass_on(2, 1, "later")
        each(suffixes, 1)

        @pl.when(more)
        def early():
            pass_on(0, 0, "earlier")

        each(unmix, 1)

        @pl.when(last)
        def leave_too():
            for z in members(1):
                store(z).start()

        rest = take(2, 1)

        @pl.when(more)
        def once_more():
            renew(1, *rest)

        @pl.when(last)
        def finish():
            end(1, *rest)
            for z in range(ZS):
                store(z).wait()

        return carry

    lax.fori_loop(0, STEPS, turn, 0)


def close(c_hbm, dx_hbm, dy_hbm, out_hbm, c_ref, dx_ref, dy_ref, sems):
    loads = [pltpu.make_async_copy(a, b, sems.at[k]) for k, (a, b) in enumerate(((dx_hbm, dx_ref), (dy_hbm, dy_ref)))]
    loads += [pltpu.make_async_copy(c_hbm.at[:, z], c_ref.at[:, z], sems.at[2 + z]) for z in range(ZS)]
    for load in loads:
        load.start()
    loads[0].wait()
    loads[1].wait()
    stores = []
    for z in range(ZS):
        g = z // PER
        cols = jnp.concatenate([dy_ref[g], jnp.zeros((N - SIZES[2], N), F32)], 0).T
        loads[2 + z].wait()
        for e in range(ELEMENTS):
            k = spot(z, e)
            c_ref[e, z] = c_ref[e, z] + dx_ref[g, k : k + 1] + cols[:, k : k + 1]
        stores.append(pltpu.make_async_copy(c_ref.at[:, z], out_hbm.at[:, z], sems.at[2 + z]))
        stores[z].start()
    for store in stores:
        store.wait()


def solution(mesh):
    beams, dets = mesh.shape["beam"], mesh.shape["det"]

    def shards(conc, inc, sig, yld, rate, axis, m1, live1, m2, live2):
        step_x = 1.0 / (conc.shape[2] * beams)
        step_y = 1.0 / (conc.shape[3] * dets)

        def body(*refs):
            kernel(beams, dets, step_x, step_y, *refs)

        def exchange(count):
            def rows(*slots):
                return pltpu.VMEM((3, GROUPS) + slots + (ROWS, N), F32)

            sems = pltpu.SemaphoreType.DMA((3, GROUPS, 2, 2))
            return [rows(), rows(count // AHEAD), rows(2), rows(AHEAD), sems]

        def grouped(rows):
            return pltpu.VMEM((GROUPS, rows, N), F32)

        field = (N, N)
        anywhere = pl.BlockSpec(memory_space=pl.ANY)
        vmem = pl.BlockSpec(memory_space=pltpu.VMEM)
        small = (axis[None], inc, sig, yld, rate[None], m1, live1, m2, live2)
        inner, dx, dy = pl.pallas_call(
            body,
            out_shape=[
                jax.ShapeDtypeStruct(conc.shape, F32),
                jax.ShapeDtypeStruct((GROUPS, SIZES[2], N), F32),
                jax.ShapeDtypeStruct((GROUPS, SIZES[2], N), F32),
            ],
            in_specs=[anywhere] * (len(small) + 1),
            out_specs=[anywhere, vmem, vmem],
            scratch_shapes=[
                *[pltpu.VMEM(a.shape, a.dtype) for a in small + (conc,)],
                pltpu.SemaphoreType.DMA((len(small),)),
                pltpu.SemaphoreType.DMA((ZS,)),
                pltpu.VMEM((ZS, PATHS, N, 2 * N), BF16),
                pltpu.VMEM((ZS, LINES) + field, F32),
                *[pltpu.VMEM((ZS, LINES + 1) + field, F32)] * 2,
                *[pltpu.VMEM((ZS, LINES) + field, F32)] * 3,
                *[pltpu.VMEM((ZS, LINES + 1, N, 2 * N), BF16)] * 2,
                *[pltpu.VMEM((ZS, PATHS) + field, F32)] * 2,
                pltpu.VMEM(conc.shape, F32),
                grouped(ROWS),
                pltpu.VMEM((GROUPS, N, N), BF16),
                pltpu.VMEM((N, ROWS * N), BF16),
                *[grouped(ROWS)] * 4,
                *[grouped(ROWS)] * 2,
                pltpu.VMEM((64, N), F32),
                pltpu.VMEM((32, N), F32),
                pltpu.VMEM((8 * FIELDS, 2 * N), BF16),
                pltpu.VMEM((16 * ELEMENTS, 8 * PARTS), BF16),
                *[pltpu.VMEM((2 * N, 2 * N), BF16)] * 2,
                pltpu.VMEM((N, 2 * N), BF16),
                *[pltpu.VMEM((ROWS, 3 * N), BF16)] * 2,
                *exchange(beams),
                *exchange(dets),
            ],
            compiler_params=pltpu.CompilerParams(
                collective_id=0, has_side_effects=True, vmem_limit_bytes=64 * 1024 * 1024
            ),
        )(*small, conc)

        return pl.pallas_call(
            close,
            out_shape=jax.ShapeDtypeStruct(conc.shape, F32),
            in_specs=[anywhere] * 3,
            out_specs=anywhere,
            scratch_shapes=[
                pltpu.VMEM(conc.shape, F32),
                *[pltpu.VMEM((GROUPS, SIZES[2], N), F32)] * 2,
                pltpu.SemaphoreType.DMA((2 + ZS,)),
            ],
            compiler_params=pltpu.CompilerParams(vmem_limit_bytes=64 * 1024 * 1024),
        )(inner, dx, dy)

    in_specs = (
        P(None, None, "beam", "det"),
        P(),
        P(),
        P(),
        P(),
        P(),
        P(None, None, "det"),
        P(None, "det"),
        P(None, None, "beam"),
        P(None, "beam"),
    )
    out_specs = P(None, None, "beam", "det")
    return jax.shard_map(shards, mesh=mesh, in_specs=in_specs, out_specs=out_specs, check_vma=False)
```

```python
import math

import jax
import jax.numpy as jnp
from jax import lax
from jax.experimental import pallas as pl
from jax.experimental.pallas import tpu as pltpu
from jax.sharding import PartitionSpec as P

STEPS = 2
HIGH = lax.Precision.HIGHEST
MESH = pl.DeviceIdType.MESH
F32 = jnp.float32
BF16 = jnp.bfloat16
ELEMENTS = 10
LINES = 12
ZS = 4
N = 128
PATHS = LINES + 1
FIELDS = 3 * PATHS + LINES
AHEAD = 4
PARTS = 2 * LINES + 2
GROUPS = 2
PER = ZS // GROUPS
ROWS = 16 * PER
SIZES = (ROWS, LINES * PER, LINES * PER)
LOG2E = math.log2(math.e)


def split(value):
    high = value.astype(BF16)
    return high, (value - high.astype(F32)).astype(BF16)


def iota(shape, dim):
    return lax.broadcasted_iota(jnp.int32, shape, dim)


def dot(a, b):
    return jnp.dot(a, b, preferred_element_type=F32)


def exact(a, b):
    return jnp.dot(a, b, preferred_element_type=F32, precision=HIGH)


def exact_nt(a, b):
    return lax.dot_general(
        a, b, (((1,), (1,)), ((), ())), preferred_element_type=F32, precision=HIGH
    )


def triple(table):
    high, low = split(table)
    return jnp.concatenate([high, high, low], 1)


def rows_of(value):
    high, low = split(jnp.concatenate([value, jnp.zeros((-value.shape[0] % 128, value.shape[1]), F32)], 0))
    return jnp.concatenate([high, low, high], 0)


def one_hot(condition):
    return jnp.where(condition, 1.0, 0.0).astype(F32)


def spot(z, k):
    return PER * k + z % PER


class Ring:
    def __init__(self, axis, count, send, near, out, far, sems):
        self.axis, self.count = axis, count
        self.send, self.near, self.out, self.far, self.sems = send, near, out, far, sems
        self.slots = count // AHEAD
        self.cores = self.slots // 2
        me = lax.axis_index(axis)
        self.c = lax.rem(me, self.cores)
        self.x = lax.rem(me // self.cores, AHEAD)
        self.y = me // (self.cores * AHEAD)
        self.slot = self.y * self.cores + self.c

    def index(self, y, x, c):
        return (y * AHEAD + x) * self.cores + c

    def near_peers(self):
        slots = [lax.rem(self.slot + d, self.slots) for d in ((2, 1, 3) if self.slots == 4 else (1,))]
        return [self.index(k // self.cores, self.x, lax.rem(k, self.cores)) for k in slots]

    def far_peers(self):
        return [(d, self.index(self.y, lax.rem(self.x + d, AHEAD), self.c)) for d in (2, 1, 3)]

    def greet(self, barrier):
        peers = self.near_peers() + [peer for _, peer in self.far_peers()]
        for peer in peers:
            pl.semaphore_signal(barrier, inc=1, device_id={self.axis: peer}, device_id_type=MESH)
        return len(peers)

    def copy(self, src, dst, phase, g, leg, peer):
        return pltpu.make_async_remote_copy(
            src_ref=src,
            dst_ref=dst,
            send_sem=self.sems.at[phase, g, leg, 0],
            recv_sem=self.sems.at[phase, g, leg, 1],
            device_id={self.axis: peer},
            device_id_type=MESH,
        )

    def start(self, phase, g):
        rows = pl.ds(0, SIZES[phase])
        for peer in self.near_peers():
            src, dst = self.send.at[phase, g, rows], self.near.at[phase, g, self.slot, rows]
            self.copy(src, dst, phase, g, 0, peer).start()
        self.near[phase, g, pl.ds(self.slot, 1), rows] = self.send[phase, g, rows][None]

    def whole(self, phase, g, leg):
        ref, count = ((self.near, self.slots - 1), (self.far, AHEAD - 1))[leg]
        some = ref.at[phase, g, pl.ds(0, count), pl.ds(0, SIZES[phase])]
        return self.copy(some, some, phase, g, leg, self.near_peers()[0])

    def settle(self, phase, g):
        self.whole(phase, g, 0).wait_send()
        self.whole(phase, g, 1).wait_send()

    def middle(self, phase, g, mode):
        self.whole(phase, g, 0).wait_recv()
        rows = pl.ds(0, SIZES[phase])
        have = [[self.near[phase, g, y * self.cores + c, rows] for c in range(self.cores)] for y in range(2)]
        sums = [sum(cores[1:], cores[0]) for cores in have]
        if mode == "sum":
            mine = sums[0] + sums[1]
            self.out[phase, g, 0, rows] = mine
        else:
            earlier = mode == "earlier"

            def chosen(other, own):
                return (other < own if earlier else other > own).astype(F32)

            base = sum(sums[y] * chosen(y, self.y) for y in range(2))
            same = sum(sums[y] * (self.y == y).astype(F32) for y in range(2))
            mine = base
            for y in range(2):
                for c in range(self.cores):
                    mine = mine + have[y][c] * ((self.y == y).astype(F32) * chosen(c, self.c))
            self.out[phase, g, 0, rows] = base
            self.out[phase, g, 1, rows] = base + same
        for d, peer in self.far_peers():
            wrap = (self.x + d) // AHEAD
            which = {"sum": 0, "earlier": 1 - wrap, "later": wrap}[mode]
            src, dst = self.out.at[phase, g, which, rows], self.far.at[phase, g, self.x, rows]
            self.copy(src, dst, phase, g, 1, peer).start()
        self.far[phase, g, pl.ds(self.x, 1), rows] = mine[None]

    def finish(self, phase, g):
        self.whole(phase, g, 1).wait_recv()
        far = [self.far[phase, g, x, pl.ds(0, SIZES[phase])] for x in range(AHEAD)]
        return (far[0] + far[1]) + (far[2] + far[3])

    def put(self, phase, g, row, value):
        self.send[phase, g, row : row + 1, :] = value


def kernel(
    beams, dets, step_x, step_y,
    axis_hbm, inc_hbm, sig_hbm, yld_hbm, rate_hbm, m1_hbm, live1_hbm, m2_hbm, live2_hbm, conc_hbm,
    out_hbm, dx_ref, dy_ref,
    axis_ref, inc_ref, sig_ref, yld_ref, rate_ref, m1_ref, live1_ref, m2_ref, live2_ref, c_ref,
    load_sems, conc_sems,
    m_ref, q_ref, e1_ref, e2_ref, a1_ref, a2_ref, w_ref, p1_ref, p2_ref, vx_ref, vy_ref, d_ref, rows_ref, cols_ref, spread_ref,
    mx_ref, my_ref, lx_ref, ly_ref,
    tx_ref, ty_ref, tab_ref, back_ref, mix_ref, unmix_ref, up_ref, down_ref, right_ref,
    wcx_ref, wcy_ref,
    bsend, bnear, bout, bfar, bsems, dsend, dnear, dout, dfar, dsems,
):
    def conc_load(z):
        return pltpu.make_async_copy(conc_hbm.at[:, z], c_ref.at[:, z], conc_sems.at[z])

    hbm = (axis_hbm, inc_hbm, sig_hbm, yld_hbm, rate_hbm, m1_hbm, live1_hbm, m2_hbm, live2_hbm)
    vmem = (axis_ref, inc_ref, sig_ref, yld_ref, rate_ref, m1_ref, live1_ref, m2_ref, live2_ref)
    loads = [pltpu.make_async_copy(a, b, load_sems.at[k]) for k, (a, b) in enumerate(zip(hbm, vmem))]
    for load in [conc_load(z) for z in range(ZS)] + loads:
        load.start()
    beam = Ring("beam", beams, bsend, bnear, bout, bfar, bsems)
    det = Ring("det", dets, dsend, dnear, dout, dfar, dsems)
    barrier = pltpu.get_barrier_semaphore()
    greeted = det.greet(barrier) + beam.greet(barrier)

    for ref in (bsend, dsend, mx_ref, my_ref, lx_ref, ly_ref, tx_ref, ty_ref, tab_ref, back_ref):
        ref[...] = jnp.zeros(ref.shape, F32)

    lane = iota((N, N), 1)

    def members(g):
        return range(g * PER, (g + 1) * PER)

    def send_off(phase, g):
        det.start(phase, g)
        beam.start(phase, g)

    def pass_on(phase, g, mode):
        det.middle(phase, g, mode)
        beam.middle(phase, g, mode)

    def settle(phase, g):
        det.settle(phase, g)
        beam.settle(phase, g)

    def take(phase, g):
        across = det.finish(phase, g)
        return beam.finish(phase, g), across

    def turn_over(g, rows):
        rows = jnp.concatenate([rows, jnp.zeros((ROWS - rows.shape[0], N), F32)], 0) if rows.shape[0] < ROWS else rows
        high = rows.astype(BF16).astype(F32)
        rest = rows - high
        middle = rest.astype(BF16).astype(F32)
        parts = [high, middle, rest - middle, jnp.zeros((N - 3 * ROWS, N), F32)]
        cols_ref[g] = jnp.concatenate(parts, 0).T.astype(BF16)

    def spread(g, z, k, count):
        k += 16 * (z % PER)
        out = dot(cols_ref[g], spread_ref[:, k * N : (k + count) * N])
        return [out[:, n * N : (n + 1) * N] for n in range(count)]

    def row_sum(value):
        return jnp.sum(jnp.sum(value.reshape(N // 8, 8, N), 0), 0, keepdims=True)

    for load in loads:
        load.wait()

    def tables():
        first = axis_ref[0:1, 0:1] == 0
        one, two = inc_ref[0:1, :], inc_ref[1:2, :]
        s1 = jnp.where(first, one, two)
        s2 = jnp.where(first, two, one)
        scale = -LOG2E * step_y
        sig, yld, rate = sig_ref[...], yld_ref[...], rate_ref[...]
        cols = pl.ds(0, ELEMENTS)
        tab_ref[0:LINES, cols] = scale * sig
        tab_ref[LINES:PATHS, cols] = scale * s2
        for k in (PATHS, 2 * PATHS):
            tab_ref[k : k + LINES, cols] = -LOG2E * step_x * sig
            tab_ref[k + LINES : k + PATHS, cols] = -LOG2E * step_x * s1
        tab_ref[3 * PATHS : FIELDS, cols] = yld
        back_ref[0:LINES, cols] = yld * rate
        back_ref[LINES : 2 * LINES, cols] = -sig * rate
        back_ref[2 * LINES : 2 * LINES + 1, cols] = -s1 * rate
        back_ref[2 * LINES + 1 : 2 * LINES + 2, cols] = -s2 * rate

        tab, back = tab_ref[...], back_ref[...]
        wide = 8 * ELEMENTS
        pick = one_hot((iota((8 * FIELDS, 64), 0) >> 3) == iota((8 * FIELDS, 64), 1))
        col = iota((N, 256), 1)
        part = (col >= wide).astype(jnp.int32) + (col >= 2 * wide).astype(jnp.int32)
        spread = one_hot(((col - wide * part) >> 3) == iota((N, 256), 0))
        spread = jnp.where(col < 3 * wide, spread, 0.0)
        full = exact(pick, exact(tab, spread))
        shape = (8 * FIELDS, 256)
        field, gap = iota(shape, 0) >> 3, (iota(shape, 0) & 7) - (iota(shape, 1) & 7)
        within = (field >= PATHS) & (field < 2 * PATHS)
        whole = (field >= 2 * PATHS) & (field < 3 * PATHS)
        full = jnp.where(whole | (within & (gap > 0)) | ((gap == 0) & jnp.logical_not(within)), full, 0.0)
        high, low = split(full)
        part = iota(shape, 1)
        mix_ref[...] = jnp.where((part >= wide) & (part < 2 * wide), low.astype(F32), high.astype(F32)).astype(BF16)

        pick = one_hot((iota((wide, N), 0) >> 3) == iota((wide, N), 1))
        shape = (wide, 8 * PARTS)
        spread = one_hot((iota((32, 8 * PARTS), 1) >> 3) == iota((32, 8 * PARTS), 0))
        full = exact(exact_nt(pick, back), spread)
        full = jnp.where((iota(shape, 0) & 7) == (iota(shape, 1) & 7), full, 0.0)
        high, low = split(full)
        unmix_ref[0:wide] = high
        unmix_ref[wide : 2 * wide] = low

        r, m = iota((16 * PER, 32), 0) & 15, iota((16 * PER, 32), 1)
        sums_x = exact(one_hot(m == jnp.where(r < LINES, r + LINES, 2 * LINES)), back)
        sums_y = exact(one_hot(m == jnp.where(r < LINES, r + LINES, 2 * LINES + 1)), back)
        r = iota((16 * PER, N), 0) & 15
        sums_x = jnp.where(r <= LINES, -step_x * sums_x, 0.0)
        sums_y = jnp.where(r <= LINES, -step_y * sums_y, 0.0)

        shape = (ROWS, N)
        place = one_hot(((iota(shape, 0) // PER) == iota(shape, 1)) & (iota(shape, 1) < ELEMENTS))
        same = (iota(shape, 0) & (PER - 1)) == (iota(shape, 1) >> 4)
        fill = jnp.zeros((N - ROWS, N), F32)
        for ref, sums in ((wcx_ref, sums_x), (wcy_ref, sums_y)):
            ref[...] = triple(jnp.where(same, exact_nt(place, jnp.concatenate([sums, fill], 0)), 0.0))
        shape = spread_ref.shape
        k = iota(shape, 0)
        wanted = iota(shape, 1) >> 7
        wanted = PER * (wanted & 15) + (wanted >> 4)
        spread_ref[...] = one_hot((k < 3 * ROWS) & ((k & (ROWS - 1)) == wanted)).astype(BF16)

        r, c = iota((2 * N, N), 0) & (N - 1), iota((2 * N, N), 1)
        ones = jnp.ones((2 * N, N), F32)
        up_ref[...] = jnp.concatenate([one_hot(r < c), ones], 1).astype(BF16)
        down_ref[...] = jnp.concatenate([step_y * one_hot(r > c), ones], 1).astype(BF16)
        r, c = iota((N, 2 * N), 0), iota((N, 2 * N), 1) & (N - 1)
        right_ref[...] = (step_x * one_hot(c > r)).astype(BF16)
        for z in range(ZS):
            live1 = live1_ref[z : z + 1, :].astype(F32)
            live2 = live2_ref[z : z + 1, :].astype(F32)
            for l in range(LINES):
                g, k = z // PER, spot(z, l)
                lx_ref[g, k : k + 1, :] = live1
                ly_ref[g, k : k + 1, :] = live2
                mx_ref[g, k : k + 1, :] = m1_ref[l, z : z + 1, :]
                my_ref[g, k : k + 1, :] = m2_ref[l, z : z + 1, :]

    tables()

    def mix(z):
        run = [jnp.zeros((8, N), F32)] * PATHS
        for r0 in range(0, N, 16):
            parts = []
            for b in range(2):
                high, low = split(c_ref[:, z, pl.ds(r0 + 8 * b, 8), :].reshape(8 * ELEMENTS, N))
                parts.append(jnp.concatenate([high, high, low, jnp.zeros((16, N), BF16)], 0))
            out = dot(mix_ref[...], jnp.concatenate(parts, 1))

            def field(f):
                return [out[8 * f : 8 * f + 8, b * N : (b + 1) * N] for b in range(2)]

            rows = pl.ds(r0, 16)
            for l in range(PATHS):
                high, low = split(jnp.concatenate(field(l), 0))
                m_ref[z, l, rows, 0:N] = high
                m_ref[z, l, rows, N : 2 * N] = low
                within, whole = field(PATHS + l), field(2 * PATHS + l)
                for b in range(2):
                    e2_ref[z, l, pl.ds(r0 + 8 * b, 8)] = run[l] + within[b]
                    run[l] = run[l] + whole[b]
            for l in range(LINES):
                q_ref[z, l, rows, :] = jnp.concatenate(field(3 * PATHS + l), 0)
        for l in range(PATHS):
            beam.put(0, z // PER, spot(z, l), run[l][0:1])

    def unmix(z):
        wide = 8 * ELEMENTS
        for r0 in range(0, N, 16):
            highs, lows = [], []
            for b in range(2):
                rows = pl.ds(r0 + 8 * b, 8)
                w = w_ref[z, :, rows, :].reshape(8 * LINES, N)
                along_x, along_y = vx_ref[z, :, rows, :], vy_ref[z, :, rows, :]
                both = (along_x[0:LINES] + along_y[0:LINES]).reshape(8 * LINES, N)
                high, low = split(jnp.concatenate([w, both, along_x[LINES], along_y[LINES]], 0))
                highs.append(high)
                lows.append(low)
            one = dot(unmix_ref[...], jnp.concatenate(highs, 1))
            two = dot(unmix_ref[0:wide], jnp.concatenate(lows, 1))
            out = one[0:wide] + (one[wide:] + two)
            for b in range(2):
                rows = pl.ds(r0 + 8 * b, 8)
                new = c_ref[:, z, rows, :] - out[:, b * N : (b + 1) * N].reshape(ELEMENTS, 8, N)
                d_ref[:, z, rows, :] = new

    def stacked(ref, z, fields):
        value = [ref[z, f] for f in fields]
        high = jnp.concatenate([v[:, 0:N] for v in value], 1)
        low = jnp.concatenate([v[:, N : 2 * N] for v in value], 1)
        return jnp.concatenate([high, low], 0)

    def prefixes(g):
        acc = jnp.zeros((N, N), F32)
        for z in members(g):
            out = dot(m_ref[z].reshape(PATHS * N, 2 * N), up_ref[...])
            for l in range(PATHS):
                part = out[l * N : (l + 1) * N]
                e1_ref[z, l] = part[:, 0:N]
                acc = jnp.where(lane == spot(z, l), part[:, N : 2 * N], acc)
        dsend[0, g] = acc.T[0:ROWS]

    def suffixes(z):
        for l in range(0, LINES, 2):
            over_x = dot(right_ref[...], stacked(p2_ref, z, (l, l + 1)))
            vx_ref[z, l] = over_x[:, 0:N]
            vx_ref[z, l + 1] = over_x[:, N : 2 * N]
        vx_ref[z, LINES] = dot(right_ref[...], stacked(p2_ref, z, (LINES,)))

    def counts(g, enter_x, enter_y):
        rows_ref[g] = enter_x
        turn_over(g, enter_y)
        acc = jnp.zeros((N, N), F32)
        for z in members(g):
            k = spot(z, LINES)
            tin1 = jnp.exp2(e2_ref[z, LINES] + rows_ref[g, k : k + 1])
            tin2 = jnp.exp2(e1_ref[z, LINES] + spread(g, z, LINES, 1)[0])
            for l in range(LINES):
                k = spot(z, l)
                if l % 2 == 0:
                    cols = spread(g, z, l, 2)
                a1 = tin1 * jnp.exp2(e1_ref[z, l] + cols[l % 2])
                a2 = tin2 * jnp.exp2(e2_ref[z, l] + rows_ref[g, k : k + 1])
                a1_ref[z, l] = a1
                a2_ref[z, l] = a2
                q = q_ref[z, l]
                beam.put(1, g, k, step_x * row_sum(q * a1))
                acc = jnp.where(lane == k, jnp.sum(q * a2, 1, keepdims=True), acc)
        dsend[1, g] = step_y * acc.T[0:ROWS]

    def residuals(g, pred1, pred2):
        used = pl.ds(0, LINES * PER)
        res1 = lx_ref[g, used] * (pred1 - mx_ref[g, used])
        res2 = ly_ref[g, used] * (pred2 - my_ref[g, used])
        sum1 = res1 * bsend[1, g, used] / step_x
        sum2 = res2 * dsend[1, g, used] / step_y
        rows_ref[g, used] = res1
        turn_over(g, res2)

        def keep(ref, z, f, value):
            high, low = split(value)
            ref[z, f, :, 0:N] = high
            ref[z, f, :, N : 2 * N] = low

        acc = jnp.zeros((N, N), F32)
        for z in members(g):
            all1 = jnp.zeros((N, N), F32)
            all2 = jnp.zeros((N, N), F32)
            for l in range(LINES):
                k = 16 * (z % PER) + l
                if l % 2 == 0:
                    cols = spread(g, z, l, 2)
                w1 = a1_ref[z, l] * rows_ref[g, spot(z, l) : spot(z, l) + 1]
                w2 = a2_ref[z, l] * cols[l % 2]
                w_ref[z, l] = w1 + w2
                q = q_ref[z, l]
                p1, p2 = q * w1, q * w2
                all1, all2 = all1 + p1, all2 + p2
                tx_ref[g, k : k + 1] = row_sum(p2)
                keep(p1_ref, z, l, p1)
                keep(p2_ref, z, l, p2)
            keep(p1_ref, z, LINES, all2)
            keep(p2_ref, z, LINES, all1)
            out = dot(p1_ref[z].reshape(PATHS * N, 2 * N), down_ref[...])
            for l in range(PATHS):
                part = out[l * N : (l + 1) * N]
                vy_ref[z, l] = part[:, 0:N]
                if l < LINES:
                    acc = jnp.where(lane == 16 * (z % PER) + l, part[:, N : 2 * N], acc)
        ty_ref[g] = acc.T[0:ROWS]
        for z in range(PER):
            k = 16 * z + LINES
            own = (iota((LINES * PER, N), 0) & (PER - 1)) == z
            tx_ref[g, k : k + 1] = jnp.sum(jnp.where(own, sum1, 0.0), 0, keepdims=True)
            ty_ref[g, k : k + 1] = jnp.sum(jnp.where(own, sum2, 0.0), 0, keepdims=True)
        bsend[2, g] = dot(wcx_ref[...], rows_of(tx_ref[g]))
        dsend[2, g] = dot(wcy_ref[...], rows_of(ty_ref[g]))

    def store(z):
        return pltpu.make_async_copy(d_ref.at[:, z], out_hbm.at[:, z], conc_sems.at[z])

    def end(g, after_x, after_y):
        dx_ref[g], dy_ref[g] = after_x, after_y

    def renew(g, after_x, after_y):
        rows_ref[g, 0 : SIZES[2]] = after_x
        turn_over(g, after_y)
        for z in members(g):
            for e in range(ELEMENTS):
                k = spot(z, e)
                if e % 2 == 0:
                    cols = spread(g, z, e, 2)
                c_ref[e, z] = d_ref[e, z] + rows_ref[g, k : k + 1] + cols[e % 2]

    def each(stage, g):
        for z in members(g):
            stage(z)

    def opening(g):
        each(mix, g)
        prefixes(g)

    for z in range(ZS):
        conc_load(z).wait()
    opening(0)
    pl.semaphore_wait(barrier, greeted)
    send_off(0, 0)

    def turn(step, carry):
        last = step == STEPS - 1
        more = jnp.logical_not(last)
        each(mix, 1)

        @pl.when(step == 0)
        def late():
            pass_on(0, 0, "earlier")

        prefixes(1)
        send_off(0, 1)
        counts(0, *take(0, 0))
        send_off(1, 0)
        pass_on(0, 1, "earlier")
        pass_on(1, 0, "sum")
        counts(1, *take(0, 1))
        send_off(1, 1)
        residuals(0, *take(1, 0))
        send_off(2, 0)
        settle(0, 0)
        pass_on(1, 1, "sum")
        each(suffixes, 0)
        pass_on(2, 0, "later")
        residuals(1, *take(1, 1))
        send_off(2, 1)
        settle(0, 1)
        each(unmix, 0)

        @pl.when(last)
        def leave():
            for z in members(0):
                store(z).start()

        after = take(2, 0)
        settle(1, 0)

        @pl.when(more)
        def again():
            renew(0, *after)
            opening(0)
            send_off(0, 0)

        @pl.when(last)
        def part():
            end(0, *after)

        pass_on(2, 1, "later")
        each(suffixes, 1)

        @pl.when(more)
        def early():
            pass_on(0, 0, "earlier")

        each(unmix, 1)

        @pl.when(last)
        def leave_too():
            for z in members(1):
                store(z).start()

        rest = take(2, 1)

        @pl.when(more)
        def once_more():
            renew(1, *rest)

        settle(1, 1)
        settle(2, 0)
        settle(2, 1)

        @pl.when(last)
        def finish():
            end(1, *rest)
            for z in range(ZS):
                store(z).wait()

        return carry

    lax.fori_loop(0, STEPS, turn, 0)


def close(c_hbm, dx_hbm, dy_hbm, out_hbm, c_ref, dx_ref, dy_ref, sems):
    loads = [pltpu.make_async_copy(a, b, sems.at[k]) for k, (a, b) in enumerate(((dx_hbm, dx_ref), (dy_hbm, dy_ref)))]
    loads += [pltpu.make_async_copy(c_hbm.at[:, z], c_ref.at[:, z], sems.at[2 + z]) for z in range(ZS)]
    for load in loads:
        load.start()
    loads[0].wait()
    loads[1].wait()
    stores = []
    for z in range(ZS):
        g = z // PER
        cols = jnp.concatenate([dy_ref[g], jnp.zeros((N - SIZES[2], N), F32)], 0).T
        loads[2 + z].wait()
        for e in range(ELEMENTS):
            k = spot(z, e)
            c_ref[e, z] = c_ref[e, z] + dx_ref[g, k : k + 1] + cols[:, k : k + 1]
        stores.append(pltpu.make_async_copy(c_ref.at[:, z], out_hbm.at[:, z], sems.at[2 + z]))
        stores[z].start()
    for store in stores:
        store.wait()


def solution(mesh):
    beams, dets = mesh.shape["beam"], mesh.shape["det"]

    def shards(conc, inc, sig, yld, rate, axis, m1, live1, m2, live2):
        step_x = 1.0 / (conc.shape[2] * beams)
        step_y = 1.0 / (conc.shape[3] * dets)

        def body(*refs):
            kernel(beams, dets, step_x, step_y, *refs)

        def exchange(count):
            def rows(*slots):
                return pltpu.VMEM((3, GROUPS) + slots + (ROWS, N), F32)

            sems = pltpu.SemaphoreType.DMA((3, GROUPS, 2, 2))
            return [rows(), rows(count // AHEAD), rows(2), rows(AHEAD), sems]

        def grouped(rows):
            return pltpu.VMEM((GROUPS, rows, N), F32)

        field = (N, N)
        anywhere = pl.BlockSpec(memory_space=pl.ANY)
        vmem = pl.BlockSpec(memory_space=pltpu.VMEM)
        small = (axis[None], inc, sig, yld, rate[None], m1, live1, m2, live2)
        inner, dx, dy = pl.pallas_call(
            body,
            out_shape=[
                jax.ShapeDtypeStruct(conc.shape, F32),
                jax.ShapeDtypeStruct((GROUPS, SIZES[2], N), F32),
                jax.ShapeDtypeStruct((GROUPS, SIZES[2], N), F32),
            ],
            in_specs=[anywhere] * (len(small) + 1),
            out_specs=[anywhere, vmem, vmem],
            scratch_shapes=[
                *[pltpu.VMEM(a.shape, a.dtype) for a in small + (conc,)],
                pltpu.SemaphoreType.DMA((len(small),)),
                pltpu.SemaphoreType.DMA((ZS,)),
                pltpu.VMEM((ZS, PATHS, N, 2 * N), BF16),
                pltpu.VMEM((ZS, LINES) + field, F32),
                *[pltpu.VMEM((ZS, LINES + 1) + field, F32)] * 2,
                *[pltpu.VMEM((ZS, LINES) + field, F32)] * 3,
                *[pltpu.VMEM((ZS, LINES + 1, N, 2 * N), BF16)] * 2,
                *[pltpu.VMEM((ZS, PATHS) + field, F32)] * 2,
                pltpu.VMEM(conc.shape, F32),
                grouped(ROWS),
                pltpu.VMEM((GROUPS, N, N), BF16),
                pltpu.VMEM((N, ROWS * N), BF16),
                *[grouped(ROWS)] * 4,
                *[grouped(ROWS)] * 2,
                pltpu.VMEM((64, N), F32),
                pltpu.VMEM((32, N), F32),
                pltpu.VMEM((8 * FIELDS, 2 * N), BF16),
                pltpu.VMEM((16 * ELEMENTS, 8 * PARTS), BF16),
                *[pltpu.VMEM((2 * N, 2 * N), BF16)] * 2,
                pltpu.VMEM((N, 2 * N), BF16),
                *[pltpu.VMEM((ROWS, 3 * N), BF16)] * 2,
                *exchange(beams),
                *exchange(dets),
            ],
            compiler_params=pltpu.CompilerParams(
                collective_id=0, has_side_effects=True, vmem_limit_bytes=64 * 1024 * 1024
            ),
        )(*small, conc)

        return pl.pallas_call(
            close,
            out_shape=jax.ShapeDtypeStruct(conc.shape, F32),
            in_specs=[anywhere] * 3,
            out_specs=anywhere,
            scratch_shapes=[
                pltpu.VMEM(conc.shape, F32),
                *[pltpu.VMEM((GROUPS, SIZES[2], N), F32)] * 2,
                pltpu.SemaphoreType.DMA((2 + ZS,)),
            ],
            compiler_params=pltpu.CompilerParams(vmem_limit_bytes=64 * 1024 * 1024),
        )(inner, dx, dy)

    in_specs = (
        P(None, None, "beam", "det"),
        P(),
        P(),
        P(),
        P(),
        P(),
        P(None, None, "det"),
        P(None, "det"),
        P(None, None, "beam"),
        P(None, "beam"),
    )
    out_specs = P(None, None, "beam", "det")
    return jax.shard_map(shards, mesh=mesh, in_specs=in_specs, out_specs=out_specs, check_vma=False)
```

```python
import math

import jax
import jax.numpy as jnp
from jax import lax
from jax.experimental import pallas as pl
from jax.experimental.pallas import tpu as pltpu
from jax.sharding import PartitionSpec as P

STEPS = 2
HIGH = lax.Precision.HIGHEST
MESH = pl.DeviceIdType.MESH
F32 = jnp.float32
BF16 = jnp.bfloat16
ELEMENTS = 10
LINES = 12
ZS = 4
N = 128
PATHS = LINES + 1
FIELDS = 3 * PATHS + LINES
AHEAD = 4
PARTS = 2 * LINES + 2
GROUPS = 2
PER = ZS // GROUPS
ROWS = 16 * PER
SIZES = (ROWS, LINES * PER, LINES * PER)
LOG2E = math.log2(math.e)


def split(value):
    high = value.astype(BF16)
    return high, (value - high.astype(F32)).astype(BF16)


def iota(shape, dim):
    return lax.broadcasted_iota(jnp.int32, shape, dim)


def dot(a, b):
    return jnp.dot(a, b, preferred_element_type=F32)


def exact(a, b):
    return jnp.dot(a, b, preferred_element_type=F32, precision=HIGH)


def exact_nt(a, b):
    return lax.dot_general(
        a, b, (((1,), (1,)), ((), ())), preferred_element_type=F32, precision=HIGH
    )


def triple(table):
    high, low = split(table)
    return jnp.concatenate([high, high, low], 1)


def rows_of(value):
    high, low = split(jnp.concatenate([value, jnp.zeros((-value.shape[0] % 128, value.shape[1]), F32)], 0))
    return jnp.concatenate([high, low, high], 0)


def one_hot(condition):
    return jnp.where(condition, 1.0, 0.0).astype(F32)


def spot(z, k):
    return PER * k + z % PER


class Ring:
    def __init__(self, axis, count, send, near, out, far, sems):
        self.axis, self.count = axis, count
        self.send, self.near, self.out, self.far, self.sems = send, near, out, far, sems
        self.slots = count // AHEAD
        self.cores = self.slots // 2
        me = lax.axis_index(axis)
        self.c = lax.rem(me, self.cores)
        self.x = lax.rem(me // self.cores, AHEAD)
        self.y = me // (self.cores * AHEAD)
        self.slot = self.y * self.cores + self.c

    def index(self, y, x, c):
        return (y * AHEAD + x) * self.cores + c

    def near_peers(self):
        slots = [lax.rem(self.slot + d, self.slots) for d in ((2, 1, 3) if self.slots == 4 else (1,))]
        return [self.index(k // self.cores, self.x, lax.rem(k, self.cores)) for k in slots]

    def far_peers(self):
        return [(d, self.index(self.y, lax.rem(self.x + d, AHEAD), self.c)) for d in (2, 1, 3)]

    def greet(self, barrier):
        peers = self.near_peers() + [peer for _, peer in self.far_peers()]
        for peer in peers:
            pl.semaphore_signal(barrier, inc=1, device_id={self.axis: peer}, device_id_type=MESH)
        return len(peers)

    def copy(self, src, dst, phase, g, leg, peer):
        return pltpu.make_async_remote_copy(
            src_ref=src,
            dst_ref=dst,
            send_sem=self.sems.at[phase, g, leg, 0],
            recv_sem=self.sems.at[phase, g, leg, 1],
            device_id={self.axis: peer},
            device_id_type=MESH,
        )

    def start(self, phase, g):
        rows = pl.ds(0, SIZES[phase])
        for peer in self.near_peers():
            src, dst = self.send.at[phase, g, rows], self.near.at[phase, g, self.slot, rows]
            self.copy(src, dst, phase, g, 0, peer).start()
        self.near[phase, g, pl.ds(self.slot, 1), rows] = self.send[phase, g, rows][None]

    def whole(self, phase, g, leg):
        ref, count = ((self.near, self.slots - 1), (self.far, AHEAD - 1))[leg]
        some = ref.at[phase, g, pl.ds(0, count), pl.ds(0, SIZES[phase])]
        return self.copy(some, some, phase, g, leg, self.near_peers()[0])

    def settle(self, phase, g):
        self.whole(phase, g, 0).wait_send()
        self.whole(phase, g, 1).wait_send()

    def middle(self, phase, g, mode):
        self.whole(phase, g, 0).wait_recv()
        rows = pl.ds(0, SIZES[phase])
        have = [[self.near[phase, g, y * self.cores + c, rows] for c in range(self.cores)] for y in range(2)]
        sums = [sum(cores[1:], cores[0]) for cores in have]
        if mode == "sum":
            mine = sums[0] + sums[1]
            self.out[phase, g, 0, rows] = mine
        else:
            earlier = mode == "earlier"

            def chosen(other, own):
                return (other < own if earlier else other > own).astype(F32)

            base = sum(sums[y] * chosen(y, self.y) for y in range(2))
            same = sum(sums[y] * (self.y == y).astype(F32) for y in range(2))
            mine = base
            for y in range(2):
                for c in range(self.cores):
                    mine = mine + have[y][c] * ((self.y == y).astype(F32) * chosen(c, self.c))
            self.out[phase, g, 0, rows] = base
            self.out[phase, g, 1, rows] = base + same
        for d, peer in self.far_peers():
            wrap = (self.x + d) // AHEAD
            which = {"sum": 0, "earlier": 1 - wrap, "later": wrap}[mode]
            src, dst = self.out.at[phase, g, which, rows], self.far.at[phase, g, self.x, rows]
            self.copy(src, dst, phase, g, 1, peer).start()
        self.far[phase, g, pl.ds(self.x, 1), rows] = mine[None]

    def finish(self, phase, g):
        self.whole(phase, g, 1).wait_recv()
        far = [self.far[phase, g, x, pl.ds(0, SIZES[phase])] for x in range(AHEAD)]
        return (far[0] + far[1]) + (far[2] + far[3])

    def put(self, phase, g, row, value):
        self.send[phase, g, row : row + 1, :] = value


def kernel(
    beams, dets, step_x, step_y,
    axis_hbm, inc_hbm, sig_hbm, yld_hbm, rate_hbm, m1_hbm, live1_hbm, m2_hbm, live2_hbm, conc_hbm,
    out_hbm, dx_ref, dy_ref,
    axis_ref, inc_ref, sig_ref, yld_ref, rate_ref, m1_ref, live1_ref, m2_ref, live2_ref, c_ref,
    load_sems, conc_sems,
    m_ref, q_ref, e1_ref, e2_ref, a1_ref, a2_ref, w_ref, p1_ref, p2_ref, vx_ref, vy_ref, d_ref, rows_ref, cols_ref, spread_ref,
    mx_ref, my_ref, lx_ref, ly_ref,
    tx_ref, ty_ref, tab_ref, back_ref, mix_ref, unmix_ref, up_ref, down_ref, right_ref,
    wcx_ref, wcy_ref,
    bsend, bnear, bout, bfar, bsems, dsend, dnear, dout, dfar, dsems,
):
    def conc_load(z):
        return pltpu.make_async_copy(conc_hbm.at[:, z], c_ref.at[:, z], conc_sems.at[z])

    hbm = (axis_hbm, inc_hbm, sig_hbm, yld_hbm, rate_hbm, m1_hbm, live1_hbm, m2_hbm, live2_hbm)
    vmem = (axis_ref, inc_ref, sig_ref, yld_ref, rate_ref, m1_ref, live1_ref, m2_ref, live2_ref)
    loads = [pltpu.make_async_copy(a, b, load_sems.at[k]) for k, (a, b) in enumerate(zip(hbm, vmem))]
    for load in loads + [conc_load(z) for z in range(ZS)]:
        load.start()
    beam = Ring("beam", beams, bsend, bnear, bout, bfar, bsems)
    det = Ring("det", dets, dsend, dnear, dout, dfar, dsems)
    barrier = pltpu.get_barrier_semaphore()
    greeted = det.greet(barrier) + beam.greet(barrier)

    for ref in (bsend, dsend, mx_ref, my_ref, lx_ref, ly_ref, tx_ref, ty_ref, tab_ref, back_ref):
        ref[...] = jnp.zeros(ref.shape, F32)

    lane = iota((N, N), 1)

    def members(g):
        return range(g * PER, (g + 1) * PER)

    def send_off(phase, g):
        det.start(phase, g)
        beam.start(phase, g)

    def pass_on(phase, g, mode):
        det.middle(phase, g, mode)
        beam.middle(phase, g, mode)

    def settle(phase, g):
        det.settle(phase, g)
        beam.settle(phase, g)

    def take(phase, g):
        across = det.finish(phase, g)
        return beam.finish(phase, g), across

    def turn_over(g, rows):
        rows = jnp.concatenate([rows, jnp.zeros((ROWS - rows.shape[0], N), F32)], 0) if rows.shape[0] < ROWS else rows
        high = rows.astype(BF16).astype(F32)
        rest = rows - high
        middle = rest.astype(BF16).astype(F32)
        parts = [high, middle, rest - middle, jnp.zeros((N - 3 * ROWS, N), F32)]
        cols_ref[g] = jnp.concatenate(parts, 0).T.astype(BF16)

    def spread(g, z, k, count):
        k += 16 * (z % PER)
        out = dot(cols_ref[g], spread_ref[:, k * N : (k + count) * N])
        return [out[:, n * N : (n + 1) * N] for n in range(count)]

    def row_sum(value):
        return jnp.sum(jnp.sum(value.reshape(N // 8, 8, N), 0), 0, keepdims=True)

    for load in loads:
        load.wait()

    def tables():
        first = axis_ref[0:1, 0:1] == 0
        one, two = inc_ref[0:1, :], inc_ref[1:2, :]
        s1 = jnp.where(first, one, two)
        s2 = jnp.where(first, two, one)
        scale = -LOG2E * step_y
        sig, yld, rate = sig_ref[...], yld_ref[...], rate_ref[...]
        cols = pl.ds(0, ELEMENTS)
        tab_ref[0:LINES, cols] = scale * sig
        tab_ref[LINES:PATHS, cols] = scale * s2
        for k in (PATHS, 2 * PATHS):
            tab_ref[k : k + LINES, cols] = -LOG2E * step_x * sig
            tab_ref[k + LINES : k + PATHS, cols] = -LOG2E * step_x * s1
        tab_ref[3 * PATHS : FIELDS, cols] = yld
        back_ref[0:LINES, cols] = yld * rate
        back_ref[LINES : 2 * LINES, cols] = -sig * rate
        back_ref[2 * LINES : 2 * LINES + 1, cols] = -s1 * rate
        back_ref[2 * LINES + 1 : 2 * LINES + 2, cols] = -s2 * rate

        tab, back = tab_ref[...], back_ref[...]
        wide = 8 * ELEMENTS
        pick = one_hot((iota((8 * FIELDS, 64), 0) >> 3) == iota((8 * FIELDS, 64), 1))
        col = iota((N, 256), 1)
        part = (col >= wide).astype(jnp.int32) + (col >= 2 * wide).astype(jnp.int32)
        spread = one_hot(((col - wide * part) >> 3) == iota((N, 256), 0))
        spread = jnp.where(col < 3 * wide, spread, 0.0)
        full = exact(pick, exact(tab, spread))
        shape = (8 * FIELDS, 256)
        field, gap = iota(shape, 0) >> 3, (iota(shape, 0) & 7) - (iota(shape, 1) & 7)
        within = (field >= PATHS) & (field < 2 * PATHS)
        whole = (field >= 2 * PATHS) & (field < 3 * PATHS)
        full = jnp.where(whole | (within & (gap > 0)) | ((gap == 0) & jnp.logical_not(within)), full, 0.0)
        high, low = split(full)
        part = iota(shape, 1)
        mix_ref[...] = jnp.where((part >= wide) & (part < 2 * wide), low.astype(F32), high.astype(F32)).astype(BF16)

        pick = one_hot((iota((wide, N), 0) >> 3) == iota((wide, N), 1))
        shape = (wide, 8 * PARTS)
        spread = one_hot((iota((32, 8 * PARTS), 1) >> 3) == iota((32, 8 * PARTS), 0))
        full = exact(exact_nt(pick, back), spread)
        full = jnp.where((iota(shape, 0) & 7) == (iota(shape, 1) & 7), full, 0.0)
        high, low = split(full)
        unmix_ref[0:wide] = high
        unmix_ref[wide : 2 * wide] = low

        r, m = iota((16 * PER, 32), 0) & 15, iota((16 * PER, 32), 1)
        sums_x = exact(one_hot(m == jnp.where(r < LINES, r + LINES, 2 * LINES)), back)
        sums_y = exact(one_hot(m == jnp.where(r < LINES, r + LINES, 2 * LINES + 1)), back)
        r = iota((16 * PER, N), 0) & 15
        sums_x = jnp.where(r <= LINES, -step_x * sums_x, 0.0)
        sums_y = jnp.where(r <= LINES, -step_y * sums_y, 0.0)

        shape = (ROWS, N)
        place = one_hot(((iota(shape, 0) // PER) == iota(shape, 1)) & (iota(shape, 1) < ELEMENTS))
        same = (iota(shape, 0) & (PER - 1)) == (iota(shape, 1) >> 4)
        fill = jnp.zeros((N - ROWS, N), F32)
        for ref, sums in ((wcx_ref, sums_x), (wcy_ref, sums_y)):
            ref[...] = triple(jnp.where(same, exact_nt(place, jnp.concatenate([sums, fill], 0)), 0.0))
        shape = spread_ref.shape
        k = iota(shape, 0)
        wanted = iota(shape, 1) >> 7
        wanted = PER * (wanted & 15) + (wanted >> 4)
        spread_ref[...] = one_hot((k < 3 * ROWS) & ((k & (ROWS - 1)) == wanted)).astype(BF16)

        r, c = iota((2 * N, N), 0) & (N - 1), iota((2 * N, N), 1)
        ones = jnp.ones((2 * N, N), F32)
        up_ref[...] = jnp.concatenate([one_hot(r < c), ones], 1).astype(BF16)
        down_ref[...] = jnp.concatenate([step_y * one_hot(r > c), ones], 1).astype(BF16)
        r, c = iota((N, 2 * N), 0), iota((N, 2 * N), 1) & (N - 1)
        right_ref[...] = (step_x * one_hot(c > r)).astype(BF16)
        for z in range(ZS):
            live1 = live1_ref[z : z + 1, :].astype(F32)
            live2 = live2_ref[z : z + 1, :].astype(F32)
            for l in range(LINES):
                g, k = z // PER, spot(z, l)
                lx_ref[g, k : k + 1, :] = live1
                ly_ref[g, k : k + 1, :] = live2
                mx_ref[g, k : k + 1, :] = m1_ref[l, z : z + 1, :]
                my_ref[g, k : k + 1, :] = m2_ref[l, z : z + 1, :]

    tables()

    def mix(z):
        run = [jnp.zeros((8, N), F32)] * PATHS
        for r0 in range(0, N, 16):
            parts = []
            for b in range(2):
                high, low = split(c_ref[:, z, pl.ds(r0 + 8 * b, 8), :].reshape(8 * ELEMENTS, N))
                parts.append(jnp.concatenate([high, high, low, jnp.zeros((16, N), BF16)], 0))
            out = dot(mix_ref[...], jnp.concatenate(parts, 1))

            def field(f):
                return [out[8 * f : 8 * f + 8, b * N : (b + 1) * N] for b in range(2)]

            rows = pl.ds(r0, 16)
            for l in range(PATHS):
                high, low = split(jnp.concatenate(field(l), 0))
                m_ref[z, l, rows, 0:N] = high
                m_ref[z, l, rows, N : 2 * N] = low
                within, whole = field(PATHS + l), field(2 * PATHS + l)
                for b in range(2):
                    e2_ref[z, l, pl.ds(r0 + 8 * b, 8)] = run[l] + within[b]
                    run[l] = run[l] + whole[b]
            for l in range(LINES):
                q_ref[z, l, rows, :] = jnp.concatenate(field(3 * PATHS + l), 0)
        for l in range(PATHS):
            beam.put(0, z // PER, spot(z, l), run[l][0:1])

    def unmix(z):
        wide = 8 * ELEMENTS
        for r0 in range(0, N, 16):
            highs, lows = [], []
            for b in range(2):
                rows = pl.ds(r0 + 8 * b, 8)
                w = w_ref[z, :, rows, :].reshape(8 * LINES, N)
                along_x, along_y = vx_ref[z, :, rows, :], vy_ref[z, :, rows, :]
                both = (along_x[0:LINES] + along_y[0:LINES]).reshape(8 * LINES, N)
                high, low = split(jnp.concatenate([w, both, along_x[LINES], along_y[LINES]], 0))
                highs.append(high)
                lows.append(low)
            one = dot(unmix_ref[...], jnp.concatenate(highs, 1))
            two = dot(unmix_ref[0:wide], jnp.concatenate(lows, 1))
            out = one[0:wide] + (one[wide:] + two)
            for b in range(2):
                rows = pl.ds(r0 + 8 * b, 8)
                new = c_ref[:, z, rows, :] - out[:, b * N : (b + 1) * N].reshape(ELEMENTS, 8, N)
                d_ref[:, z, rows, :] = new

    def stacked(ref, z, fields):
        value = [ref[z, f] for f in fields]
        high = jnp.concatenate([v[:, 0:N] for v in value], 1)
        low = jnp.concatenate([v[:, N : 2 * N] for v in value], 1)
        return jnp.concatenate([high, low], 0)

    def prefixes(g):
        acc = jnp.zeros((N, N), F32)
        for z in members(g):
            out = dot(m_ref[z].reshape(PATHS * N, 2 * N), up_ref[...])
            for l in range(PATHS):
                part = out[l * N : (l + 1) * N]
                e1_ref[z, l] = part[:, 0:N]
                acc = jnp.where(lane == spot(z, l), part[:, N : 2 * N], acc)
        dsend[0, g] = acc.T[0:ROWS]

    def suffixes(z):
        for l in range(0, LINES, 2):
            over_x = dot(right_ref[...], stacked(p2_ref, z, (l, l + 1)))
            vx_ref[z, l] = over_x[:, 0:N]
            vx_ref[z, l + 1] = over_x[:, N : 2 * N]
        vx_ref[z, LINES] = dot(right_ref[...], stacked(p2_ref, z, (LINES,)))

    def counts(g, enter_x, enter_y):
        rows_ref[g] = enter_x
        turn_over(g, enter_y)
        acc = jnp.zeros((N, N), F32)
        for z in members(g):
            k = spot(z, LINES)
            tin1 = jnp.exp2(e2_ref[z, LINES] + rows_ref[g, k : k + 1])
            tin2 = jnp.exp2(e1_ref[z, LINES] + spread(g, z, LINES, 1)[0])
            for l in range(LINES):
                k = spot(z, l)
                if l % 2 == 0:
                    cols = spread(g, z, l, 2)
                a1 = tin1 * jnp.exp2(e1_ref[z, l] + cols[l % 2])
                a2 = tin2 * jnp.exp2(e2_ref[z, l] + rows_ref[g, k : k + 1])
                a1_ref[z, l] = a1
                a2_ref[z, l] = a2
                q = q_ref[z, l]
                beam.put(1, g, k, step_x * row_sum(q * a1))
                acc = jnp.where(lane == k, jnp.sum(q * a2, 1, keepdims=True), acc)
        dsend[1, g] = step_y * acc.T[0:ROWS]

    def residuals(g, pred1, pred2):
        used = pl.ds(0, LINES * PER)
        res1 = lx_ref[g, used] * (pred1 - mx_ref[g, used])
        res2 = ly_ref[g, used] * (pred2 - my_ref[g, used])
        sum1 = res1 * bsend[1, g, used] / step_x
        sum2 = res2 * dsend[1, g, used] / step_y
        rows_ref[g, used] = res1
        turn_over(g, res2)

        def keep(ref, z, f, value):
            high, low = split(value)
            ref[z, f, :, 0:N] = high
            ref[z, f, :, N : 2 * N] = low

        acc = jnp.zeros((N, N), F32)
        for z in members(g):
            all1 = jnp.zeros((N, N), F32)
            all2 = jnp.zeros((N, N), F32)
            for l in range(LINES):
                k = 16 * (z % PER) + l
                if l % 2 == 0:
                    cols = spread(g, z, l, 2)
                w1 = a1_ref[z, l] * rows_ref[g, spot(z, l) : spot(z, l) + 1]
                w2 = a2_ref[z, l] * cols[l % 2]
                w_ref[z, l] = w1 + w2
                q = q_ref[z, l]
                p1, p2 = q * w1, q * w2
                all1, all2 = all1 + p1, all2 + p2
                tx_ref[g, k : k + 1] = row_sum(p2)
                keep(p1_ref, z, l, p1)
                keep(p2_ref, z, l, p2)
            keep(p1_ref, z, LINES, all2)
            keep(p2_ref, z, LINES, all1)
            out = dot(p1_ref[z].reshape(PATHS * N, 2 * N), down_ref[...])
            for l in range(PATHS):
                part = out[l * N : (l + 1) * N]
                vy_ref[z, l] = part[:, 0:N]
                if l < LINES:
                    acc = jnp.where(lane == 16 * (z % PER) + l, part[:, N : 2 * N], acc)
        ty_ref[g] = acc.T[0:ROWS]
        for z in range(PER):
            k = 16 * z + LINES
            own = (iota((LINES * PER, N), 0) & (PER - 1)) == z
            tx_ref[g, k : k + 1] = jnp.sum(jnp.where(own, sum1, 0.0), 0, keepdims=True)
            ty_ref[g, k : k + 1] = jnp.sum(jnp.where(own, sum2, 0.0), 0, keepdims=True)
        bsend[2, g] = dot(wcx_ref[...], rows_of(tx_ref[g]))
        dsend[2, g] = dot(wcy_ref[...], rows_of(ty_ref[g]))

    def store(z):
        return pltpu.make_async_copy(d_ref.at[:, z], out_hbm.at[:, z], conc_sems.at[z])

    def end(g, after_x, after_y):
        dx_ref[g], dy_ref[g] = after_x, after_y

    def renew(g, after_x, after_y):
        rows_ref[g, 0 : SIZES[2]] = after_x
        turn_over(g, after_y)
        for z in members(g):
            for e in range(ELEMENTS):
                k = spot(z, e)
                if e % 2 == 0:
                    cols = spread(g, z, e, 2)
                c_ref[e, z] = d_ref[e, z] + rows_ref[g, k : k + 1] + cols[e % 2]

    def each(stage, g):
        for z in members(g):
            stage(z)

    def opening(g):
        each(mix, g)
        prefixes(g)

    for z in members(0):
        conc_load(z).wait()
    opening(0)
    pl.semaphore_wait(barrier, greeted)
    send_off(0, 0)

    def turn(step, carry):
        last = step == STEPS - 1
        more = jnp.logical_not(last)

        @pl.when(step == 0)
        def arrive():
            for z in members(1):
                conc_load(z).wait()

        each(mix, 1)

        @pl.when(step == 0)
        def late():
            pass_on(0, 0, "earlier")

        prefixes(1)
        send_off(0, 1)
        counts(0, *take(0, 0))
        send_off(1, 0)
        pass_on(0, 1, "earlier")
        pass_on(1, 0, "sum")
        counts(1, *take(0, 1))
        send_off(1, 1)
        residuals(0, *take(1, 0))
        send_off(2, 0)
        settle(0, 0)
        pass_on(1, 1, "sum")
        each(suffixes, 0)
        pass_on(2, 0, "later")
        residuals(1, *take(1, 1))
        send_off(2, 1)
        settle(0, 1)
        each(unmix, 0)

        @pl.when(last)
        def leave():
            for z in members(0):
                store(z).start()

        after = take(2, 0)
        settle(1, 0)

        @pl.when(more)
        def again():
            renew(0, *after)
            opening(0)
            send_off(0, 0)

        @pl.when(last)
        def part():
            end(0, *after)

        pass_on(2, 1, "later")
        each(suffixes, 1)

        @pl.when(more)
        def early():
            pass_on(0, 0, "earlier")

        each(unmix, 1)

        @pl.when(last)
        def leave_too():
            for z in members(1):
                store(z).start()

        rest = take(2, 1)

        @pl.when(more)
        def once_more():
            renew(1, *rest)

        settle(1, 1)
        settle(2, 0)
        settle(2, 1)

        @pl.when(last)
        def finish():
            end(1, *rest)
            for z in range(ZS):
                store(z).wait()

        return carry

    lax.fori_loop(0, STEPS, turn, 0)


def close(c_hbm, dx_hbm, dy_hbm, out_hbm, c_ref, dx_ref, dy_ref, sems):
    loads = [pltpu.make_async_copy(a, b, sems.at[k]) for k, (a, b) in enumerate(((dx_hbm, dx_ref), (dy_hbm, dy_ref)))]
    loads += [pltpu.make_async_copy(c_hbm.at[:, z], c_ref.at[:, z], sems.at[2 + z]) for z in range(ZS)]
    for load in loads:
        load.start()
    loads[0].wait()
    loads[1].wait()
    stores = []
    for z in range(ZS):
        g = z // PER
        cols = jnp.concatenate([dy_ref[g], jnp.zeros((N - SIZES[2], N), F32)], 0).T
        loads[2 + z].wait()
        for e in range(ELEMENTS):
            k = spot(z, e)
            c_ref[e, z] = c_ref[e, z] + dx_ref[g, k : k + 1] + cols[:, k : k + 1]
        stores.append(pltpu.make_async_copy(c_ref.at[:, z], out_hbm.at[:, z], sems.at[2 + z]))
        stores[z].start()
    for store in stores:
        store.wait()


def solution(mesh):
    beams, dets = mesh.shape["beam"], mesh.shape["det"]

    def shards(conc, inc, sig, yld, rate, axis, m1, live1, m2, live2):
        step_x = 1.0 / (conc.shape[2] * beams)
        step_y = 1.0 / (conc.shape[3] * dets)

        def body(*refs):
            kernel(beams, dets, step_x, step_y, *refs)

        def exchange(count):
            def rows(*slots):
                return pltpu.VMEM((3, GROUPS) + slots + (ROWS, N), F32)

            sems = pltpu.SemaphoreType.DMA((3, GROUPS, 2, 2))
            return [rows(), rows(count // AHEAD), rows(2), rows(AHEAD), sems]

        def grouped(rows):
            return pltpu.VMEM((GROUPS, rows, N), F32)

        field = (N, N)
        anywhere = pl.BlockSpec(memory_space=pl.ANY)
        vmem = pl.BlockSpec(memory_space=pltpu.VMEM)
        small = (axis[None], inc, sig, yld, rate[None], m1, live1, m2, live2)
        inner, dx, dy = pl.pallas_call(
            body,
            out_shape=[
                jax.ShapeDtypeStruct(conc.shape, F32),
                jax.ShapeDtypeStruct((GROUPS, SIZES[2], N), F32),
                jax.ShapeDtypeStruct((GROUPS, SIZES[2], N), F32),
            ],
            in_specs=[anywhere] * (len(small) + 1),
            out_specs=[anywhere, vmem, vmem],
            scratch_shapes=[
                *[pltpu.VMEM(a.shape, a.dtype) for a in small + (conc,)],
                pltpu.SemaphoreType.DMA((len(small),)),
                pltpu.SemaphoreType.DMA((ZS,)),
                pltpu.VMEM((ZS, PATHS, N, 2 * N), BF16),
                pltpu.VMEM((ZS, LINES) + field, F32),
                *[pltpu.VMEM((ZS, LINES + 1) + field, F32)] * 2,
                *[pltpu.VMEM((ZS, LINES) + field, F32)] * 3,
                *[pltpu.VMEM((ZS, LINES + 1, N, 2 * N), BF16)] * 2,
                *[pltpu.VMEM((ZS, PATHS) + field, F32)] * 2,
                pltpu.VMEM(conc.shape, F32),
                grouped(ROWS),
                pltpu.VMEM((GROUPS, N, N), BF16),
                pltpu.VMEM((N, ROWS * N), BF16),
                *[grouped(ROWS)] * 4,
                *[grouped(ROWS)] * 2,
                pltpu.VMEM((64, N), F32),
                pltpu.VMEM((32, N), F32),
                pltpu.VMEM((8 * FIELDS, 2 * N), BF16),
                pltpu.VMEM((16 * ELEMENTS, 8 * PARTS), BF16),
                *[pltpu.VMEM((2 * N, 2 * N), BF16)] * 2,
                pltpu.VMEM((N, 2 * N), BF16),
                *[pltpu.VMEM((ROWS, 3 * N), BF16)] * 2,
                *exchange(beams),
                *exchange(dets),
            ],
            compiler_params=pltpu.CompilerParams(
                collective_id=0, has_side_effects=True, vmem_limit_bytes=64 * 1024 * 1024
            ),
        )(*small, conc)

        return pl.pallas_call(
            close,
            out_shape=jax.ShapeDtypeStruct(conc.shape, F32),
            in_specs=[anywhere] * 3,
            out_specs=anywhere,
            scratch_shapes=[
                pltpu.VMEM(conc.shape, F32),
                *[pltpu.VMEM((GROUPS, SIZES[2], N), F32)] * 2,
                pltpu.SemaphoreType.DMA((2 + ZS,)),
            ],
            compiler_params=pltpu.CompilerParams(vmem_limit_bytes=64 * 1024 * 1024),
        )(inner, dx, dy)

    in_specs = (
        P(None, None, "beam", "det"),
        P(),
        P(),
        P(),
        P(),
        P(),
        P(None, None, "det"),
        P(None, "det"),
        P(None, None, "beam"),
        P(None, "beam"),
    )
    out_specs = P(None, None, "beam", "det")
    return jax.shard_map(shards, mesh=mesh, in_specs=in_specs, out_specs=out_specs, check_vma=False)
```
